32 devices in a mesh: ka: 2 (over x), gy: 4 (over z), gz: 4 (over y, core).
Axes of the slice: x: 2, y: 2, z: 4, core: 2. Of those that a mesh axis runs over, the one named last changes fastest.
Arguments:
- loads: float32 [32, 3, 128, 512], P('ka', None, 'gy', 'gz'), may hold values from -1 to 1
- sleeper_pos: int32 [32], P('ka'), may hold values from 0 to 127
- material: int32 [128, 512], P('gy', 'gz'), may hold values from 0 to 7, as said below
- material_table: float32 [8, 8], replicated, may hold values from -1 to 3, as said below
Outputs:
- adjoint_field: float32 [128, 2, 3, 128, 512], P('ka', None, None, 'gy', 'gz')
The draws below stay inside these ranges and needn't reach their ends.
Inputs may be any that keep to these rules, and one draw needn't show every extreme that they name: layered: the material index never falls with depth in a column, layer boundaries vary from column to column, and every material occurs. `material_table`: shifts and damping positive, each material's coupling matrix diagonally dominant with a positive diagonal.
All inputs are finite; a program needn't handle non-finite values.
Results may differ from the reference program's by a relative error of at most 0.0002.
Values sent between devices are 32-bit elements; how exact they have to be, the bound alone decides.
No kernel may reach another device: no remote copies, remote signals or barrier semaphores. Data moves between devices by JAX's collectives and lax.ppermute only.
A program may use at most 128 MiB of HBM per device.

```python
import math
import jax
import jax.numpy as jnp
from jax import lax

KW = 128
NMAT = 8
SWEEPS = 2
DEG = 4
NY = 128
NZ = 512
SLEEPERS = 32


def draw_material(key, part):
    jitter = NZ // (4 * NMAT)
    offsets = jax.random.randint(key, (NMAT - 1, NY), -jitter, jitter + 1)
    boundary = (jnp.arange(1, NMAT, dtype=jnp.int32) * (NZ // NMAT))[:, None] + offsets
    depths = jnp.arange(NZ, dtype=jnp.int32)
    return jnp.sum((depths[None, None, :] >= boundary[:, :, None]).astype(jnp.int32), axis=0)


def draw_material_table(key, part):
    subkeys = jax.random.split(key, 4)
    diagonal_part = jnp.exp(jax.random.uniform(subkeys[0], (NMAT, 3), jnp.float32, jnp.log(0.5), jnp.log(3.0)))
    shifts = jnp.exp(jax.random.uniform(subkeys[1], (NMAT,), jnp.float32, jnp.log(0.05), jnp.log(1.0)))
    smallest = jnp.min(diagonal_part, axis=1)
    off_diagonal = jax.random.uniform(subkeys[2], (NMAT, 3), jnp.float32, -0.2, 0.2) * smallest[:, None]
    damping = jax.random.uniform(subkeys[3], (NMAT,), jnp.float32, 0.05, 0.3)
    return jnp.concatenate([shifts[:, None], diagonal_part, off_diagonal, damping[:, None]], axis=1)


def touch_ends(values, own_key, low, high):
    spot = [jax.random.randint(jax.random.fold_in(own_key, axis), (), 0, length) for axis, length in enumerate(values.shape)]
    main_axis = values.shape.index(max(values.shape))
    next_to = spot[:main_axis] + [(spot[main_axis] + 1) % values.shape[main_axis]] + spot[main_axis + 1:]
    return values.at[tuple(spot)].set(low).at[tuple(next_to)].set(high)


def block_scale(own_key, extent, shards, least, largest):
    gain, own = 1.0, jax.random.fold_in(own_key, 6)
    for axis_at, shards_of in shards:
        draws = jnp.exp(jax.random.uniform(jax.random.fold_in(own, axis_at), (shards_of,), jnp.float32, least / len(shards), largest / len(shards)))
        gain = gain * jnp.repeat(draws, extent[axis_at] // shards_of).reshape([-1 if axis == axis_at else 1 for axis in range(len(extent))])
    return gain


def noise(rng, extent, scale, bound, pieces=(), held_as=jnp.bfloat16):
    values = jax.random.normal(rng, extent, jnp.float32) * scale
    if len(pieces) > 0:
        values = block_scale(rng, extent, pieces, -0.22, 0.18) * values
    return jnp.clip(values, min=-bound, max=bound).astype(held_as)


def setup_inputs(seed: int = 0) -> dict:
    seeds = jax.random.split(jax.random.key(seed), 5)
    loads = noise(seeds[0], (SLEEPERS, 3, NY, NZ), SLEEPERS ** -0.5, 1.0, ((0, 2), (2, 4), (3, 4)), jnp.float32)
    sleeper_pos = touch_ends(jax.random.randint(seeds[1], (SLEEPERS,), 0, KW), jax.random.fold_in(seeds[1], 1), 0, KW - 1).astype(jnp.int32)
    material = draw_material(jax.random.fold_in(seeds[4], 71), 0)
    material_table = draw_material_table(jax.random.fold_in(seeds[4], 71), 0)
    return {"loads": loads, "sleeper_pos": sleeper_pos, "material": material, "material_table": material_table}


def local_operator(padded, wavefield, coefficients, wave_square):
    neighbours = padded[..., 2:, 1:-1] + padded[..., :-2, 1:-1] + padded[..., 1:-1, 2:] + padded[..., 1:-1, :-2]
    components = [wavefield[..., row_no, :, :] for row_no in range(3)]
    coupling_index = ((1, 4, 5), (4, 2, 6), (5, 6, 3))
    coupled = jnp.stack([sum(coefficients[coupling_index[row_no][column_no]] * components[column_no] for column_no in range(3)) for row_no in range(3)], axis=-3)
    real_op = 4.0 * wavefield - neighbours + coefficients[0] * wavefield + wave_square * coupled
    damping = coefficients[7] * wave_square * wavefield
    rotated = jnp.stack([-damping[..., 1, :, :, :], damping[..., 0, :, :, :]], axis=-4)
    return real_op + rotated


def spectral_bounds(material_table, squares):
    shifts = material_table[:, 0]
    diagonal_part = material_table[:, 1:4]
    off_diagonal = jnp.abs(material_table[:, 4:7])
    row_sums = jnp.stack([off_diagonal[:, 0] + off_diagonal[:, 1], off_diagonal[:, 0] + off_diagonal[:, 2], off_diagonal[:, 1] + off_diagonal[:, 2]], axis=1)
    gersh_low = jnp.min(diagonal_part - row_sums, axis=1)
    gersh_high = jnp.max(diagonal_part + row_sums, axis=1)
    lowest = jnp.min(shifts[:, None] + gersh_low[:, None] * squares[None, :], axis=0)
    highest = 8.0 + jnp.max(shifts[:, None] + gersh_high[:, None] * squares[None, :], axis=0)
    return lowest, highest


def wave_squares(waves):
    return (2.0 * jnp.sin(waves.astype(jnp.float32) * (math.pi / KW))) ** 2


def phase_table(positions, waves):
    turn_index = (positions[:, None] * waves[None, :]) % KW
    angles = turn_index.astype(jnp.float32) * (2.0 * math.pi / KW)
    return jnp.cos(angles), jnp.sin(angles)


def chebyshev(source, operate, lowest, highest):
    center = 0.5 * (highest + lowest)
    half_width = 0.5 * (highest - lowest)
    center_ratio = center / half_width
    solution = jnp.zeros_like(source)
    for sweep_no in range(SWEEPS):
        residual = source if sweep_no == 0 else source - operate(solution)
        weight = 1.0 / center_ratio
        direction = residual / center
        for inner_no in range(DEG):
            solution = solution + direction
            if inner_no + 1 < DEG:
                residual = residual - operate(direction)
                weight_next = 1.0 / (2.0 * center_ratio - weight)
                direction = (weight_next * weight) * direction + (2.0 * weight_next / half_width) * residual
                weight = weight_next
    return solution


def reference(loads, sleeper_pos, material, material_table):
    coefficients = jnp.moveaxis(material_table[material], -1, 0)
    waves = jnp.arange(KW, dtype=jnp.int32)
    cosines, sines = phase_table(sleeper_pos, waves)
    squares = wave_squares(waves)
    lowest, highest = spectral_bounds(material_table, squares)

    def solve_wave(inputs):
        cos_column, sin_column, wave_square, low_bound, high_bound = inputs
        real_part = jnp.tensordot(cos_column, loads, axes=(0, 0), precision=lax.Precision.HIGHEST)
        imag_part = -jnp.tensordot(sin_column, loads, axes=(0, 0), precision=lax.Precision.HIGHEST)
        source = jnp.stack([real_part, imag_part], axis=0)

        def operate(wavefield):
            padded = jnp.pad(wavefield, ((0, 0), (0, 0), (1, 1), (1, 1)))
            return local_operator(padded, wavefield, coefficients, wave_square)

        return chebyshev(source, operate, low_bound, high_bound)

    return lax.map(solve_wave, (cosines.T, sines.T, squares, lowest, highest))
```

```python
import functools
import math

import jax
import jax.numpy as jnp
import numpy as np
from jax import lax
from jax.experimental import pallas as pl
from jax.experimental.pallas import tpu as pltpu
from jax.sharding import PartitionSpec as P

KW = 128
NMAT = 8
DEG = 4
LANES = 128
HALF = 64
SEGS = 16
HY = 7
HB = 8


def spectral_bounds(material_table, squares):
    shifts = material_table[:, 0]
    diagonal_part = material_table[:, 1:4]
    off_diagonal = jnp.abs(material_table[:, 4:7])
    row_sums = jnp.stack(
        [
            off_diagonal[:, 0] + off_diagonal[:, 1],
            off_diagonal[:, 0] + off_diagonal[:, 2],
            off_diagonal[:, 1] + off_diagonal[:, 2],
        ],
        axis=1,
    )
    gersh_low = jnp.min(diagonal_part - row_sums, axis=1)
    gersh_high = jnp.max(diagonal_part + row_sums, axis=1)
    lowest = jnp.min(shifts[:, None] + gersh_low[:, None] * squares[None, :], axis=0)
    highest = 8.0 + jnp.max(shifts[:, None] + gersh_high[:, None] * squares[None, :], axis=0)
    return (lowest, highest)


def wave_squares(waves):
    return (2.0 * jnp.sin(waves.astype(jnp.float32) * (math.pi / KW))) ** 2


def phase_table(positions, waves):
    turn_index = positions[:, None] * waves[None, :] % KW
    angles = turn_index.astype(jnp.float32) * (2.0 * math.pi / KW)
    return (jnp.cos(angles), jnp.sin(angles))


def short(values):
    return lax.reduce_precision(values, exponent_bits=8, mantissa_bits=7)


def tables(positions, material_table, waves):
    count = waves.shape[0]
    squares = wave_squares(waves)
    lowest, highest = spectral_bounds(material_table, squares)
    center = 0.5 * (highest + lowest)
    half_width = 0.5 * (highest - lowest)
    ratio2 = (center / half_width) ** 2
    top = 8.0 * ratio2 * (ratio2 - 1.0) + 1.0
    h2 = half_width * half_width
    h4 = h2 * h2
    scale = 8.0 / (top * h4)
    scale = scale * scale

    cosines, sines = phase_table(positions, waves)
    phases = jnp.stack([cosines * scale, -sines * scale], axis=1)
    phases = jnp.pad(phases, ((0, 0), (0, 0), (0, HALF - count)))
    high = short(phases)
    low = short(phases - high)
    stacked = jnp.stack([high, high, low, low])
    eye = jnp.eye(2, dtype=jnp.float32)
    t8 = eye[:, None, None, None, :, None] * stacked[None, :, :, :, None, :]
    t8 = t8.reshape(2 * 4 * positions.shape[0], 4 * HALF).astype(jnp.bfloat16)

    q = squares[None, :]
    entry = lambda column: material_table[:, column][:, None]
    fields = [center[None, :] - 4.0 - entry(0) - q * entry(c) for c in (1, 2, 3)]
    fields += [-q * entry(c) for c in (4, 5, 6)] + [q * entry(7)]
    fields = jnp.stack(fields, axis=1)
    fields = jnp.pad(fields, ((0, 0), (0, 0), (0, HALF - count)))
    first = short(fields)
    second = short(fields - first)
    third = short(fields - first - second)
    split = jnp.stack([first, second, third]).reshape(3 * NMAT, 7, HALF)
    split = jnp.pad(split, ((0, LANES - 3 * NMAT), (0, 0), (0, 0)))
    tc = eye[:, None, None, :, None] * split[None, :, :, None, :]
    tc = tc.reshape(2 * LANES, 7 * LANES).astype(jnp.bfloat16)

    vectors = jnp.stack([-h2, (top + 1.0) * h4 * 0.125, lowest * highest, center])
    vectors = jnp.pad(vectors, ((0, 0), (0, HALF - count)))
    vectors = jnp.broadcast_to(vectors[:, None, None, :], (4, 8, 2, HALF)).reshape(4, 8, LANES)
    return t8, tc, vectors


def placement(depth, sleepers, width):
    seglen = (depth + 2 * HB) // SEGS
    rows = -(-(8 * seglen) // 16) * 16
    perm = np.zeros((2, rows, depth), np.float32)
    permh = np.zeros((2, rows, 2 * HB), np.float32)
    for z in range(depth + 2 * HB):
        seg, at = divmod(z, seglen)
        half, sub = divmod(seg, 8)
        if z < HB:
            permh[half, at * 8 + sub, z] = 1
        elif z < HB + depth:
            perm[half, at * 8 + sub, z - HB] = 1
        else:
            permh[half, at * 8 + sub, z - depth] = 1
    rep = np.zeros((2, width, 3, 4, sleepers), np.float32)
    for c in range(3):
        for j in range(sleepers):
            for g in range(4):
                rep[g % 2, c * sleepers + j, c, g, j] = 1
    as_type = lambda a, r, c: jnp.asarray(a.reshape(r, c), dtype=jnp.bfloat16)
    return (
        as_type(perm, 2 * rows, depth),
        as_type(permh, 2 * rows, 2 * HB),
        as_type(rep, 2 * width, 12 * sleepers),
    )


def two_parts(values):
    high = values.astype(jnp.bfloat16)
    low = (values - high.astype(jnp.float32)).astype(jnp.bfloat16)
    return high, low


def dot(a, b):
    return lax.dot_general(a, b, (((1,), (0,)), ((), ())), preferred_element_type=jnp.float32)


def dot_t(a, b):
    return lax.dot_general(a, b, (((1,), (1,)), ((), ())), preferred_element_type=jnp.float32)


def edge_kernel(sleepers, height, planes, out):
    depth = planes.shape[1]
    width = out.shape[2]
    spot = lax.broadcasted_iota(jnp.int32, (16, depth), 0)
    at = lax.broadcasted_iota(jnp.int32, (16, depth), 1)
    pick = (at == jnp.where(spot < HB, spot, spot + (depth - 2 * HB))).astype(jnp.bfloat16)

    def one_row(row, carry):
        parts = [
            planes[pl.ds(c * height + row, sleepers, stride=3 * height), :] for c in range(3)
        ]
        material = planes[pl.ds(3 * sleepers * height + row, 1), :]
        parts.append(jnp.broadcast_to(material, (width - 3 * sleepers, depth)))
        high, low = two_parts(jnp.concatenate(parts, axis=0))
        out[row, :, :] = dot_t(pick, high) + dot_t(pick, low)
        return carry

    lax.fori_loop(0, height, one_row, 0)


def edges_of(planes, sleepers):
    height, depth = planes.shape[1:]
    width = -(-(3 * sleepers + 1) // LANES) * LANES
    return pl.pallas_call(
        functools.partial(edge_kernel, sleepers, height),
        out_shape=jax.ShapeDtypeStruct((height, 2 * HB, width), jnp.float32),
        in_specs=[pl.BlockSpec(memory_space=pltpu.VMEM)],
        out_specs=pl.BlockSpec(memory_space=pltpu.VMEM),
        compiler_params=pltpu.CompilerParams(vmem_limit_bytes=32 * 1024 * 1024),
        name="edge_columns",
    )(planes.reshape(-1, depth))


def field_kernel(
    sleepers, height, count, seglen,
    flags, planes, left, right, t8, tc, vectors, edge, perm, permh, rep,
    out, source, coefs, a1, a2, a3, wide, b1, b2, turn,
):
    depth = planes.shape[1]
    ny = height - 2 * HB
    group = 4 * sleepers
    rows = perm.shape[0] // 2
    cells = 8 * seglen
    block = pl.program_id(0)
    out_rows = out.reshape(count * 48, depth)
    lane = lax.broadcasted_iota(jnp.int32, (8, LANES), 1)
    sub = lax.broadcasted_iota(jnp.int32, (8, LANES), 0)

    def at(zm):
        return pl.ds(8 * (zm + 1), 8)

    def store_ghosts(dst, slot, q, first, last):
        before = pltpu.roll(last, 1, 0)
        after = pltpu.roll(first, 7, 0)
        dst[slot, q, at(-1), :] = jnp.where(sub == 0, pltpu.roll(before, HALF, 1), before)
        dst[slot, q, at(seglen), :] = jnp.where(sub == 7, pltpu.roll(after, HALF, 1), after)

    def produce(row):
        srow = row + (HB - HY)
        parts = []
        for c in range(3):
            high, low = two_parts(
                planes[pl.ds(c * height + srow, sleepers, stride=3 * height), :]
            )
            parts += [high, low, high, low]
        material = planes[pl.ds(3 * sleepers * height + srow, 1), :]
        number = lax.broadcasted_iota(jnp.int32, (LANES, depth), 0)
        kind = jnp.where(number < 3 * NMAT, number % NMAT, -1).astype(jnp.float32)
        parts.append((kind == material).astype(jnp.float32).astype(jnp.bfloat16))
        placed = dot_t(perm[...], jnp.concatenate(parts, axis=0))
        halo = jnp.concatenate([left[srow], right[srow]], axis=0)
        halo_high, halo_low = two_parts(halo)
        spread = dot(jnp.concatenate([halo_high, halo_low], axis=1), rep[...])
        number = lax.broadcasted_iota(jnp.int32, (2 * HB, LANES), 1)
        kind = jnp.where(number < 3 * NMAT, number % NMAT, -1).astype(jnp.float32)
        hot = kind == jnp.broadcast_to(halo[:, 3 * sleepers : 3 * sleepers + 1], kind.shape)
        spread = jnp.concatenate([spread, hot.astype(jnp.float32)], axis=1).astype(jnp.bfloat16)
        placed = placed + dot(permh[...], spread)
        low_half = placed[:rows].astype(jnp.bfloat16)
        high_half = placed[rows:].astype(jnp.bfloat16)
        slot = row & 7
        for c in range(3):
            span = slice(c * group, (c + 1) * group)
            both = jnp.concatenate([low_half[:, span], high_half[:, span]], axis=1)
            made = dot(both, t8[...])
            for part in range(2):
                q = part * 3 + c
                plane = made[:cells, part * LANES : (part + 1) * LANES]
                source[slot, q, 8 : 8 + cells, :] = plane
                store_ghosts(source, slot, q, plane[:8], plane[cells - 8 :])
        both = jnp.concatenate([low_half[:, 3 * group :], high_half[:, 3 * group :]], axis=1)
        made = dot(both, tc[...])
        for f in range(7):
            coefs[row & 15, f, :, :] = made[:cells, f * LANES : (f + 1) * LANES]

    def apply(src, size, row, emit, shift=None, extra=None):
        up, mid, down = ((row + d) & (size - 1) for d in (-1, 0, 1))
        field_slot = row & 15
        prev = [src[mid, q, at(-1), :] for q in range(6)]
        cur = [src[mid, q, at(0), :] for q in range(6)]
        for zm in range(seglen):
            nxt = [src[mid, q, at(zm + 1), :] for q in range(6)]
            f = [coefs[field_slot, n, pl.ds(8 * zm, 8), :] for n in range(7)]
            diagonal = f[:3]
            if shift is not None:
                diagonal = [d + shift for d in diagonal]
            matrix = (
                (diagonal[0], f[3], f[4]),
                (f[3], diagonal[1], f[5]),
                (f[4], f[5], diagonal[2]),
            )
            results = []
            for q in range(6):
                part, c = divmod(q, 3)
                near = (src[up, q, at(zm), :] + src[down, q, at(zm), :]) + (prev[q] + nxt[q])
                mine = cur[3 * part : 3 * part + 3]
                local = matrix[c][0] * mine[0] + matrix[c][1] * mine[1] + matrix[c][2] * mine[2]
                damp = f[6] * cur[3 * (1 - part) + c]
                total = near + local
                total = total + damp if part == 0 else total - damp
                if extra is not None:
                    other, other_slot, weight = extra
                    total = total + weight * other[other_slot, q, at(zm), :]
                results.append(total)
            emit(zm, results)
            prev, cur = cur, nxt

    def stage(src, size, dst, row, extra=None):
        slot = row & 3
        ends = {}

        def emit(zm, results):
            if zm == HB - 1:
                results = [value * edge[0] for value in results]
            if zm == (HB + depth) % seglen:
                results = [value * edge[1] for value in results]
            for q in range(6):
                dst[slot, q, at(zm), :] = results[q]
            if zm in (0, seglen - 1):
                ends[zm] = results

        apply(src, size, row, emit, extra=extra)
        for q in range(6):
            store_ghosts(dst, slot, q, ends[0][q], ends[seglen - 1][q])

        outside = ((row == HY - 1) & (flags[0] == 1)) | ((row == HY + ny) & (flags[1] == 1))

        @pl.when(outside)
        def _():
            for q in range(6):
                dst[slot, q, :, :] = jnp.zeros(dst.shape[2:], jnp.float32)

    def finish(row, line):
        def emit(zm, results):
            for c in range(3):
                real, imag = results[c], results[3 + c]
                first = jnp.where(lane < HALF, real, pltpu.roll(imag, HALF, 1))
                second = jnp.where(lane < HALF, pltpu.roll(real, HALF, 1), imag)
                turn[c, pl.ds(zm, 8, stride=seglen), :] = first
                turn[c, pl.ds(cells + zm, 8, stride=seglen), :] = second

        apply(b2, 4, row, emit, shift=vectors[3])
        for c in range(3):
            page = turn[c, HB : HB + depth, :]
            turned = jnp.transpose(page)
            for part in range(2):
                start = (part * 3 + c) * 8 + line
                out_rows[pl.ds(start, count, stride=48), :] = turned[
                    part * HALF : part * HALF + count
                ]

    def one_row(line, carry):
        row = 8 * block + line - (HB - 2 * HY % HB)

        @pl.when(row >= 0)
        def _():
            produce(row)

        @pl.when(row >= 2)
        def _():
            stage(source, 8, a1, row - 1)

        @pl.when(row >= 4)
        def _():
            stage(a1, 4, a2, row - 2, (source, (row - 2) & 7, vectors[0]))

        @pl.when(row >= 6)
        def _():
            stage(a2, 4, a3, row - 3)

        @pl.when(row >= 8)
        def _():
            stage(a3, 4, wide, row - 4, (source, (row - 4) & 7, vectors[1]))

        @pl.when(row >= 10)
        def _():
            stage(wide, 4, b1, row - 5)

        @pl.when(row >= 12)
        def _():
            stage(b1, 4, b2, row - 6, (wide, (row - 6) & 3, vectors[2]))

        @pl.when(row >= 14)
        def _():
            finish(row - 7, line)

        return carry

    lax.fori_loop(0, 8, one_row, 0)


def solve_field(flags, planes, left, right, t8, tc, vectors, edge, count):
    height, depth = planes.shape[1:]
    sleepers = t8.shape[0] // 8
    width = left.shape[2]
    ny = height - 2 * HB
    seglen = (depth + 2 * HB) // SEGS
    perm, permh, rep = placement(depth, sleepers, width)
    blocks = ny // 8
    ring = lambda size: pltpu.VMEM((size, 6, 8 * (seglen + 2), LANES), jnp.float32)
    whole = pl.BlockSpec(memory_space=pltpu.VMEM)
    return pl.pallas_call(
        functools.partial(field_kernel, sleepers, height, count, seglen),
        grid=(blocks + 2,),
        out_shape=jax.ShapeDtypeStruct((count, 2, 3, ny, depth), jnp.float32),
        in_specs=[pl.BlockSpec(memory_space=pltpu.SMEM)] + [whole] * 10,
        out_specs=pl.BlockSpec(
            (count, 2, 3, 8, depth), lambda b: (0, 0, 0, jnp.maximum(b - 2, 0), 0)
        ),
        scratch_shapes=[
            ring(8),
            pltpu.VMEM((16, 7, 8 * seglen, LANES), jnp.float32),
            ring(4), ring(4), ring(4), ring(4), ring(4), ring(4),
            pltpu.VMEM((3, SEGS * seglen, LANES), jnp.float32),
        ],
        compiler_params=pltpu.CompilerParams(
            dimension_semantics=("arbitrary",), vmem_limit_bytes=48 * 1024 * 1024
        ),
        name="adjoint_field",
    )(flags, planes.reshape(-1, depth), left, right, t8, tc, vectors, edge, perm, permh, rep)


def local(loads, sleeper_pos, material, material_table):
    ka = lax.axis_size("ka")
    gy, gz = lax.axis_size("gy"), lax.axis_size("gz")
    count = KW // ka
    waves = lax.axis_index("ka") * count + jnp.arange(count, dtype=jnp.int32)

    all_loads, all_pos = [loads], [sleeper_pos]
    for step in range(1, ka):
        turn = [(i, (i + step) % ka) for i in range(ka)]
        all_pos.append(lax.ppermute(sleeper_pos, "ka", turn))
        all_loads.append(lax.ppermute(loads, "ka", turn))
    positions = jnp.concatenate(all_pos)
    sleepers = positions.shape[0]
    ny, depth = material.shape
    planes = jnp.concatenate(
        [part.reshape(-1, ny, depth) for part in all_loads]
        + [material.astype(jnp.float32)[None]],
        axis=0,
    )

    def swap(low_part, high_part, axis, size):
        forward = [(i, i + 1) for i in range(size - 1)]
        backward = [(i + 1, i) for i in range(size - 1)]
        return lax.ppermute(high_part, axis, forward), lax.ppermute(low_part, axis, backward)

    above, below = swap(planes[:, :HB], planes[:, ny - HB :], "gy", gy)
    planes = jnp.concatenate([above, planes, below], axis=1)
    columns = edges_of(planes, sleepers)
    left, right = swap(columns[:, :HB], columns[:, HB:], "gz", gz)

    t8, tc, vectors = tables(positions, material_table, waves)
    y_at, z_at = lax.axis_index("gy"), lax.axis_index("gz")
    flags = jnp.stack([y_at == 0, y_at == gy - 1]).astype(jnp.int32)
    sub = jnp.arange(8)[:, None]
    lane = jnp.arange(LANES)[None, :]
    edge = jnp.stack(
        [
            jnp.where((z_at == 0) & (sub == 0) & (lane < HALF), 0.0, 1.0),
            jnp.where((z_at == gz - 1) & (sub == 7) & (lane >= HALF), 0.0, 1.0),
        ]
    ).astype(jnp.float32)
    return solve_field(flags, planes, left, right, t8, tc, vectors, edge, count)


def solution(mesh):
    return jax.shard_map(
        local,
        mesh=mesh,
        in_specs=(P("ka", None, "gy", "gz"), P("ka"), P("gy", "gz"), P()),
        out_specs=P("ka", None, None, "gy", "gz"),
        check_vma=False,
    )
```

```python
import functools
import math

import jax
import jax.numpy as jnp
from jax import lax
from jax.experimental import pallas as pl
from jax.experimental.pallas import tpu as pltpu
from jax.sharding import PartitionSpec as P

KW = 128
NMAT = 8
DEG = 4
LANES = 128
HALF = 64
SEGS = 16
HY = 7
HB = 8


def spectral_bounds(material_table, squares):
    shifts = material_table[:, 0]
    diagonal_part = material_table[:, 1:4]
    off_diagonal = jnp.abs(material_table[:, 4:7])
    row_sums = jnp.stack(
        [
            off_diagonal[:, 0] + off_diagonal[:, 1],
            off_diagonal[:, 0] + off_diagonal[:, 2],
            off_diagonal[:, 1] + off_diagonal[:, 2],
        ],
        axis=1,
    )
    gersh_low = jnp.min(diagonal_part - row_sums, axis=1)
    gersh_high = jnp.max(diagonal_part + row_sums, axis=1)
    lowest = jnp.min(shifts[:, None] + gersh_low[:, None] * squares[None, :], axis=0)
    highest = 8.0 + jnp.max(shifts[:, None] + gersh_high[:, None] * squares[None, :], axis=0)
    return (lowest, highest)


def wave_squares(waves):
    return (2.0 * jnp.sin(waves.astype(jnp.float32) * (math.pi / KW))) ** 2


def phase_table(positions, waves):
    turn_index = positions[:, None] * waves[None, :] % KW
    angles = turn_index.astype(jnp.float32) * (2.0 * math.pi / KW)
    return (jnp.cos(angles), jnp.sin(angles))


def short(values):
    return lax.reduce_precision(values, exponent_bits=8, mantissa_bits=7)


def tables(positions, material_table, waves, width):
    count = waves.shape[0]
    squares = wave_squares(waves)
    lowest, highest = spectral_bounds(material_table, squares)
    center = 0.5 * (highest + lowest)
    half_width = 0.5 * (highest - lowest)
    ratio2 = (center / half_width) ** 2
    top = 8.0 * ratio2 * (ratio2 - 1.0) + 1.0
    h2 = half_width * half_width
    h4 = h2 * h2
    scale = 8.0 / (top * h4)
    scale = scale * scale

    cosines, sines = phase_table(positions, waves)
    phases = jnp.stack([cosines * scale, -sines * scale], axis=1)
    phases = jnp.pad(phases, ((0, 0), (0, 0), (0, HALF - count)))
    high = short(phases)
    low = short(phases - high)
    eye = jnp.eye(2, dtype=jnp.float32)
    three = jnp.eye(3, dtype=jnp.float32)
    spare = width - 3 * positions.shape[0]

    def blocks(table):
        wide = three[:, None, :, None, None] * table[None, :, None, :, :]
        wide = wide.reshape(3 * positions.shape[0], 6, HALF)
        wide = jnp.pad(wide, ((0, spare), (0, 0), (0, 0)))
        wide = eye[:, None, None, :, None] * wide[None, :, :, None, :]
        return wide.reshape(2 * width, 6 * LANES).astype(jnp.bfloat16)

    tw = jnp.concatenate([blocks(high), blocks(high), blocks(low)], axis=0)

    q = squares[None, :]
    entry = lambda column: material_table[:, column][:, None]
    fields = [center[None, :] - 4.0 - entry(0) - q * entry(c) for c in (1, 2, 3)]
    fields += [-q * entry(c) for c in (4, 5, 6)] + [q * entry(7)]
    fields = jnp.stack(fields, axis=1)
    fields = jnp.pad(fields, ((0, 0), (0, 0), (0, HALF - count)))
    first = short(fields)
    second = short(fields - first)
    third = short(fields - first - second)
    split = jnp.stack([first, second, third]).reshape(3 * NMAT, 7, HALF)
    split = jnp.pad(split, ((width - spare, spare - 3 * NMAT), (0, 0), (0, 0)))
    tc = eye[:, None, None, :, None] * split[None, :, :, None, :]
    tc = jnp.pad(tc.reshape(2 * width, 7 * LANES), ((0, 0), (0, LANES))).astype(jnp.bfloat16)

    vectors = jnp.stack([-h2, (top + 1.0) * h4 * 0.125, lowest * highest, center])
    vectors = jnp.pad(vectors, ((0, 0), (0, HALF - count)))
    vectors = jnp.broadcast_to(vectors[:, None, None, :], (4, 8, 2, HALF)).reshape(4, 8, LANES)
    return tw, tc, vectors


def lanes_for(sleepers):
    return -(-(3 * sleepers + 3 * NMAT) // LANES) * LANES


def two_parts(values):
    high = values.astype(jnp.bfloat16)
    low = (values - high.astype(jnp.float32)).astype(jnp.bfloat16)
    return high, low


def dot(a, b):
    return lax.dot_general(a, b, (((1,), (0,)), ((), ())), preferred_element_type=jnp.float32)


def dot_t(a, b):
    return lax.dot_general(a, b, (((1,), (1,)), ((), ())), preferred_element_type=jnp.float32)


def row_values(planes, row, height, sleepers, width):
    depth = planes.shape[1]
    parts = [planes[pl.ds(c * height + row, sleepers, stride=3 * height), :] for c in range(3)]
    material = planes[pl.ds(3 * sleepers * height + row, 1), :]
    number = lax.broadcasted_iota(jnp.int32, (width - 3 * sleepers, depth), 0)
    kind = jnp.where(number < 3 * NMAT, number % NMAT, -1).astype(jnp.float32)
    parts.append((kind == material).astype(jnp.float32))
    return jnp.concatenate(parts, axis=0)


def edge_kernel(sleepers, height, planes, out):
    depth = planes.shape[1]
    width = out.shape[2]
    spot = lax.broadcasted_iota(jnp.int32, (2 * HB, depth), 0)
    at = lax.broadcasted_iota(jnp.int32, (2 * HB, depth), 1)
    pick = (at == jnp.where(spot < HB, spot, spot + (depth - 2 * HB))).astype(jnp.bfloat16)

    def some_rows(block, carry):
        for line in range(8):
            row = 8 * block + line
            high, low = two_parts(row_values(planes, row, height, sleepers, width))
            out[row, :, :] = dot_t(pick, high) + dot_t(pick, low)
        return carry

    lax.fori_loop(0, height // 8, some_rows, 0)


def edges_of(planes, sleepers):
    height, depth = planes.shape[1:]
    return pl.pallas_call(
        functools.partial(edge_kernel, sleepers, height),
        out_shape=jax.ShapeDtypeStruct((height, 2 * HB, lanes_for(sleepers)), jnp.float32),
        in_specs=[pl.BlockSpec(memory_space=pltpu.VMEM)],
        out_specs=pl.BlockSpec(memory_space=pltpu.VMEM),
        compiler_params=pltpu.CompilerParams(vmem_limit_bytes=32 * 1024 * 1024),
        name="edge_columns",
    )(planes.reshape(-1, depth))


def field_kernel(
    sleepers, height, count, seglen,
    flags, planes, left, right, tw, tc, vectors, edge,
    out, source, coefs, a1, a2, a3, wide, b1, b2, turn, cells_of,
):
    depth = planes.shape[1]
    ny = height - 2 * HB
    width = left.shape[2]
    cells = 8 * seglen
    block = pl.program_id(0)
    out_rows = out.reshape(count * 48, depth)
    lane = lax.broadcasted_iota(jnp.int32, (8, LANES), 1)
    sub = lax.broadcasted_iota(jnp.int32, (8, LANES), 0)

    def at(zm):
        return pl.ds(8 * (zm + 1), 8)

    def store_ghosts(dst, slot, q, first, last):
        before = pltpu.roll(last, 1, 0)
        after = pltpu.roll(first, 7, 0)
        dst[slot, q, at(-1), :] = jnp.where(sub == 0, pltpu.roll(before, HALF, 1), before)
        dst[slot, q, at(seglen), :] = jnp.where(sub == 7, pltpu.roll(after, HALF, 1), after)

    def produce(first_row):
        halves = [[], []]
        for k in range(2):
            srow = first_row + k + (HB - HY)
            values = row_values(planes, srow, height, sleepers, width)
            for n in range(width // LANES):
                span = slice(n * LANES, (n + 1) * LANES)
                cells_of[k, n, HB : HB + depth, :] = jnp.transpose(values[span])
                cells_of[k, n, :HB, :] = left[srow, :, span]
                cells_of[k, n, HB + depth :, :] = right[srow, :, span]
        for k in range(2):
            for half in range(2):
                for zm in range(seglen):
                    spot = pl.ds(half * cells + zm, 8, stride=seglen)
                    pieces = [cells_of[k, n, spot, :] for n in range(width // LANES)]
                    halves[half].append(jnp.concatenate(pieces, axis=1))
        values = [jnp.concatenate(half, axis=0) for half in halves]
        parts = [two_parts(value) for value in values]
        high = jnp.concatenate([parts[0][0], parts[1][0]], axis=1)
        low = jnp.concatenate([parts[0][1], parts[1][1]], axis=1)
        three = jnp.concatenate([high, low, high], axis=1)
        for c in range(3):
            made = dot(three, tw[:, 2 * c * LANES : 2 * (c + 1) * LANES])
            for k in range(2):
                slot = (first_row + k) & 7
                for part in range(2):
                    q = part * 3 + c
                    plane = made[k * cells : (k + 1) * cells, part * LANES : (part + 1) * LANES]
                    source[slot, q, 8 : 8 + cells, :] = plane
                    store_ghosts(source, slot, q, plane[:8], plane[cells - 8 :])
        for f in range(0, 7, 2):
            made = dot(high, tc[:, f * LANES : (f + 2) * LANES])
            for k in range(2):
                slot = (first_row + k) & 15
                for g in range(f, min(f + 2, 7)):
                    coefs[slot, g, :, :] = made[
                        k * cells : (k + 1) * cells, (g - f) * LANES : (g - f + 1) * LANES
                    ]

    def apply(src, size, row, emit, shift=None, extra=None):
        slots = [(row + d) & (size - 1) for d in (-1, 0, 1, 2)]
        prev = [[src[slots[k + 1], q, at(-1), :] for q in range(6)] for k in range(2)]
        cur = [[src[slots[k + 1], q, at(0), :] for q in range(6)] for k in range(2)]
        for zm in range(seglen):
            nxt = [[src[slots[k + 1], q, at(zm + 1), :] for q in range(6)] for k in range(2)]
            for k in range(2):
                f = [coefs[(row + k) & 15, n, pl.ds(8 * zm, 8), :] for n in range(7)]
                diagonal = f[:3]
                if shift is not None:
                    diagonal = [d + shift for d in diagonal]
                matrix = (
                    (diagonal[0], f[3], f[4]),
                    (f[3], diagonal[1], f[5]),
                    (f[4], f[5], diagonal[2]),
                )
                results = []
                for q in range(6):
                    part, c = divmod(q, 3)
                    outer = src[slots[3 * k], q, at(zm), :]
                    near = (outer + cur[1 - k][q]) + (prev[k][q] + nxt[k][q])
                    mine = cur[k][3 * part : 3 * part + 3]
                    own = matrix[c][0] * mine[0] + matrix[c][1] * mine[1] + matrix[c][2] * mine[2]
                    damp = f[6] * cur[k][3 * (1 - part) + c]
                    total = near + own
                    total = total + damp if part == 0 else total - damp
                    if extra is not None:
                        other, other_size, weight = extra
                        slot = (row + k) & (other_size - 1)
                        total = total + weight * other[slot, q, at(zm), :]
                    results.append(total)
                emit(k, zm, results)
            prev, cur = cur, nxt

    def stage(src, size, dst, row, extra=None):
        ends = {}

        def emit(k, zm, results):
            if zm == HB - 1:
                results = [value * edge[0] for value in results]
            if zm == (HB + depth) % seglen:
                results = [value * edge[1] for value in results]
            for q in range(6):
                dst[(row + k) & 3, q, at(zm), :] = results[q]
            if zm in (0, seglen - 1):
                ends[k, zm] = results
            if zm == seglen - 1:
                for q in range(6):
                    store_ghosts(dst, (row + k) & 3, q, ends[k, 0][q], results[q])

        apply(src, size, row, emit, extra=extra)
        for k in range(2):
            spot = row + k
            outside = ((spot == HY - 1) & (flags[0] == 1)) | ((spot == HY + ny) & (flags[1] == 1))

            @pl.when(outside)
            def _():
                for q in range(6):
                    dst[spot & 3, q, :, :] = jnp.zeros(dst.shape[2:], jnp.float32)

    def finish(row, line):
        def emit(k, zm, results):
            for c in range(3):
                real, imag = results[c], results[3 + c]
                first = jnp.where(lane < HALF, real, pltpu.roll(imag, HALF, 1))
                second = jnp.where(lane < HALF, pltpu.roll(real, HALF, 1), imag)
                turn[3 * k + c, pl.ds(zm, 8, stride=seglen), :] = first
                turn[3 * k + c, pl.ds(cells + zm, 8, stride=seglen), :] = second

        apply(b2, 4, row, emit, shift=vectors[3])
        for k in range(2):
            for c in range(3):
                turned = jnp.transpose(turn[3 * k + c, HB : HB + depth, :])
                for part in range(2):
                    start = (part * 3 + c) * 8 + line + k
                    out_rows[pl.ds(start, count, stride=48), :] = turned[
                        part * HALF : part * HALF + count
                    ]

    def two_rows(pair, carry):
        base = 8 * block + 2 * pair - 2

        @pl.when(base >= 0)
        def _():
            produce(base)

        @pl.when(base >= 2)
        def _():
            stage(source, 8, a1, base - 1)

        @pl.when(base >= 4)
        def _():
            stage(a1, 4, a2, base - 2, (source, 8, vectors[0]))

        @pl.when(base >= 6)
        def _():
            stage(a2, 4, a3, base - 3)

        @pl.when(base >= 8)
        def _():
            stage(a3, 4, wide, base - 4, (source, 8, vectors[1]))

        @pl.when(base >= 10)
        def _():
            stage(wide, 4, b1, base - 5)

        @pl.when(base >= 12)
        def _():
            stage(b1, 4, b2, base - 6, (wide, 4, vectors[2]))

        @pl.when(base >= 14)
        def _():
            finish(base - 7, 2 * pair)

        return carry

    lax.fori_loop(0, 4, two_rows, 0)


def solve_field(flags, planes, left, right, tw, tc, vectors, edge, sleepers, count):
    height, depth = planes.shape[1:]
    width = left.shape[2]
    ny = height - 2 * HB
    seglen = (depth + 2 * HB) // SEGS
    blocks = ny // 8
    ring = lambda size: pltpu.VMEM((size, 6, 8 * (seglen + 2), LANES), jnp.float32)
    whole = pl.BlockSpec(memory_space=pltpu.VMEM)
    return pl.pallas_call(
        functools.partial(field_kernel, sleepers, height, count, seglen),
        grid=(blocks + 2,),
        out_shape=jax.ShapeDtypeStruct((count, 2, 3, ny, depth), jnp.float32),
        in_specs=[pl.BlockSpec(memory_space=pltpu.SMEM)] + [whole] * 7,
        out_specs=pl.BlockSpec(
            (count, 2, 3, 8, depth), lambda b: (0, 0, 0, jnp.maximum(b - 2, 0), 0)
        ),
        scratch_shapes=[
            ring(8),
            pltpu.VMEM((16, 7, 8 * seglen, LANES), jnp.float32),
            ring(4), ring(4), ring(4), ring(4), ring(4), ring(4),
            pltpu.VMEM((6, SEGS * seglen, LANES), jnp.float32),
            pltpu.VMEM((2, width // LANES, SEGS * seglen, LANES), jnp.float32),
        ],
        compiler_params=pltpu.CompilerParams(
            dimension_semantics=("arbitrary",), vmem_limit_bytes=56 * 1024 * 1024
        ),
        name="adjoint_field",
    )(flags, planes.reshape(-1, depth), left, right, tw, tc, vectors, edge)


def local(loads, sleeper_pos, material, material_table):
    ka = lax.axis_size("ka")
    gy, gz = lax.axis_size("gy"), lax.axis_size("gz")
    count = KW // ka
    waves = lax.axis_index("ka") * count + jnp.arange(count, dtype=jnp.int32)

    all_loads, all_pos = [loads], [sleeper_pos]
    for step in range(1, ka):
        turn = [(i, (i + step) % ka) for i in range(ka)]
        all_pos.append(lax.ppermute(sleeper_pos, "ka", turn))
        all_loads.append(lax.ppermute(loads, "ka", turn))
    positions = jnp.concatenate(all_pos)
    sleepers = positions.shape[0]
    ny, depth = material.shape
    planes = jnp.concatenate(
        [part.reshape(-1, ny, depth) for part in all_loads]
        + [material.astype(jnp.float32)[None]],
        axis=0,
    )

    def swap(low_part, high_part, axis, size):
        forward = [(i, i + 1) for i in range(size - 1)]
        backward = [(i + 1, i) for i in range(size - 1)]
        return lax.ppermute(high_part, axis, forward), lax.ppermute(low_part, axis, backward)

    above, below = swap(planes[:, :HB], planes[:, ny - HB :], "gy", gy)
    planes = jnp.concatenate([above, planes, below], axis=1)
    columns = edges_of(planes, sleepers)
    left, right = swap(columns[:, :HB], columns[:, HB:], "gz", gz)

    tw, tc, vectors = tables(positions, material_table, waves, lanes_for(sleepers))
    y_at, z_at = lax.axis_index("gy"), lax.axis_index("gz")
    flags = jnp.stack([y_at == 0, y_at == gy - 1]).astype(jnp.int32)
    sub = jnp.arange(8)[:, None]
    lane = jnp.arange(LANES)[None, :]
    edge = jnp.stack(
        [
            jnp.where((z_at == 0) & (sub == 0) & (lane < HALF), 0.0, 1.0),
            jnp.where((z_at == gz - 1) & (sub == 7) & (lane >= HALF), 0.0, 1.0),
        ]
    ).astype(jnp.float32)
    return solve_field(flags, planes, left, right, tw, tc, vectors, edge, sleepers, count)


def solution(mesh):
    return jax.shard_map(
        local,
        mesh=mesh,
        in_specs=(P("ka", None, "gy", "gz"), P("ka"), P("gy", "gz"), P()),
        out_specs=P("ka", None, None, "gy", "gz"),
        check_vma=False,
    )
```

```python
import functools
import math

import jax
import jax.numpy as jnp
from jax import lax
from jax.experimental import pallas as pl
from jax.experimental.pallas import tpu as pltpu
from jax.sharding import PartitionSpec as P

KW = 128
NMAT = 8
DEG = 4
LANES = 128
HALF = 64
SEGS = 16
HY = 7
HB = 8


def spectral_bounds(material_table, squares):
    shifts = material_table[:, 0]
    diagonal_part = material_table[:, 1:4]
    off_diagonal = jnp.abs(material_table[:, 4:7])
    row_sums = jnp.stack(
        [
            off_diagonal[:, 0] + off_diagonal[:, 1],
            off_diagonal[:, 0] + off_diagonal[:, 2],
            off_diagonal[:, 1] + off_diagonal[:, 2],
        ],
        axis=1,
    )
    gersh_low = jnp.min(diagonal_part - row_sums, axis=1)
    gersh_high = jnp.max(diagonal_part + row_sums, axis=1)
    lowest = jnp.min(shifts[:, None] + gersh_low[:, None] * squares[None, :], axis=0)
    highest = 8.0 + jnp.max(shifts[:, None] + gersh_high[:, None] * squares[None, :], axis=0)
    return (lowest, highest)


def wave_squares(waves):
    return (2.0 * jnp.sin(waves.astype(jnp.float32) * (math.pi / KW))) ** 2


def phase_table(positions, waves):
    turn_index = positions[:, None] * waves[None, :] % KW
    angles = turn_index.astype(jnp.float32) * (2.0 * math.pi / KW)
    return (jnp.cos(angles), jnp.sin(angles))


def short(values):
    return lax.reduce_precision(values, exponent_bits=8, mantissa_bits=7)


def tables(positions, material_table, waves, width):
    count = waves.shape[0]
    squares = wave_squares(waves)
    lowest, highest = spectral_bounds(material_table, squares)
    center = 0.5 * (highest + lowest)
    half_width = 0.5 * (highest - lowest)
    ratio2 = (center / half_width) ** 2
    top = 8.0 * ratio2 * (ratio2 - 1.0) + 1.0
    h2 = half_width * half_width
    h4 = h2 * h2
    scale = 8.0 / (top * h4)
    scale = scale * scale

    cosines, sines = phase_table(positions, waves)
    phases = jnp.stack([cosines * scale, -sines * scale], axis=1)
    phases = jnp.pad(phases, ((0, 0), (0, 0), (0, HALF - count)))
    high = short(phases)
    low = short(phases - high)
    eye = jnp.eye(2, dtype=jnp.float32)
    three = jnp.eye(3, dtype=jnp.float32)
    spare = width - 3 * positions.shape[0]

    def blocks(table):
        wide = three[:, None, :, None, None] * table[None, :, None, :, :]
        wide = wide.reshape(3 * positions.shape[0], 6, HALF)
        wide = jnp.pad(wide, ((0, spare), (0, 0), (0, 0)))
        wide = eye[:, None, None, :, None] * wide[None, :, :, None, :]
        return wide.reshape(2 * width, 6 * LANES).astype(jnp.bfloat16)

    tw = jnp.concatenate([blocks(high), blocks(high), blocks(low)], axis=0)

    q = squares[None, :]
    entry = lambda column: material_table[:, column][:, None]
    fields = [center[None, :] - 4.0 - entry(0) - q * entry(c) for c in (1, 2, 3)]
    fields += [-q * entry(c) for c in (4, 5, 6)] + [q * entry(7)]
    fields = jnp.stack(fields, axis=1)
    fields = jnp.pad(fields, ((0, 0), (0, 0), (0, HALF - count)))
    first = short(fields)
    second = short(fields - first)
    third = short(fields - first - second)
    split = jnp.stack([first, second, third]).reshape(3 * NMAT, 7, HALF)
    split = jnp.pad(split, ((width - spare, spare - 3 * NMAT), (0, 0), (0, 0)))
    tc = eye[:, None, None, :, None] * split[None, :, :, None, :]
    tc = jnp.pad(tc.reshape(2 * width, 7 * LANES), ((0, 0), (0, LANES))).astype(jnp.bfloat16)

    vectors = jnp.stack([-h2, (top + 1.0) * h4 * 0.125, lowest * highest, center])
    vectors = jnp.pad(vectors, ((0, 0), (0, HALF - count)))
    vectors = jnp.broadcast_to(vectors[:, None, None, :], (4, 8, 2, HALF)).reshape(4, 8, LANES)
    return tw, tc, vectors


def lanes_for(sleepers):
    return -(-(3 * sleepers + 3 * NMAT) // LANES) * LANES


def two_parts(values):
    high = values.astype(jnp.bfloat16)
    low = (values - high.astype(jnp.float32)).astype(jnp.bfloat16)
    return high, low


def dot(a, b):
    return lax.dot_general(a, b, (((1,), (0,)), ((), ())), preferred_element_type=jnp.float32)


def dot_t(a, b):
    return lax.dot_general(a, b, (((1,), (1,)), ((), ())), preferred_element_type=jnp.float32)


def row_values(planes, row, height, sleepers, width):
    depth = planes.shape[1]
    parts = [planes[pl.ds(c * height + row, sleepers, stride=3 * height), :] for c in range(3)]
    material = planes[pl.ds(3 * sleepers * height + row, 1), :]
    number = lax.broadcasted_iota(jnp.int32, (width - 3 * sleepers, depth), 0)
    kind = jnp.where(number < 3 * NMAT, number % NMAT, -1).astype(jnp.float32)
    parts.append((kind == material).astype(jnp.float32))
    return jnp.concatenate(parts, axis=0)


def gather(spots, pieces, planes, sems):
    copies = []
    for n, (piece, first, count, plane, row, target) in enumerate(spots):
        src = pieces[piece]
        copies.append(
            pltpu.make_async_copy(
                src.at[plane : plane + count, row[0] : row[0] + row[1], :],
                planes.at[first : first + count, target : target + row[1], :],
                sems.at[n],
            )
        )
    for copy in copies:
        copy.start()
    for copy in copies:
        copy.wait()


def edge_kernel(sleepers, spots, *refs):
    *pieces, out, planes, sems = refs
    gather(spots, pieces, planes, sems)
    height, depth = planes.shape[1:]
    width = out.shape[2]
    spot = lax.broadcasted_iota(jnp.int32, (2 * HB, depth), 0)
    at = lax.broadcasted_iota(jnp.int32, (2 * HB, depth), 1)
    pick = (at == jnp.where(spot < HB, spot, spot + (depth - 2 * HB))).astype(jnp.bfloat16)
    flat = planes.reshape(planes.shape[0] * height, depth)

    def some_rows(block, carry):
        for line in range(8):
            row = 8 * block + line
            high, low = two_parts(row_values(flat, row, height, sleepers, width))
            out[row, :, :] = dot_t(pick, high) + dot_t(pick, low)
        return carry

    lax.fori_loop(0, height // 8, some_rows, 0)


def edges_of(spots, pieces, sleepers, height, depth):
    return pl.pallas_call(
        functools.partial(edge_kernel, sleepers, spots),
        out_shape=jax.ShapeDtypeStruct((height, 2 * HB, lanes_for(sleepers)), jnp.float32),
        in_specs=[pl.BlockSpec(memory_space=pl.ANY)] * len(pieces),
        out_specs=pl.BlockSpec(memory_space=pltpu.VMEM),
        scratch_shapes=[
            pltpu.VMEM((3 * sleepers + 1, height, depth), jnp.float32),
            pltpu.SemaphoreType.DMA((len(spots),)),
        ],
        compiler_params=pltpu.CompilerParams(vmem_limit_bytes=32 * 1024 * 1024),
        name="edge_columns",
    )(*pieces)


def field_kernel(sleepers, count, seglen, spots, *refs):
    flags, left, right, tw, tc, vectors, edge, *pieces = refs[: 7 + len(refs) - 21]
    (out, planes, sems, source, ghosts, coefs, lhs,
     a1, a2, a3, wide, b1, b2, turn) = refs[7 + len(refs) - 21 :]
    height, depth = planes.shape[1:]
    flat = planes.reshape(planes.shape[0] * height, depth)
    ny = height - 2 * HB
    width = left.shape[2]
    cells = 8 * seglen
    block = pl.program_id(0)
    out_rows = out.reshape(count * 48, depth)
    lane = lax.broadcasted_iota(jnp.int32, (8, LANES), 1)
    sub = lax.broadcasted_iota(jnp.int32, (8, LANES), 0)

    @pl.when(block == 0)
    def _():
        gather(spots, pieces, planes, sems)

    def at(zm):
        return pl.ds(8 * (zm + 1), 8)

    def around(first, last):
        before = pltpu.roll(last, 1, 0)
        after = pltpu.roll(first, 7, 0)
        return (
            jnp.where(sub == 0, pltpu.roll(before, HALF, 1), before),
            jnp.where(sub == 7, pltpu.roll(after, HALF, 1), after),
        )

    def store_ghosts(dst, slot, q, first, last):
        dst[slot, q, at(-1), :], dst[slot, q, at(seglen), :] = around(first, last)

    def line_at(row, zm):
        return pl.ds(pl.multiple_of(((row + 2) & 15) * cells, 8) + 8 * zm, 8)

    def column(q):
        part, c = divmod(q, 3)
        return slice((2 * c + part) * LANES, (2 * c + part + 1) * LANES)

    def read_source(row, q, zm):
        if zm == -1:
            return ghosts[(row + 2) & 15, q, :8, :]
        if zm == seglen:
            return ghosts[(row + 2) & 15, q, 8:, :]
        return source[line_at(row, zm), column(q)]

    def reader(ring):
        return lambda row, q, zm: ring[row & 3, q, at(zm), :]

    def produce():
        chunks = width // LANES
        for line in range(8):
            srow = jnp.maximum(8 * block + line - 2 + (HB - HY), 0)
            values = row_values(flat, srow, height, sleepers, width)
            for n in range(chunks):
                span = slice(n * LANES, (n + 1) * LANES)
                turn[line * chunks + n, HB : HB + depth, :] = jnp.transpose(values[span])
                turn[line * chunks + n, :HB, :] = left[srow, :, span]
                turn[line * chunks + n, HB + depth :, :] = right[srow, :, span]
        for pair in range(4):
            halves = [[], []]
            for line in (2 * pair, 2 * pair + 1):
                for half in range(2):
                    for zm in range(seglen):
                        spot = pl.ds(half * cells + zm, 8, stride=seglen)
                        pieces_at = [turn[line * chunks + n, spot, :] for n in range(chunks)]
                        halves[half].append(jnp.concatenate(pieces_at, axis=1))
            values = jnp.concatenate(
                [jnp.concatenate(half, axis=0) for half in halves], axis=1
            )
            high, low = two_parts(values)
            rows = slice(2 * pair * cells, 2 * (pair + 1) * cells)
            lhs[rows, : 2 * width] = high
            lhs[rows, 2 * width : 4 * width] = low
            lhs[rows, 4 * width :] = high
        target = pl.ds(pl.multiple_of((block & 1) * (8 * cells), 8), 8 * cells)
        for c in range(3):
            span = slice(2 * c * LANES, 2 * (c + 1) * LANES)
            source[target, span] = dot(lhs[...], tw[:, span])
        for f in range(0, 8, 2):
            span = slice(f * LANES, (f + 2) * LANES)
            coefs[target, span] = dot(lhs[:, : 2 * width], tc[:, span])
        for line in range(8):
            row = 8 * block - 2 + line
            for q in range(6):
                first = read_source(row, q, 0)
                last = read_source(row, q, seglen - 1)
                ghosts[(row + 2) & 15, q, :8, :], ghosts[(row + 2) & 15, q, 8:, :] = around(
                    first, last
                )

    def apply(src, row, emit, shift=None, extra=None):
        prev = [[src(row + k, q, -1) for q in range(6)] for k in range(2)]
        cur = [[src(row + k, q, 0) for q in range(6)] for k in range(2)]
        for zm in range(seglen):
            nxt = [[src(row + k, q, zm + 1) for q in range(6)] for k in range(2)]
            for k in range(2):
                f = [
                    coefs[line_at(row + k, zm), n * LANES : (n + 1) * LANES] for n in range(7)
                ]
                diagonal = f[:3]
                if shift is not None:
                    diagonal = [d + shift for d in diagonal]
                matrix = (
                    (diagonal[0], f[3], f[4]),
                    (f[3], diagonal[1], f[5]),
                    (f[4], f[5], diagonal[2]),
                )
                results = []
                for q in range(6):
                    part, c = divmod(q, 3)
                    outer = src(row + 3 * k - 1, q, zm)
                    near = (outer + cur[1 - k][q]) + (prev[k][q] + nxt[k][q])
                    mine = cur[k][3 * part : 3 * part + 3]
                    own = matrix[c][0] * mine[0] + matrix[c][1] * mine[1] + matrix[c][2] * mine[2]
                    damp = f[6] * cur[k][3 * (1 - part) + c]
                    total = near + own
                    total = total + damp if part == 0 else total - damp
                    if extra is not None:
                        other, weight = extra
                        total = total + weight * other(row + k, q, zm)
                    results.append(total)
                emit(k, zm, results)
            prev, cur = cur, nxt

    def stage(src, dst, row, extra=None):
        ends = {}

        def emit(k, zm, results):
            if zm == HB - 1:
                results = [value * edge[0] for value in results]
            if zm == (HB + depth) % seglen:
                results = [value * edge[1] for value in results]
            for q in range(6):
                dst[(row + k) & 3, q, at(zm), :] = results[q]
            if zm in (0, seglen - 1):
                ends[k, zm] = results
            if zm == seglen - 1:
                for q in range(6):
                    store_ghosts(dst, (row + k) & 3, q, ends[k, 0][q], results[q])

        apply(src, row, emit, extra=extra)
        for k in range(2):
            spot = row + k
            outside = ((spot == HY - 1) & (flags[0] == 1)) | ((spot == HY + ny) & (flags[1] == 1))

            @pl.when(outside)
            def _():
                for q in range(6):
                    dst[spot & 3, q, :, :] = jnp.zeros(dst.shape[2:], jnp.float32)

    def finish(row, line):
        def emit(k, zm, results):
            for c in range(3):
                real, imag = results[c], results[3 + c]
                first = jnp.where(lane < HALF, real, pltpu.roll(imag, HALF, 1))
                second = jnp.where(lane < HALF, pltpu.roll(real, HALF, 1), imag)
                turn[3 * k + c, pl.ds(zm, 8, stride=seglen), :] = first
                turn[3 * k + c, pl.ds(cells + zm, 8, stride=seglen), :] = second

        apply(reader(b2), row, emit, shift=vectors[3])
        for k in range(2):
            for c in range(3):
                turned = jnp.transpose(turn[3 * k + c, HB : HB + depth, :])
                for part in range(2):
                    start = (part * 3 + c) * 8 + line + k
                    out_rows[pl.ds(start, count, stride=48), :] = turned[
                        part * HALF : part * HALF + count
                    ]

    def two_rows(pair, carry):
        base = 8 * block + 2 * pair - 2

        @pl.when(base >= 2)
        def _():
            stage(read_source, a1, base - 1)

        @pl.when(base >= 4)
        def _():
            stage(reader(a1), a2, base - 2, (read_source, vectors[0]))

        @pl.when(base >= 6)
        def _():
            stage(reader(a2), a3, base - 3)

        @pl.when(base >= 8)
        def _():
            stage(reader(a3), wide, base - 4, (read_source, vectors[1]))

        @pl.when(base >= 10)
        def _():
            stage(reader(wide), b1, base - 5)

        @pl.when(base >= 12)
        def _():
            stage(reader(b1), b2, base - 6, (reader(wide), vectors[2]))

        @pl.when(base >= 14)
        def _():
            finish(base - 7, 2 * pair)

        return carry

    produce()
    lax.fori_loop(0, 4, two_rows, 0)


def solve_field(spots, pieces, flags, left, right, tw, tc, vectors, edge, sleepers, count):
    height, _, width = left.shape
    depth = pieces[0].shape[2]
    ny = height - 2 * HB
    seglen = (depth + 2 * HB) // SEGS
    blocks = ny // 8
    ring = pltpu.VMEM((4, 6, 8 * (seglen + 2), LANES), jnp.float32)
    whole = pl.BlockSpec(memory_space=pltpu.VMEM)
    return pl.pallas_call(
        functools.partial(field_kernel, sleepers, count, seglen, spots),
        grid=(blocks + 2,),
        out_shape=jax.ShapeDtypeStruct((count, 2, 3, ny, depth), jnp.float32),
        in_specs=[pl.BlockSpec(memory_space=pltpu.SMEM)]
        + [whole] * 6
        + [pl.BlockSpec(memory_space=pl.ANY)] * len(pieces),
        out_specs=pl.BlockSpec(
            (count, 2, 3, 8, depth), lambda b: (0, 0, 0, jnp.maximum(b - 2, 0), 0)
        ),
        scratch_shapes=[
            pltpu.VMEM((3 * sleepers + 1, height, depth), jnp.float32),
            pltpu.SemaphoreType.DMA((len(spots),)),
            pltpu.VMEM((16 * 8 * seglen, 6 * LANES), jnp.float32),
            pltpu.VMEM((16, 6, 16, LANES), jnp.float32),
            pltpu.VMEM((16 * 8 * seglen, 8 * LANES), jnp.float32),
            pltpu.VMEM((8 * 8 * seglen, 6 * width), jnp.bfloat16),
            ring, ring, ring, ring, ring, ring,
            pltpu.VMEM((max(8 * (width // LANES), 6), SEGS * seglen, LANES), jnp.float32),
        ],
        compiler_params=pltpu.CompilerParams(
            dimension_semantics=("arbitrary",), vmem_limit_bytes=56 * 1024 * 1024
        ),
        name="adjoint_field",
    )(flags, left, right, tw, tc, vectors, edge, *pieces)


def local(loads, sleeper_pos, material, material_table):
    ka = lax.axis_size("ka")
    gy, gz = lax.axis_size("gy"), lax.axis_size("gz")
    count = KW // ka
    waves = lax.axis_index("ka") * count + jnp.arange(count, dtype=jnp.int32)
    sleepers = ka * loads.shape[0]
    own = 3 * loads.shape[0]
    ny, depth = material.shape
    height = ny + 2 * HB
    loads = loads.reshape(own, ny, depth)
    material = material.astype(jnp.float32)[None]

    def shift(array, axis, size, by):
        pairs = [(i, i + by) for i in range(size) if 0 <= i + by < size]
        return lax.ppermute(array, axis, pairs)

    turns = [[(i, (i + step) % ka) for i in range(ka)] for step in range(1, ka)]
    ends = jnp.concatenate([loads[:, :HB], loads[:, ny - HB :]], axis=1)
    got_ends = [lax.ppermute(ends, "ka", turn) for turn in turns]
    inner = loads[:, HB : ny - HB]
    got_inner = [lax.ppermute(inner, "ka", turn) for turn in turns]
    all_pos = [sleeper_pos] + [lax.ppermute(sleeper_pos, "ka", turn) for turn in turns]
    low = jnp.concatenate([loads[:, :HB], material[:, :HB]], axis=0)
    high = jnp.concatenate([loads[:, ny - HB :], material[:, ny - HB :]], axis=0)
    above, below = shift(high, "gy", gy, 1), shift(low, "gy", gy, -1)

    pieces = [loads, material, above, below]
    spots = [
        (0, 0, own, 0, (0, ny), HB),
        (1, 3 * sleepers, 1, 0, (0, ny), HB),
        (2, 0, own, 0, (0, HB), 0),
        (2, 3 * sleepers, 1, own, (0, HB), 0),
        (3, 0, own, 0, (0, HB), HB + ny),
        (3, 3 * sleepers, 1, own, (0, HB), HB + ny),
    ]
    for step, (outer, middle) in enumerate(zip(got_ends, got_inner)):
        first = own * (step + 1)
        number = len(pieces)
        pieces += [
            outer,
            middle,
            shift(outer[:, HB:], "gy", gy, 1),
            shift(outer[:, :HB], "gy", gy, -1),
        ]
        spots += [
            (number, first, own, 0, (0, HB), HB),
            (number, first, own, 0, (HB, HB), ny),
            (number + 1, first, own, 0, (0, ny - 2 * HB), 2 * HB),
            (number + 2, first, own, 0, (0, HB), 0),
            (number + 3, first, own, 0, (0, HB), HB + ny),
        ]

    tw, tc, vectors = tables(
        jnp.concatenate(all_pos), material_table, waves, lanes_for(sleepers)
    )
    y_at, z_at = lax.axis_index("gy"), lax.axis_index("gz")
    flags = jnp.stack([y_at == 0, y_at == gy - 1]).astype(jnp.int32)
    sub = jnp.arange(8)[:, None]
    lane = jnp.arange(LANES)[None, :]
    edge = jnp.stack(
        [
            jnp.where((z_at == 0) & (sub == 0) & (lane < HALF), 0.0, 1.0),
            jnp.where((z_at == gz - 1) & (sub == 7) & (lane >= HALF), 0.0, 1.0),
        ]
    ).astype(jnp.float32)
    tied = lax.optimization_barrier((pieces[-1], tw, tc, vectors, flags, edge))
    pieces[-1], tw, tc, vectors, flags, edge = tied

    columns = edges_of(spots, pieces, sleepers, height, depth)
    left = shift(columns[:, HB:], "gz", gz, 1)
    right = shift(columns[:, :HB], "gz", gz, -1)
    return solve_field(
        spots, pieces, flags, left, right, tw, tc, vectors, edge, sleepers, count
    )


def solution(mesh):
    return jax.shard_map(
        local,
        mesh=mesh,
        in_specs=(P("ka", None, "gy", "gz"), P("ka"), P("gy", "gz"), P()),
        out_specs=P("ka", None, None, "gy", "gz"),
        check_vma=False,
    )
```

```python
import functools
import math

import jax
import jax.numpy as jnp
from jax import lax
from jax.experimental import pallas as pl
from jax.experimental.pallas import tpu as pltpu
from jax.sharding import PartitionSpec as P

KW = 128
NMAT = 8
DEG = 4
LANES = 128
HALF = 64
SEGS = 16
HY = 7
HB = 8


def lanes_for(sleepers):
    return -(-(3 * sleepers + 3 * NMAT) // LANES) * LANES


def two_parts(values):
    high = values.astype(jnp.bfloat16)
    low = (values - high.astype(jnp.float32)).astype(jnp.bfloat16)
    return high, low


def dot(a, b):
    return lax.dot_general(a, b, (((1,), (0,)), ((), ())), preferred_element_type=jnp.float32)


def dot_t(a, b):
    return lax.dot_general(a, b, (((1,), (1,)), ((), ())), preferred_element_type=jnp.float32)


def table_kernel(sleepers, count, start, table, cells, positions, tw, tc, vectors):
    width = tc.shape[0] // 2
    lane = lax.broadcasted_iota(jnp.int32, (8, LANES), 1)
    wave = lane % HALF
    live = wave < count
    wave = wave + start[0]
    q = (2.0 * jnp.sin(wave.astype(jnp.float32) * (math.pi / KW))) ** 2
    lowest = highest = None
    for m in range(NMAT):
        s, xx, yy, zz, xy, xz, yz = (jnp.full((8, LANES), table[m, f]) for f in range(7))
        xy, xz, yz = jnp.abs(xy), jnp.abs(xz), jnp.abs(yz)
        sums = (xy + xz, xy + yz, xz + yz)
        low = s + q * functools.reduce(jnp.minimum, [d - r for d, r in zip((xx, yy, zz), sums)])
        high = s + q * functools.reduce(jnp.maximum, [d + r for d, r in zip((xx, yy, zz), sums)])
        lowest = low if m == 0 else jnp.minimum(lowest, low)
        highest = high if m == 0 else jnp.maximum(highest, high)
    highest = 8.0 + highest
    center = 0.5 * (highest + lowest)
    half_width = 0.5 * (highest - lowest)
    ratio2 = (center / half_width) ** 2
    top = 8.0 * ratio2 * (ratio2 - 1.0) + 1.0
    h2 = half_width * half_width
    h4 = h2 * h2
    scale = 8.0 / (top * h4)
    scale = jnp.where(live, scale * scale, 0.0)
    for n, vector in enumerate((-h2, (top + 1.0) * h4 * 0.125, lowest * highest, center)):
        vectors[n, :, :] = jnp.where(live, vector, 0.0)

    tc[...] = jnp.zeros(tc.shape, jnp.bfloat16)
    tw[...] = jnp.zeros(tw.shape, jnp.bfloat16)
    column = [jnp.broadcast_to(cells[:, f : f + 1], (8, LANES)) for f in range(8)]
    fields = [center - 4.0 - column[0] - q * column[c] for c in (1, 2, 3)]
    fields += [-q * column[c] for c in (4, 5, 6)] + [q * column[7]]
    rounded = lambda values: values.astype(jnp.bfloat16).astype(jnp.float32)
    for f, field in enumerate(fields):
        field = jnp.where(live, field, 0.0)
        first = rounded(field)
        second = rounded(field - first)
        third = field - first - second
        rows = jnp.concatenate([first, second, third, jnp.zeros_like(first)], axis=0)
        lanes = lax.broadcasted_iota(jnp.int32, rows.shape, 1)
        for half in range(2):
            kept = jnp.where(lanes // HALF == half, rows, 0.0).astype(jnp.bfloat16)
            at = half * width + 3 * sleepers
            tc[at : at + 32, f * LANES : (f + 1) * LANES] = kept

    turns = (positions[...] * wave[:1]) & (KW - 1)
    angles = turns.astype(jnp.float32) * (2.0 * math.pi / KW)
    lanes = lax.broadcasted_iota(jnp.int32, turns.shape, 1)
    for part, phase in enumerate((jnp.cos(angles), -jnp.sin(angles))):
        phase = phase * scale[:1]
        high = rounded(phase)
        for segment, values in enumerate((high, high, phase - high)):
            for half in range(2):
                kept = jnp.where(lanes // HALF == half, values, 0.0).astype(jnp.bfloat16)
                for c in range(3):
                    at = (2 * segment + half) * width + c * sleepers
                    to = (2 * c + part) * LANES
                    tw[at : at + sleepers, to : to + LANES] = kept


def tables(positions, material_table, start, count, width):
    sleepers = positions.shape[0]
    spots = jnp.broadcast_to(positions[:, None], (sleepers, LANES))
    return pl.pallas_call(
        functools.partial(table_kernel, sleepers, count),
        out_shape=(
            jax.ShapeDtypeStruct((6 * width, 6 * LANES), jnp.bfloat16),
            jax.ShapeDtypeStruct((2 * width, 8 * LANES), jnp.bfloat16),
            jax.ShapeDtypeStruct((4, 8, LANES), jnp.float32),
        ),
        in_specs=[pl.BlockSpec(memory_space=pltpu.SMEM)] * 2
        + [pl.BlockSpec(memory_space=pltpu.VMEM)] * 2,
        out_specs=(pl.BlockSpec(memory_space=pltpu.VMEM),) * 3,
        compiler_params=pltpu.CompilerParams(vmem_limit_bytes=32 * 1024 * 1024),
        name="tables",
    )(start.reshape(1), material_table, material_table, spots)


def row_values(planes, row, height, sleepers, width):
    depth = planes.shape[1]
    parts = [planes[pl.ds(c * height + row, sleepers, stride=3 * height), :] for c in range(3)]
    material = planes[pl.ds(3 * sleepers * height + row, 1), :]
    number = lax.broadcasted_iota(jnp.int32, (width - 3 * sleepers, depth), 0)
    kind = jnp.where(number < 3 * NMAT, number % NMAT, -1).astype(jnp.float32)
    parts.append((kind == material).astype(jnp.float32))
    return jnp.concatenate(parts, axis=0)


def gather(spots, pieces, planes, sems):
    copies = []
    for n, (piece, first, count, plane, row, target) in enumerate(spots):
        src = pieces[piece]
        copies.append(
            pltpu.make_async_copy(
                src.at[plane : plane + count, row[0] : row[0] + row[1], :],
                planes.at[first : first + count, target : target + row[1], :],
                sems.at[n],
            )
        )
    for copy in copies:
        copy.start()
    for copy in copies:
        copy.wait()


def edge_kernel(sleepers, spots, *refs):
    *pieces, out, planes, sems = refs
    gather(spots, pieces, planes, sems)
    height, depth = planes.shape[1:]
    width = out.shape[2]
    spot = lax.broadcasted_iota(jnp.int32, (2 * HB, depth), 0)
    at = lax.broadcasted_iota(jnp.int32, (2 * HB, depth), 1)
    pick = (at == jnp.where(spot < HB, spot, spot + (depth - 2 * HB))).astype(jnp.bfloat16)
    flat = planes.reshape(planes.shape[0] * height, depth)

    def some_rows(block, carry):
        for line in range(8):
            row = 8 * block + line
            high, low = two_parts(row_values(flat, row, height, sleepers, width))
            out[row, :, :] = dot_t(pick, high) + dot_t(pick, low)
        return carry

    lax.fori_loop(0, height // 8, some_rows, 0)


def edges_of(spots, pieces, sleepers, height, depth):
    return pl.pallas_call(
        functools.partial(edge_kernel, sleepers, spots),
        out_shape=jax.ShapeDtypeStruct((height, 2 * HB, lanes_for(sleepers)), jnp.float32),
        in_specs=[pl.BlockSpec(memory_space=pl.ANY)] * len(pieces),
        out_specs=pl.BlockSpec(memory_space=pltpu.VMEM),
        scratch_shapes=[
            pltpu.VMEM((3 * sleepers + 1, height, depth), jnp.float32),
            pltpu.SemaphoreType.DMA((len(spots),)),
        ],
        compiler_params=pltpu.CompilerParams(vmem_limit_bytes=32 * 1024 * 1024),
        name="edge_columns",
    )(*pieces)


def field_kernel(sleepers, count, seglen, spots, *refs):
    scratch = 19
    flags, left, right, tw, tc, vectors, edge, *pieces = refs[: len(refs) - scratch]
    (out, planes, sems, source, ghosts, coefs, made_source, made_coefs, lhs, lay,
     a1, a2, a3, wide, b1, b2, turn, pages, page_sems) = refs[len(refs) - scratch :]
    height, depth = planes.shape[1:]
    flat = planes.reshape(planes.shape[0] * height, depth)
    ny = height - 2 * HB
    width = left.shape[2]
    chunks = width // LANES
    cells = 8 * seglen
    page_rows = pages.reshape(2 * count * 48, depth)
    lane = lax.broadcasted_iota(jnp.int32, (8, LANES), 1)
    sub = lax.broadcasted_iota(jnp.int32, (8, LANES), 0)

    def at(zm):
        return pl.ds(8 * (zm + 1), 8)

    def around(first, last):
        before = pltpu.roll(last, 1, 0)
        after = pltpu.roll(first, 7, 0)
        return (
            jnp.where(sub == 0, pltpu.roll(before, HALF, 1), before),
            jnp.where(sub == 7, pltpu.roll(after, HALF, 1), after),
        )

    def line_at(row, zm):
        return pl.ds(pl.multiple_of((row & 15) * cells, 8) + 8 * zm, 8)

    def column(q):
        part, c = divmod(q, 3)
        return slice((2 * c + part) * LANES, (2 * c + part + 1) * LANES)

    def read_source(row, q, zm):
        if zm == -1:
            return ghosts[row & 15, q, :8, :]
        if zm == seglen:
            return ghosts[row & 15, q, 8:, :]
        return source[line_at(row, zm), column(q)]

    def reader(ring):
        def read(row, q, zm):
            outside = ((row < HY) & (flags[0] == 1)) | ((row >= HY + ny) & (flags[1] == 1))
            return ring[jnp.where(outside, 4, row & 3), q, at(zm), :]

        return read

    def produce(pair):
        def lay_out(k):
            srow = jnp.clip(2 * pair - 2 + k + (HB - HY), 0, height - 1)
            values = row_values(flat, srow, height, sleepers, width)
            for n in range(chunks):
                span = slice(n * LANES, (n + 1) * LANES)
                lay[k * chunks + n, HB : HB + depth, :] = jnp.transpose(values[span])
                lay[k * chunks + n, :HB, :] = left[srow, :, span]
                lay[k * chunks + n, HB + depth :, :] = right[srow, :, span]

        def split():
            halves = [[], []]
            for k in range(2):
                for half in range(2):
                    for zm in range(seglen):
                        spot = pl.ds(half * cells + zm, 8, stride=seglen)
                        pieces_at = [lay[k * chunks + n, spot, :] for n in range(chunks)]
                        halves[half].append(jnp.concatenate(pieces_at, axis=1))
            values = jnp.concatenate(
                [jnp.concatenate(half, axis=0) for half in halves], axis=1
            )
            high, low = two_parts(values)
            lhs[:, : 2 * width] = high
            lhs[:, 2 * width : 4 * width] = low
            lhs[:, 4 * width :] = high

        def spectrum(c):
            span = slice(2 * c * LANES, 2 * (c + 1) * LANES)
            made_source[:, span] = dot(lhs[...], tw[:, span])

        def fields(f):
            span = slice(f * LANES, (f + 2) * LANES)
            made_coefs[:, span] = dot(lhs[:, : 2 * width], tc[:, span])

        return [
            functools.partial(lay_out, 0),
            functools.partial(lay_out, 1),
            split,
            *[functools.partial(spectrum, c) for c in range(3)],
            *[functools.partial(fields, f) for f in range(0, 8, 2)],
        ]

    def commit(pair):
        for k in range(2):
            row = 2 * pair - 2 + k
            for zm in range(seglen):
                rows = slice(k * cells + 8 * zm, k * cells + 8 * zm + 8)
                for n in range(6):
                    span = slice(n * LANES, (n + 1) * LANES)
                    source[line_at(row, zm), span] = made_source[rows, span]
                for n in range(7):
                    span = slice(n * LANES, (n + 1) * LANES)
                    coefs[line_at(row, zm), span] = made_coefs[rows, span]
            for q in range(6):
                first = made_source[k * cells : k * cells + 8, column(q)]
                last = made_source[(k + 1) * cells - 8 : (k + 1) * cells, column(q)]
                ghosts[row & 15, q, :8, :], ghosts[row & 15, q, 8:, :] = around(first, last)

    def apply(src, row, emit, shift=None, extra=None):
        prev = [[src(row + k, q, -1) for q in range(6)] for k in range(2)]
        cur = [[src(row + k, q, 0) for q in range(6)] for k in range(2)]
        for zm in range(seglen):
            nxt = [[src(row + k, q, zm + 1) for q in range(6)] for k in range(2)]
            for k in range(2):
                f = [
                    coefs[line_at(row + k, zm), n * LANES : (n + 1) * LANES] for n in range(7)
                ]
                diagonal = f[:3]
                if shift is not None:
                    diagonal = [d + shift for d in diagonal]
                matrix = (
                    (diagonal[0], f[3], f[4]),
                    (f[3], diagonal[1], f[5]),
                    (f[4], f[5], diagonal[2]),
                )
                results = []
                for q in range(6):
                    part, c = divmod(q, 3)
                    outer = src(row + 3 * k - 1, q, zm)
                    near = (outer + cur[1 - k][q]) + (prev[k][q] + nxt[k][q])
                    mine = cur[k][3 * part : 3 * part + 3]
                    own = matrix[c][0] * mine[0] + matrix[c][1] * mine[1] + matrix[c][2] * mine[2]
                    damp = f[6] * cur[k][3 * (1 - part) + c]
                    total = near + own
                    total = total + damp if part == 0 else total - damp
                    if extra is not None:
                        other, weight = extra
                        total = total + weight * other(row + k, q, zm)
                    results.append(total)
                emit(k, zm, results)
            prev, cur = cur, nxt

    def stage(src, dst, row, extra=None, between=None):
        ends = {}

        def emit(k, zm, results):
            if zm == HB - 1:
                results = [value * edge[0] for value in results]
            if zm == (HB + depth) % seglen:
                results = [value * edge[1] for value in results]
            slot = (row + k) & 3
            for q in range(6):
                dst[slot, q, at(zm), :] = results[q]
            if zm in (0, seglen - 1):
                ends[k, zm] = results
            if zm == seglen - 1:
                for q in range(6):
                    dst[slot, q, at(-1), :], dst[slot, q, at(seglen), :] = around(
                        ends[k, 0][q], results[q]
                    )
            if between is not None and k == 1:
                between()

        apply(src, row, emit, extra=extra)

    def last_stage(row):
        def emit(k, zm, results):
            for c in range(3):
                real, imag = results[c], results[3 + c]
                first = jnp.where(lane < HALF, real, pltpu.roll(imag, HALF, 1))
                second = jnp.where(lane < HALF, pltpu.roll(real, HALF, 1), imag)
                turn[3 * k + c, pl.ds(zm, 8, stride=seglen), :] = first
                turn[3 * k + c, pl.ds(cells + zm, 8, stride=seglen), :] = second

        apply(reader(b2), row, emit, shift=vectors[3])

    stages = (
        lambda base, more: stage(read_source, a1, base - 1, None, more),
        lambda base, more: stage(reader(a1), a2, base - 2, (read_source, vectors[0]), more),
        lambda base, more: stage(reader(a2), a3, base - 3, None, more),
        lambda base, more: stage(reader(a3), wide, base - 4, (read_source, vectors[1]), more),
        lambda base, more: stage(reader(wide), b1, base - 5, None, more),
        lambda base, more: stage(reader(b1), b2, base - 6, (reader(wide), vectors[2]), more),
    )

    def finish(pair):
        done = pair - HB
        block = done >> 2
        start = pl.multiple_of((block & 1) * (count * 48), 8) + 2 * (done & 3)

        def page(k, c):
            turned = jnp.transpose(turn[3 * k + c, HB : HB + depth, :])
            for part in range(2):
                rows = pl.ds(start + (part * 3 + c) * 8 + k, count, stride=48)
                page_rows[rows, :] = turned[part * HALF : part * HALF + count]

        return [functools.partial(page, k, c) for k in range(2) for c in range(3)]

    def page_copy(block):
        return pltpu.make_async_copy(
            pages.at[block & 1],
            out.at[:, :, :, pl.ds(pl.multiple_of(8 * block, 8), 8), :],
            page_sems.at[block & 1],
        )

    def ramp(pair, carry):
        base = 2 * pair - 2
        commit(pair)
        for step in produce(pair + 1):
            step()
        for t, run in enumerate(stages):

            @pl.when(base >= 2 * t + 2)
            def _():
                run(base, None)

        @pl.when(base >= 14)
        def _():
            last_stage(base - 7)

        return carry

    def steady(pair, carry):
        base = 2 * pair - 2
        done = pair - 1 - HB

        @pl.when(((done & 3) == 0) & (done >= 8))
        def _():
            page_copy((done >> 2) - 2).wait()

        commit(pair)
        pending = []
        making, turning = produce(pair + 1), finish(pair - 1)
        while making or turning:
            if turning:
                pending.append(turning.pop(0))
            if making:
                pending.append(making.pop(0))
        slots = 6 * seglen
        count_of = len(pending)
        seen = [0]

        def between():
            seen[0] += 1
            while pending and (count_of - len(pending)) * slots < seen[0] * count_of:
                pending.pop(0)()

        for run in stages:
            run(base, between)
        while pending:
            pending.pop(0)()
        last_stage(base - 7)

        @pl.when((done & 3) == 3)
        def _():
            page_copy(done >> 2).start()

        return carry

    gather(spots, pieces, planes, sems)
    for ring in (a1, a2, a3, wide, b1, b2):
        for q in range(6):
            ring[4, q, :, :] = jnp.zeros(ring.shape[2:], jnp.float32)
    for step in produce(0):
        step()
    final = HB + ny // 2 - 1
    lax.fori_loop(0, HB + 1, ramp, 0)
    lax.fori_loop(HB + 1, final + 1, steady, 0)
    for step in finish(final):
        step()
    blocks = ny // 8
    page_copy(blocks - 1).start()
    for block in range(max(blocks - 2, 0), blocks):
        page_copy(block).wait()


def solve_field(spots, pieces, flags, left, right, tw, tc, vectors, edge, sleepers, count):
    height, _, width = left.shape
    depth = pieces[0].shape[2]
    ny = height - 2 * HB
    seglen = (depth + 2 * HB) // SEGS
    cells = 8 * seglen
    chunks = width // LANES
    ring = pltpu.VMEM((5, 6, 8 * (seglen + 2), LANES), jnp.float32)
    whole = pl.BlockSpec(memory_space=pltpu.VMEM)
    return pl.pallas_call(
        functools.partial(field_kernel, sleepers, count, seglen, spots),
        out_shape=jax.ShapeDtypeStruct((count, 2, 3, ny, depth), jnp.float32),
        in_specs=[pl.BlockSpec(memory_space=pltpu.SMEM)]
        + [whole] * 6
        + [pl.BlockSpec(memory_space=pl.ANY)] * len(pieces),
        out_specs=pl.BlockSpec(memory_space=pl.ANY),
        scratch_shapes=[
            pltpu.VMEM((3 * sleepers + 1, height, depth), jnp.float32),
            pltpu.SemaphoreType.DMA((len(spots),)),
            pltpu.VMEM((16 * cells, 6 * LANES), jnp.float32),
            pltpu.VMEM((16, 6, 16, LANES), jnp.float32),
            pltpu.VMEM((16 * cells, 7 * LANES), jnp.float32),
            pltpu.VMEM((2 * cells, 6 * LANES), jnp.float32),
            pltpu.VMEM((2 * cells, 8 * LANES), jnp.float32),
            pltpu.VMEM((2 * cells, 6 * width), jnp.bfloat16),
            pltpu.VMEM((2 * chunks, 2 * cells, LANES), jnp.float32),
            ring, ring, ring, ring, ring, ring,
            pltpu.VMEM((6, 2 * cells, LANES), jnp.float32),
            pltpu.VMEM((2, count, 2, 3, 8, depth), jnp.float32),
            pltpu.SemaphoreType.DMA((2,)),
        ],
        compiler_params=pltpu.CompilerParams(vmem_limit_bytes=40 * 1024 * 1024),
        name="adjoint_field",
    )(flags, left, right, tw, tc, vectors, edge, *pieces)


def local(loads, sleeper_pos, material, material_table):
    ka = lax.axis_size("ka")
    gy, gz = lax.axis_size("gy"), lax.axis_size("gz")
    count = KW // ka
    wave_start = lax.axis_index("ka") * count
    sleepers = ka * loads.shape[0]
    own = 3 * loads.shape[0]
    ny, depth = material.shape
    height = ny + 2 * HB
    loads = loads.reshape(own, ny, depth)
    material = material.astype(jnp.float32)[None]

    def shift(array, axis, size, by):
        pairs = [(i, i + by) for i in range(size) if 0 <= i + by < size]
        return lax.ppermute(array, axis, pairs)

    turns = [[(i, (i + step) % ka) for i in range(ka)] for step in range(1, ka)]
    ends = jnp.concatenate([loads[:, :HB], loads[:, ny - HB :]], axis=1)
    got_ends = [lax.ppermute(ends, "ka", turn) for turn in turns]
    inner = loads[:, HB : ny - HB]
    got_inner = [lax.ppermute(inner, "ka", turn) for turn in turns]
    all_pos = [sleeper_pos] + [lax.ppermute(sleeper_pos, "ka", turn) for turn in turns]
    tw, tc, vectors = tables(
        jnp.concatenate(all_pos), material_table, wave_start, count, lanes_for(sleepers)
    )
    tw, tc, vectors, tied = lax.optimization_barrier((tw, tc, vectors, loads))
    low = jnp.concatenate([tied[:, :HB], material[:, :HB]], axis=0)
    high = jnp.concatenate([tied[:, ny - HB :], material[:, ny - HB :]], axis=0)
    above, below = shift(high, "gy", gy, 1), shift(low, "gy", gy, -1)

    pieces = [loads, material, above, below]
    spots = [
        (0, 0, own, 0, (0, ny), HB),
        (1, 3 * sleepers, 1, 0, (0, ny), HB),
        (2, 0, own, 0, (0, HB), 0),
        (2, 3 * sleepers, 1, own, (0, HB), 0),
        (3, 0, own, 0, (0, HB), HB + ny),
        (3, 3 * sleepers, 1, own, (0, HB), HB + ny),
    ]
    for step, (outer, middle) in enumerate(zip(got_ends, got_inner)):
        first = own * (step + 1)
        number = len(pieces)
        pieces += [
            outer,
            middle,
            shift(outer[:, HB:], "gy", gy, 1),
            shift(outer[:, :HB], "gy", gy, -1),
        ]
        spots += [
            (number, first, own, 0, (0, HB), HB),
            (number, first, own, 0, (HB, HB), ny),
            (number + 1, first, own, 0, (0, ny - 2 * HB), 2 * HB),
            (number + 2, first, own, 0, (0, HB), 0),
            (number + 3, first, own, 0, (0, HB), HB + ny),
        ]

    y_at, z_at = lax.axis_index("gy"), lax.axis_index("gz")
    flags = jnp.stack([y_at == 0, y_at == gy - 1]).astype(jnp.int32)
    sub = jnp.arange(8)[:, None]
    lane = jnp.arange(LANES)[None, :]
    edge = jnp.stack(
        [
            jnp.where((z_at == 0) & (sub == 0) & (lane < HALF), 0.0, 1.0),
            jnp.where((z_at == gz - 1) & (sub == 7) & (lane >= HALF), 0.0, 1.0),
        ]
    ).astype(jnp.float32)
    pieces[-1], flags, edge = lax.optimization_barrier((pieces[-1], flags, edge))

    columns = edges_of(spots, pieces, sleepers, height, depth)
    left = shift(columns[:, HB:], "gz", gz, 1)
    right = shift(columns[:, :HB], "gz", gz, -1)
    return solve_field(
        spots, pieces, flags, left, right, tw, tc, vectors, edge, sleepers, count
    )


def solution(mesh):
    return jax.shard_map(
        local,
        mesh=mesh,
        in_specs=(P("ka", None, "gy", "gz"), P("ka"), P("gy", "gz"), P()),
        out_specs=P("ka", None, None, "gy", "gz"),
        check_vma=False,
    )
```

```python
import functools
import math

import jax
import jax.numpy as jnp
from jax import lax
from jax.experimental import pallas as pl
from jax.experimental.pallas import tpu as pltpu
from jax.sharding import PartitionSpec as P

KW = 128
NMAT = 8
DEG = 4
LANES = 128
HALF = 64
SEGS = 16
HY = 7
HB = 8


def lanes_for(sleepers):
    return -(-(3 * sleepers + 3 * NMAT) // LANES) * LANES


def two_parts(values):
    high = values.astype(jnp.bfloat16)
    low = (values - high.astype(jnp.float32)).astype(jnp.bfloat16)
    return high, low


def dot(a, b):
    return lax.dot_general(a, b, (((1,), (0,)), ((), ())), preferred_element_type=jnp.float32)


def dot_t(a, b):
    return lax.dot_general(a, b, (((1,), (1,)), ((), ())), preferred_element_type=jnp.float32)


def table_kernel(sleepers, count, start, table, cells, positions, tw, tc, vectors):
    width = tc.shape[0] // 2
    lane = lax.broadcasted_iota(jnp.int32, (8, LANES), 1)
    wave = lane % HALF
    live = wave < count
    wave = wave + start[0]
    q = (2.0 * jnp.sin(wave.astype(jnp.float32) * (math.pi / KW))) ** 2
    lowest = highest = None
    for m in range(NMAT):
        s, xx, yy, zz, xy, xz, yz = (jnp.full((8, LANES), table[m, f]) for f in range(7))
        xy, xz, yz = jnp.abs(xy), jnp.abs(xz), jnp.abs(yz)
        sums = (xy + xz, xy + yz, xz + yz)
        low = s + q * functools.reduce(jnp.minimum, [d - r for d, r in zip((xx, yy, zz), sums)])
        high = s + q * functools.reduce(jnp.maximum, [d + r for d, r in zip((xx, yy, zz), sums)])
        lowest = low if m == 0 else jnp.minimum(lowest, low)
        highest = high if m == 0 else jnp.maximum(highest, high)
    highest = 8.0 + highest
    center = 0.5 * (highest + lowest)
    half_width = 0.5 * (highest - lowest)
    ratio2 = (center / half_width) ** 2
    top = 8.0 * ratio2 * (ratio2 - 1.0) + 1.0
    h2 = half_width * half_width
    h4 = h2 * h2
    scale = 8.0 / (top * h4)
    scale = jnp.where(live, scale * scale, 0.0)
    for n, vector in enumerate((-h2, (top + 1.0) * h4 * 0.125, lowest * highest, center)):
        vectors[n, :, :] = jnp.where(live, vector, 0.0)

    tc[...] = jnp.zeros(tc.shape, jnp.bfloat16)
    tw[...] = jnp.zeros(tw.shape, jnp.bfloat16)
    column = [jnp.broadcast_to(cells[:, f : f + 1], (8, LANES)) for f in range(8)]
    fields = [center - 4.0 - column[0] - q * column[c] for c in (1, 2, 3)]
    fields += [-q * column[c] for c in (4, 5, 6)] + [q * column[7]]
    rounded = lambda values: values.astype(jnp.bfloat16).astype(jnp.float32)
    for f, field in enumerate(fields):
        field = jnp.where(live, field, 0.0)
        first = rounded(field)
        second = rounded(field - first)
        third = field - first - second
        rows = jnp.concatenate([first, second, third, jnp.zeros_like(first)], axis=0)
        lanes = lax.broadcasted_iota(jnp.int32, rows.shape, 1)
        for half in range(2):
            kept = jnp.where(lanes // HALF == half, rows, 0.0).astype(jnp.bfloat16)
            at = half * width + 3 * sleepers
            tc[at : at + 32, f * LANES : (f + 1) * LANES] = kept

    turns = (positions[...] * wave[:1]) & (KW - 1)
    angles = turns.astype(jnp.float32) * (2.0 * math.pi / KW)
    lanes = lax.broadcasted_iota(jnp.int32, turns.shape, 1)
    for part, phase in enumerate((jnp.cos(angles), -jnp.sin(angles))):
        phase = phase * scale[:1]
        high = rounded(phase)
        for segment, values in enumerate((high, high, phase - high)):
            for half in range(2):
                kept = jnp.where(lanes // HALF == half, values, 0.0).astype(jnp.bfloat16)
                for c in range(3):
                    at = (2 * segment + half) * width + c * sleepers
                    to = (2 * c + part) * LANES
                    tw[at : at + sleepers, to : to + LANES] = kept


def tables(positions, material_table, start, count, width):
    sleepers = positions.shape[0]
    spots = jnp.broadcast_to(positions[:, None], (sleepers, LANES))
    return pl.pallas_call(
        functools.partial(table_kernel, sleepers, count),
        out_shape=(
            jax.ShapeDtypeStruct((6 * width, 6 * LANES), jnp.bfloat16),
            jax.ShapeDtypeStruct((2 * width, 8 * LANES), jnp.bfloat16),
            jax.ShapeDtypeStruct((4, 8, LANES), jnp.float32),
        ),
        in_specs=[pl.BlockSpec(memory_space=pltpu.SMEM)] * 2
        + [pl.BlockSpec(memory_space=pltpu.VMEM)] * 2,
        out_specs=(pl.BlockSpec(memory_space=pltpu.VMEM),) * 3,
        compiler_params=pltpu.CompilerParams(vmem_limit_bytes=32 * 1024 * 1024),
        name="tables",
    )(start.reshape(1), material_table, material_table, spots)


def row_values(planes, row, height, sleepers, width):
    depth = planes.shape[1]
    parts = [planes[pl.ds(c * height + row, sleepers, stride=3 * height), :] for c in range(3)]
    material = planes[pl.ds(3 * sleepers * height + row, 1), :]
    number = lax.broadcasted_iota(jnp.int32, (width - 3 * sleepers, depth), 0)
    kind = jnp.where(number < 3 * NMAT, number % NMAT, -1).astype(jnp.float32)
    parts.append((kind == material).astype(jnp.float32))
    return jnp.concatenate(parts, axis=0)


def gather(spots, pieces, planes, sems):
    copies = []
    for n, (piece, first, count, plane, row, target) in enumerate(spots):
        src = pieces[piece]
        copies.append(
            pltpu.make_async_copy(
                src.at[plane : plane + count, row[0] : row[0] + row[1], :],
                planes.at[first : first + count, target : target + row[1], :],
                sems.at[n],
            )
        )
    for copy in copies:
        copy.start()
    for copy in copies:
        copy.wait()


def edge_kernel(sleepers, spots, *refs):
    *pieces, out, planes, sems = refs
    gather(spots, pieces, planes, sems)
    height, depth = planes.shape[1:]
    width = out.shape[2]
    spot = lax.broadcasted_iota(jnp.int32, (2 * HB, depth), 0)
    at = lax.broadcasted_iota(jnp.int32, (2 * HB, depth), 1)
    pick = (at == jnp.where(spot < HB, spot, spot + (depth - 2 * HB))).astype(jnp.bfloat16)
    flat = planes.reshape(planes.shape[0] * height, depth)

    def some_rows(block, carry):
        for line in range(8):
            row = 8 * block + line
            high, low = two_parts(row_values(flat, row, height, sleepers, width))
            out[row, :, :] = dot_t(pick, high) + dot_t(pick, low)
        return carry

    lax.fori_loop(0, height // 8, some_rows, 0)


def edges_of(spots, pieces, sleepers, height, depth):
    return pl.pallas_call(
        functools.partial(edge_kernel, sleepers, spots),
        out_shape=jax.ShapeDtypeStruct((height, 2 * HB, lanes_for(sleepers)), jnp.float32),
        in_specs=[pl.BlockSpec(memory_space=pl.ANY)] * len(pieces),
        out_specs=pl.BlockSpec(memory_space=pltpu.VMEM),
        scratch_shapes=[
            pltpu.VMEM((3 * sleepers + 1, height, depth), jnp.float32),
            pltpu.SemaphoreType.DMA((len(spots),)),
        ],
        compiler_params=pltpu.CompilerParams(vmem_limit_bytes=32 * 1024 * 1024),
        name="edge_columns",
    )(*pieces)


def field_kernel(sleepers, count, seglen, spots, scratch, *refs):
    pl.run_scoped(functools.partial(field_body, sleepers, count, seglen, spots, refs), *scratch)


def field_body(sleepers, count, seglen, spots, refs, *scratch):
    flags, left, right, tw, tc, vectors, edge, *pieces, out = refs
    (planes, sems, source, ghosts, coefs, made_source, made_coefs, lhs, lay,
     a1, a2, a3, wide, b1, b2, turn, pages, page_sems) = scratch
    height, depth = planes.shape[1:]
    flat = planes.reshape(planes.shape[0] * height, depth)
    ny = height - 2 * HB
    width = left.shape[2]
    chunks = width // LANES
    cells = 8 * seglen
    page_rows = pages.reshape(2 * count * 48, depth)
    lane = lax.broadcasted_iota(jnp.int32, (8, LANES), 1)
    sub = lax.broadcasted_iota(jnp.int32, (8, LANES), 0)

    def at(zm):
        return pl.ds(8 * (zm + 1), 8)

    def around(first, last):
        before = pltpu.roll(last, 1, 0)
        after = pltpu.roll(first, 7, 0)
        return (
            jnp.where(sub == 0, pltpu.roll(before, HALF, 1), before),
            jnp.where(sub == 7, pltpu.roll(after, HALF, 1), after),
        )

    def line_at(row, zm):
        return pl.ds(pl.multiple_of((row & 15) * cells, 8) + 8 * zm, 8)

    def column(q):
        part, c = divmod(q, 3)
        return slice((2 * c + part) * LANES, (2 * c + part + 1) * LANES)

    def read_source(row, q, zm):
        if zm == -1:
            return ghosts[row & 15, q, :8, :]
        if zm == seglen:
            return ghosts[row & 15, q, 8:, :]
        return source[line_at(row, zm), column(q)]

    def reader(ring):
        def read(row, q, zm):
            outside = ((row < HY) & (flags[0] == 1)) | ((row >= HY + ny) & (flags[1] == 1))
            return ring[jnp.where(outside, 4, row & 3), q, at(zm), :]

        return read

    def produce(pair):
        def lay_out(k):
            srow = jnp.clip(2 * pair - 2 + k + (HB - HY), 0, height - 1)
            values = row_values(flat, srow, height, sleepers, width)
            for n in range(chunks):
                span = slice(n * LANES, (n + 1) * LANES)
                lay[k * chunks + n, HB : HB + depth, :] = jnp.transpose(values[span])
                lay[k * chunks + n, :HB, :] = left[srow, :, span]
                lay[k * chunks + n, HB + depth :, :] = right[srow, :, span]

        def split():
            halves = [[], []]
            for k in range(2):
                for half in range(2):
                    for zm in range(seglen):
                        spot = pl.ds(half * cells + zm, 8, stride=seglen)
                        pieces_at = [lay[k * chunks + n, spot, :] for n in range(chunks)]
                        halves[half].append(jnp.concatenate(pieces_at, axis=1))
            values = jnp.concatenate(
                [jnp.concatenate(half, axis=0) for half in halves], axis=1
            )
            high, low = two_parts(values)
            lhs[:, : 2 * width] = high
            lhs[:, 2 * width : 4 * width] = low
            lhs[:, 4 * width :] = high

        def spectrum(c):
            span = slice(2 * c * LANES, 2 * (c + 1) * LANES)
            made_source[:, span] = dot(lhs[...], tw[:, span])

        def fields(f):
            span = slice(f * LANES, (f + 2) * LANES)
            made_coefs[:, span] = dot(lhs[:, : 2 * width], tc[:, span])

        return [
            functools.partial(lay_out, 0),
            functools.partial(lay_out, 1),
            split,
            *[functools.partial(spectrum, c) for c in range(3)],
            *[functools.partial(fields, f) for f in range(0, 8, 2)],
        ]

    def commit(pair):
        for k in range(2):
            row = 2 * pair - 2 + k
            for zm in range(seglen):
                rows = slice(k * cells + 8 * zm, k * cells + 8 * zm + 8)
                for n in range(6):
                    span = slice(n * LANES, (n + 1) * LANES)
                    source[line_at(row, zm), span] = made_source[rows, span]
                for n in range(7):
                    span = slice(n * LANES, (n + 1) * LANES)
                    coefs[line_at(row, zm), span] = made_coefs[rows, span]
            for q in range(6):
                first = made_source[k * cells : k * cells + 8, column(q)]
                last = made_source[(k + 1) * cells - 8 : (k + 1) * cells, column(q)]
                ghosts[row & 15, q, :8, :], ghosts[row & 15, q, 8:, :] = around(first, last)

    def apply(src, row, emit, shift=None, extra=None):
        prev = [[src(row + k, q, -1) for q in range(6)] for k in range(2)]
        cur = [[src(row + k, q, 0) for q in range(6)] for k in range(2)]
        held = None
        for zm in range(seglen):
            nxt = [None, None]
            for k in range(2):
                nxt[k] = [src(row + k, q, zm + 1) for q in range(6)]
                outer = [src(row + 3 * k - 1, q, zm) for q in range(6)]
                f = [
                    coefs[line_at(row + k, zm), n * LANES : (n + 1) * LANES] for n in range(7)
                ]
                if extra is not None:
                    added = [extra[0](row + k, q, zm) for q in range(6)]
                if held is not None:
                    emit(*held)
                diagonal = f[:3]
                if shift is not None:
                    diagonal = [d + shift for d in diagonal]
                matrix = (
                    (diagonal[0], f[3], f[4]),
                    (f[3], diagonal[1], f[5]),
                    (f[4], f[5], diagonal[2]),
                )
                results = []
                for q in range(6):
                    part, c = divmod(q, 3)
                    near = (outer[q] + cur[1 - k][q]) + (prev[k][q] + nxt[k][q])
                    mine = cur[k][3 * part : 3 * part + 3]
                    own = matrix[c][0] * mine[0] + matrix[c][1] * mine[1] + matrix[c][2] * mine[2]
                    damp = f[6] * cur[k][3 * (1 - part) + c]
                    total = near + own
                    total = total + damp if part == 0 else total - damp
                    if extra is not None:
                        total = total + extra[1] * added[q]
                    results.append(total)
                held = (k, zm, results)
            prev, cur = cur, nxt
        emit(*held)

    def stage(src, dst, row, extra=None, between=None):
        ends = {}

        def emit(k, zm, results):
            if zm == HB - 1:
                results = [value * edge[0] for value in results]
            if zm == (HB + depth) % seglen:
                results = [value * edge[1] for value in results]
            slot = (row + k) & 3
            for q in range(6):
                dst[slot, q, at(zm), :] = results[q]
            if zm in (0, seglen - 1):
                ends[k, zm] = results
            if zm == seglen - 1:
                for q in range(6):
                    dst[slot, q, at(-1), :], dst[slot, q, at(seglen), :] = around(
                        ends[k, 0][q], results[q]
                    )
            if between is not None and k == 1:
                between()

        apply(src, row, emit, extra=extra)

    def last_stage(row):
        def emit(k, zm, results):
            for c in range(3):
                real, imag = results[c], results[3 + c]
                first = jnp.where(lane < HALF, real, pltpu.roll(imag, HALF, 1))
                second = jnp.where(lane < HALF, pltpu.roll(real, HALF, 1), imag)
                turn[3 * k + c, pl.ds(zm, 8, stride=seglen), :] = first
                turn[3 * k + c, pl.ds(cells + zm, 8, stride=seglen), :] = second

        apply(reader(b2), row, emit, shift=vectors[3])

    stages = (
        lambda base, more: stage(read_source, a1, base - 1, None, more),
        lambda base, more: stage(reader(a1), a2, base - 2, (read_source, vectors[0]), more),
        lambda base, more: stage(reader(a2), a3, base - 3, None, more),
        lambda base, more: stage(reader(a3), wide, base - 4, (read_source, vectors[1]), more),
        lambda base, more: stage(reader(wide), b1, base - 5, None, more),
        lambda base, more: stage(reader(b1), b2, base - 6, (reader(wide), vectors[2]), more),
    )

    def finish(pair):
        done = pair - HB
        block = done >> 2
        start = pl.multiple_of((block & 1) * (count * 48), 8) + 2 * (done & 3)

        def page(k, c):
            turned = jnp.transpose(turn[3 * k + c, HB : HB + depth, :])
            for part in range(2):
                rows = pl.ds(start + (part * 3 + c) * 8 + k, count, stride=48)
                page_rows[rows, :] = turned[part * HALF : part * HALF + count]

        return [functools.partial(page, k, c) for k in range(2) for c in range(3)]

    def page_copy(block):
        return pltpu.make_async_copy(
            pages.at[block & 1],
            out.at[:, :, :, pl.ds(pl.multiple_of(8 * block, 8), 8), :],
            page_sems.at[block & 1],
        )

    def ramp(pair, carry):
        base = 2 * pair - 2
        commit(pair)
        for step in produce(pair + 1):
            step()
        for t, run in enumerate(stages):

            @pl.when(base >= 2 * t + 2)
            def _():
                run(base, None)

        @pl.when(base >= 14)
        def _():
            last_stage(base - 7)

        return carry

    def steady(pair, carry):
        base = 2 * pair - 2
        done = pair - 1 - HB

        @pl.when(((done & 3) == 0) & (done >= 8))
        def _():
            page_copy((done >> 2) - 2).wait()

        commit(pair)
        pending = []
        making, turning = produce(pair + 1), finish(pair - 1)
        while making or turning:
            if turning:
                pending.append(turning.pop(0))
            if making:
                pending.append(making.pop(0))
        slots = 6 * seglen
        count_of = len(pending)
        seen = [0]

        def between():
            seen[0] += 1
            while pending and (count_of - len(pending)) * slots < seen[0] * count_of:
                pending.pop(0)()

        for run in stages:
            run(base, between)
        while pending:
            pending.pop(0)()
        last_stage(base - 7)

        @pl.when((done & 3) == 3)
        def _():
            page_copy(done >> 2).start()

        return carry

    gather(spots, pieces, planes, sems)
    for ring in (a1, a2, a3, wide, b1, b2):
        for q in range(6):
            ring[4, q, :, :] = jnp.zeros(ring.shape[2:], jnp.float32)
    for step in produce(0):
        step()
    final = HB + ny // 2 - 1
    lax.fori_loop(0, HB + 1, ramp, 0)
    lax.fori_loop(HB + 1, final + 1, steady, 0)
    for step in finish(final):
        step()
    blocks = ny // 8
    page_copy(blocks - 1).start()
    for block in range(max(blocks - 2, 0), blocks):
        page_copy(block).wait()


def solve_field(spots, pieces, flags, left, right, tw, tc, vectors, edge, sleepers, count):
    height, _, width = left.shape
    depth = pieces[0].shape[2]
    ny = height - 2 * HB
    seglen = (depth + 2 * HB) // SEGS
    cells = 8 * seglen
    chunks = width // LANES
    ring = pltpu.VMEM((5, 6, 8 * (seglen + 2), LANES), jnp.float32)
    whole = pl.BlockSpec(memory_space=pltpu.VMEM)
    scratch = (
        pltpu.VMEM((3 * sleepers + 1, height, depth), jnp.float32),
        pltpu.SemaphoreType.DMA((len(spots),)),
        pltpu.VMEM((16 * cells, 6 * LANES), jnp.float32),
        pltpu.VMEM((16, 6, 16, LANES), jnp.float32),
        pltpu.VMEM((16 * cells, 7 * LANES), jnp.float32),
        pltpu.VMEM((2 * cells, 6 * LANES), jnp.float32),
        pltpu.VMEM((2 * cells, 8 * LANES), jnp.float32),
        pltpu.VMEM((2 * cells, 6 * width), jnp.bfloat16),
        pltpu.VMEM((2 * chunks, 2 * cells, LANES), jnp.float32),
        ring, ring, ring, ring, ring, ring,
        pltpu.VMEM((6, 2 * cells, LANES), jnp.float32),
        pltpu.VMEM((2, count, 2, 3, 8, depth), jnp.float32),
        pltpu.SemaphoreType.DMA((2,)),
    )
    return pl.pallas_call(
        functools.partial(field_kernel, sleepers, count, seglen, spots, scratch),
        out_shape=jax.ShapeDtypeStruct((count, 2, 3, ny, depth), jnp.float32),
        in_specs=[pl.BlockSpec(memory_space=pltpu.SMEM)]
        + [whole] * 6
        + [pl.BlockSpec(memory_space=pl.ANY)] * len(pieces),
        out_specs=pl.BlockSpec(memory_space=pl.ANY),
        compiler_params=pltpu.CompilerParams(vmem_limit_bytes=40 * 1024 * 1024),
        name="adjoint_field",
    )(flags, left, right, tw, tc, vectors, edge, *pieces)


def local(loads, sleeper_pos, material, material_table):
    ka = lax.axis_size("ka")
    gy, gz = lax.axis_size("gy"), lax.axis_size("gz")
    count = KW // ka
    wave_start = lax.axis_index("ka") * count
    sleepers = ka * loads.shape[0]
    own = 3 * loads.shape[0]
    ny, depth = material.shape
    height = ny + 2 * HB
    loads = loads.reshape(own, ny, depth)
    material = material.astype(jnp.float32)[None]

    def shift(array, axis, size, by):
        pairs = [(i, i + by) for i in range(size) if 0 <= i + by < size]
        return lax.ppermute(array, axis, pairs)

    turns = [[(i, (i + step) % ka) for i in range(ka)] for step in range(1, ka)]
    ends = jnp.concatenate([loads[:, :HB], loads[:, ny - HB :]], axis=1)
    got_ends = [lax.ppermute(ends, "ka", turn) for turn in turns]
    inner = loads[:, HB : ny - HB]
    got_inner = [lax.ppermute(inner, "ka", turn) for turn in turns]
    all_pos = [sleeper_pos] + [lax.ppermute(sleeper_pos, "ka", turn) for turn in turns]
    tw, tc, vectors = tables(
        jnp.concatenate(all_pos), material_table, wave_start, count, lanes_for(sleepers)
    )
    tw, tc, vectors, tied = lax.optimization_barrier((tw, tc, vectors, loads))
    low = jnp.concatenate([tied[:, :HB], material[:, :HB]], axis=0)
    high = jnp.concatenate([tied[:, ny - HB :], material[:, ny - HB :]], axis=0)
    above, below = shift(high, "gy", gy, 1), shift(low, "gy", gy, -1)

    pieces = [loads, material, above, below]
    spots = [
        (0, 0, own, 0, (0, ny), HB),
        (1, 3 * sleepers, 1, 0, (0, ny), HB),
        (2, 0, own, 0, (0, HB), 0),
        (2, 3 * sleepers, 1, own, (0, HB), 0),
        (3, 0, own, 0, (0, HB), HB + ny),
        (3, 3 * sleepers, 1, own, (0, HB), HB + ny),
    ]
    for step, (outer, middle) in enumerate(zip(got_ends, got_inner)):
        first = own * (step + 1)
        number = len(pieces)
        pieces += [
            outer,
            middle,
            shift(outer[:, HB:], "gy", gy, 1),
            shift(outer[:, :HB], "gy", gy, -1),
        ]
        spots += [
            (number, first, own, 0, (0, HB), HB),
            (number, first, own, 0, (HB, HB), ny),
            (number + 1, first, own, 0, (0, ny - 2 * HB), 2 * HB),
            (number + 2, first, own, 0, (0, HB), 0),
            (number + 3, first, own, 0, (0, HB), HB + ny),
        ]

    y_at, z_at = lax.axis_index("gy"), lax.axis_index("gz")
    flags = jnp.stack([y_at == 0, y_at == gy - 1]).astype(jnp.int32)
    sub = jnp.arange(8)[:, None]
    lane = jnp.arange(LANES)[None, :]
    edge = jnp.stack(
        [
            jnp.where((z_at == 0) & (sub == 0) & (lane < HALF), 0.0, 1.0),
            jnp.where((z_at == gz - 1) & (sub == 7) & (lane >= HALF), 0.0, 1.0),
        ]
    ).astype(jnp.float32)
    pieces[-1], flags, edge = lax.optimization_barrier((pieces[-1], flags, edge))

    columns = edges_of(spots, pieces, sleepers, height, depth)
    left = shift(columns[:, HB:], "gz", gz, 1)
    right = shift(columns[:, :HB], "gz", gz, -1)
    return solve_field(
        spots, pieces, flags, left, right, tw, tc, vectors, edge, sleepers, count
    )


def solution(mesh):
    return jax.shard_map(
        local,
        mesh=mesh,
        in_specs=(P("ka", None, "gy", "gz"), P("ka"), P("gy", "gz"), P()),
        out_specs=P("ka", None, None, "gy", "gz"),
        check_vma=False,
    )
```

```python
import functools
import math

import jax
import jax.numpy as jnp
from jax import lax
from jax.experimental import pallas as pl
from jax.experimental.pallas import tpu as pltpu
from jax.sharding import PartitionSpec as P

KW = 128
NMAT = 8
DEG = 4
LANES = 128
HALF = 64
SEGS = 16
HY = 7
HB = 8


def lanes_for(sleepers):
    return -(-(3 * sleepers + 3 * NMAT) // LANES) * LANES


def two_parts(values):
    high = values.astype(jnp.bfloat16)
    low = (values - high.astype(jnp.float32)).astype(jnp.bfloat16)
    return high, low


def dot(a, b):
    return lax.dot_general(a, b, (((1,), (0,)), ((), ())), preferred_element_type=jnp.float32)


def dot_t(a, b):
    return lax.dot_general(a, b, (((1,), (1,)), ((), ())), preferred_element_type=jnp.float32)


def table_kernel(sleepers, count, start, table, cells, positions, tw, tc, vectors):
    width = tc.shape[0] // 2
    lane = lax.broadcasted_iota(jnp.int32, (8, LANES), 1)
    wave = lane % HALF
    live = wave < count
    wave = wave + start[0]
    q = (2.0 * jnp.sin(wave.astype(jnp.float32) * (math.pi / KW))) ** 2
    lowest = highest = None
    for m in range(NMAT):
        s, xx, yy, zz, xy, xz, yz = (jnp.full((8, LANES), table[m, f]) for f in range(7))
        xy, xz, yz = jnp.abs(xy), jnp.abs(xz), jnp.abs(yz)
        sums = (xy + xz, xy + yz, xz + yz)
        low = s + q * functools.reduce(jnp.minimum, [d - r for d, r in zip((xx, yy, zz), sums)])
        high = s + q * functools.reduce(jnp.maximum, [d + r for d, r in zip((xx, yy, zz), sums)])
        lowest = low if m == 0 else jnp.minimum(lowest, low)
        highest = high if m == 0 else jnp.maximum(highest, high)
    highest = 8.0 + highest
    center = 0.5 * (highest + lowest)
    half_width = 0.5 * (highest - lowest)
    ratio2 = (center / half_width) ** 2
    top = 8.0 * ratio2 * (ratio2 - 1.0) + 1.0
    h2 = half_width * half_width
    h4 = h2 * h2
    scale = 8.0 / (top * h4)
    scale = jnp.where(live, scale * scale, 0.0)
    for n, vector in enumerate((-h2, (top + 1.0) * h4 * 0.125, lowest * highest, center)):
        vectors[n, :, :] = jnp.where(live, vector, 0.0)

    tc[...] = jnp.zeros(tc.shape, jnp.bfloat16)
    tw[...] = jnp.zeros(tw.shape, jnp.bfloat16)
    column = [jnp.broadcast_to(cells[:, f : f + 1], (8, LANES)) for f in range(8)]
    fields = [center - 4.0 - column[0] - q * column[c] for c in (1, 2, 3)]
    fields += [-q * column[c] for c in (4, 5, 6)] + [q * column[7]]
    rounded = lambda values: values.astype(jnp.bfloat16).astype(jnp.float32)
    for f, field in enumerate(fields):
        field = jnp.where(live, field, 0.0)
        first = rounded(field)
        second = rounded(field - first)
        third = field - first - second
        rows = jnp.concatenate([first, second, third, jnp.zeros_like(first)], axis=0)
        lanes = lax.broadcasted_iota(jnp.int32, rows.shape, 1)
        for half in range(2):
            kept = jnp.where(lanes // HALF == half, rows, 0.0).astype(jnp.bfloat16)
            at = half * width + 3 * sleepers
            tc[at : at + 32, f * LANES : (f + 1) * LANES] = kept

    turns = (positions[...] * wave[:1]) & (KW - 1)
    angles = turns.astype(jnp.float32) * (2.0 * math.pi / KW)
    lanes = lax.broadcasted_iota(jnp.int32, turns.shape, 1)
    for part, phase in enumerate((jnp.cos(angles), -jnp.sin(angles))):
        phase = phase * scale[:1]
        high = rounded(phase)
        for segment, values in enumerate((high, high, phase - high)):
            for half in range(2):
                kept = jnp.where(lanes // HALF == half, values, 0.0).astype(jnp.bfloat16)
                for c in range(3):
                    at = (2 * segment + half) * width + c * sleepers
                    to = (2 * c + part) * LANES
                    tw[at : at + sleepers, to : to + LANES] = kept


def tables(positions, material_table, start, count, width):
    sleepers = positions.shape[0]
    spots = jnp.broadcast_to(positions[:, None], (sleepers, LANES))
    return pl.pallas_call(
        functools.partial(table_kernel, sleepers, count),
        out_shape=(
            jax.ShapeDtypeStruct((6 * width, 6 * LANES), jnp.bfloat16),
            jax.ShapeDtypeStruct((2 * width, 8 * LANES), jnp.bfloat16),
            jax.ShapeDtypeStruct((4, 8, LANES), jnp.float32),
        ),
        in_specs=[pl.BlockSpec(memory_space=pltpu.SMEM)] * 2
        + [pl.BlockSpec(memory_space=pltpu.VMEM)] * 2,
        out_specs=(pl.BlockSpec(memory_space=pltpu.VMEM),) * 3,
        compiler_params=pltpu.CompilerParams(vmem_limit_bytes=32 * 1024 * 1024),
        name="tables",
    )(start.reshape(1), material_table, material_table, spots)


def row_values(planes, row, height, sleepers, width):
    depth = planes.shape[1]
    parts = [planes[pl.ds(c * height + row, sleepers, stride=3 * height), :] for c in range(3)]
    material = planes[pl.ds(3 * sleepers * height + row, 1), :]
    number = lax.broadcasted_iota(jnp.int32, (width - 3 * sleepers, depth), 0)
    kind = jnp.where(number < 3 * NMAT, number % NMAT, -1).astype(jnp.float32)
    parts.append((kind == material).astype(jnp.float32))
    return jnp.concatenate(parts, axis=0)


def gather(spots, pieces, planes, sems):
    copies = []
    for n, (piece, first, count, plane, row, target) in enumerate(spots):
        src = pieces[piece]
        copies.append(
            pltpu.make_async_copy(
                src.at[plane : plane + count, row[0] : row[0] + row[1], :],
                planes.at[first : first + count, target : target + row[1], :],
                sems.at[n],
            )
        )
    for copy in copies:
        copy.start()
    for copy in copies:
        copy.wait()


def edge_kernel(sleepers, spots, *refs):
    *pieces, out, planes, sems = refs
    gather(spots, pieces, planes, sems)
    height, depth = planes.shape[1:]
    width = out.shape[2]
    spot = lax.broadcasted_iota(jnp.int32, (2 * HB, depth), 0)
    at = lax.broadcasted_iota(jnp.int32, (2 * HB, depth), 1)
    pick = (at == jnp.where(spot < HB, spot, spot + (depth - 2 * HB))).astype(jnp.bfloat16)
    flat = planes.reshape(planes.shape[0] * height, depth)

    def some_rows(block, carry):
        for line in range(8):
            row = 8 * block + line
            high, low = two_parts(row_values(flat, row, height, sleepers, width))
            out[row, :, :] = dot_t(pick, high) + dot_t(pick, low)
        return carry

    lax.fori_loop(0, height // 8, some_rows, 0)


def edges_of(spots, pieces, sleepers, height, depth):
    return pl.pallas_call(
        functools.partial(edge_kernel, sleepers, spots),
        out_shape=jax.ShapeDtypeStruct((height, 2 * HB, lanes_for(sleepers)), jnp.float32),
        in_specs=[pl.BlockSpec(memory_space=pltpu.HBM)]
        + [pl.BlockSpec(memory_space=pl.ANY)] * (len(pieces) - 1),
        out_specs=pl.BlockSpec(memory_space=pltpu.VMEM),
        scratch_shapes=[
            pltpu.VMEM((3 * sleepers + 1, height, depth), jnp.float32),
            pltpu.SemaphoreType.DMA((len(spots),)),
        ],
        compiler_params=pltpu.CompilerParams(vmem_limit_bytes=32 * 1024 * 1024),
        name="edge_columns",
    )(*pieces)


def field_kernel(sleepers, count, seglen, spots, scratch, *refs):
    pl.run_scoped(functools.partial(field_body, sleepers, count, seglen, spots, refs), *scratch)


def field_body(sleepers, count, seglen, spots, refs, *scratch):
    flags, left, right, tw, tc, vectors, edge, *pieces, out = refs
    (planes, sems, source, ghosts, coefs, made_source, made_coefs, lhs, lay,
     a1, a2, a3, wide, b1, b2, turn, pages, page_sems) = scratch
    height, depth = planes.shape[1:]
    flat = planes.reshape(planes.shape[0] * height, depth)
    ny = height - 2 * HB
    width = left.shape[2]
    chunks = width // LANES
    cells = 8 * seglen
    page_rows = pages.reshape(2 * count * 48, depth)
    lane = lax.broadcasted_iota(jnp.int32, (8, LANES), 1)
    sub = lax.broadcasted_iota(jnp.int32, (8, LANES), 0)

    def at(zm):
        return pl.ds(8 * (zm + 1), 8)

    def around(first, last):
        before = pltpu.roll(last, 1, 0)
        after = pltpu.roll(first, 7, 0)
        return (
            jnp.where(sub == 0, pltpu.roll(before, HALF, 1), before),
            jnp.where(sub == 7, pltpu.roll(after, HALF, 1), after),
        )

    def line_at(row, zm):
        return pl.ds(pl.multiple_of((row & 15) * cells, 8) + 8 * zm, 8)

    def column(q):
        part, c = divmod(q, 3)
        return slice((2 * c + part) * LANES, (2 * c + part + 1) * LANES)

    def read_source(row, q, zm):
        if zm == -1:
            return ghosts[row & 15, q, :8, :]
        if zm == seglen:
            return ghosts[row & 15, q, 8:, :]
        return source[line_at(row, zm), column(q)]

    def reader(ring):
        def read(row, q, zm):
            outside = ((row < HY) & (flags[0] == 1)) | ((row >= HY + ny) & (flags[1] == 1))
            return ring[jnp.where(outside, 4, row & 3), q, at(zm), :]

        return read

    def produce(pair):
        def lay_out(k):
            srow = jnp.clip(2 * pair - 2 + k + (HB - HY), 0, height - 1)
            values = row_values(flat, srow, height, sleepers, width)
            for n in range(chunks):
                span = slice(n * LANES, (n + 1) * LANES)
                lay[k * chunks + n, HB : HB + depth, :] = jnp.transpose(values[span])
                lay[k * chunks + n, :HB, :] = left[srow, :, span]
                lay[k * chunks + n, HB + depth :, :] = right[srow, :, span]

        def split():
            halves = [[], []]
            for k in range(2):
                for half in range(2):
                    for zm in range(seglen):
                        spot = pl.ds(half * cells + zm, 8, stride=seglen)
                        pieces_at = [lay[k * chunks + n, spot, :] for n in range(chunks)]
                        halves[half].append(jnp.concatenate(pieces_at, axis=1))
            values = jnp.concatenate(
                [jnp.concatenate(half, axis=0) for half in halves], axis=1
            )
            high, low = two_parts(values)
            lhs[:, : 2 * width] = high
            lhs[:, 2 * width : 4 * width] = low
            lhs[:, 4 * width :] = high

        def spectrum(c):
            span = slice(2 * c * LANES, 2 * (c + 1) * LANES)
            made_source[:, span] = dot(lhs[...], tw[:, span])

        def fields(f):
            span = slice(f * LANES, (f + 2) * LANES)
            made_coefs[:, span] = dot(lhs[:, : 2 * width], tc[:, span])

        return [
            functools.partial(lay_out, 0),
            functools.partial(lay_out, 1),
            split,
            *[functools.partial(spectrum, c) for c in range(3)],
            *[functools.partial(fields, f) for f in range(0, 8, 2)],
        ]

    def commit(pair):
        for k in range(2):
            row = 2 * pair - 2 + k
            for zm in range(seglen):
                rows = slice(k * cells + 8 * zm, k * cells + 8 * zm + 8)
                for n in range(6):
                    span = slice(n * LANES, (n + 1) * LANES)
                    source[line_at(row, zm), span] = made_source[rows, span]
                for n in range(7):
                    span = slice(n * LANES, (n + 1) * LANES)
                    coefs[line_at(row, zm), span] = made_coefs[rows, span]
            for q in range(6):
                first = made_source[k * cells : k * cells + 8, column(q)]
                last = made_source[(k + 1) * cells - 8 : (k + 1) * cells, column(q)]
                ghosts[row & 15, q, :8, :], ghosts[row & 15, q, 8:, :] = around(first, last)

    def apply(src, row, emit, shift=None, extra=None):
        for k in range(2):
            prev = [src(row + k, q, -1) for q in range(6)]
            cur = [src(row + k, q, 0) for q in range(6)]
            for zm in range(seglen):
                nxt = [src(row + k, q, zm + 1) for q in range(6)]
                f = [
                    coefs[line_at(row + k, zm), n * LANES : (n + 1) * LANES] for n in range(7)
                ]
                diagonal = f[:3]
                if shift is not None:
                    diagonal = [d + shift for d in diagonal]
                matrix = (
                    (diagonal[0], f[3], f[4]),
                    (f[3], diagonal[1], f[5]),
                    (f[4], f[5], diagonal[2]),
                )
                results = []
                for q in range(6):
                    part, c = divmod(q, 3)
                    near = src(row + k - 1, q, zm) + src(row + k + 1, q, zm)
                    near = near + (prev[q] + nxt[q])
                    mine = cur[3 * part : 3 * part + 3]
                    own = matrix[c][0] * mine[0] + matrix[c][1] * mine[1] + matrix[c][2] * mine[2]
                    damp = f[6] * cur[3 * (1 - part) + c]
                    total = near + own
                    total = total + damp if part == 0 else total - damp
                    if extra is not None:
                        total = total + extra[1] * extra[0](row + k, q, zm)
                    results.append(total)
                emit(k, zm, results)
                prev, cur = cur, nxt

    def stage(src, dst, row, extra=None, between=None):
        ends = {}

        def emit(k, zm, results):
            if zm == HB - 1:
                results = [value * edge[0] for value in results]
            if zm == (HB + depth) % seglen:
                results = [value * edge[1] for value in results]
            slot = (row + k) & 3
            for q in range(6):
                dst[slot, q, at(zm), :] = results[q]
            if zm in (0, seglen - 1):
                ends[k, zm] = results
            if zm == seglen - 1:
                for q in range(6):
                    dst[slot, q, at(-1), :], dst[slot, q, at(seglen), :] = around(
                        ends[k, 0][q], results[q]
                    )
            if between is not None:
                between()

        apply(src, row, emit, extra=extra)

    def last_stage(row):
        def emit(k, zm, results):
            for c in range(3):
                real, imag = results[c], results[3 + c]
                first = jnp.where(lane < HALF, real, pltpu.roll(imag, HALF, 1))
                second = jnp.where(lane < HALF, pltpu.roll(real, HALF, 1), imag)
                turn[3 * k + c, pl.ds(zm, 8, stride=seglen), :] = first
                turn[3 * k + c, pl.ds(cells + zm, 8, stride=seglen), :] = second

        apply(reader(b2), row, emit, shift=vectors[3])

    stages = (
        lambda base, more: stage(read_source, a1, base - 1, None, more),
        lambda base, more: stage(reader(a1), a2, base - 2, (read_source, vectors[0]), more),
        lambda base, more: stage(reader(a2), a3, base - 3, None, more),
        lambda base, more: stage(reader(a3), wide, base - 4, (read_source, vectors[1]), more),
        lambda base, more: stage(reader(wide), b1, base - 5, None, more),
        lambda base, more: stage(reader(b1), b2, base - 6, (reader(wide), vectors[2]), more),
    )

    def finish(pair):
        done = pair - HB
        block = done >> 2
        start = pl.multiple_of((block & 1) * (count * 48), 8) + 2 * (done & 3)

        def page(k, c):
            turned = jnp.transpose(turn[3 * k + c, HB : HB + depth, :])
            for part in range(2):
                rows = pl.ds(start + (part * 3 + c) * 8 + k, count, stride=48)
                page_rows[rows, :] = turned[part * HALF : part * HALF + count]

        return [functools.partial(page, k, c) for k in range(2) for c in range(3)]

    def page_copy(block):
        return pltpu.make_async_copy(
            pages.at[block & 1],
            out.at[:, :, :, pl.ds(pl.multiple_of(8 * block, 8), 8), :],
            page_sems.at[block & 1],
        )

    def ramp(pair, carry):
        base = 2 * pair - 2
        commit(pair)
        for step in produce(pair + 1):
            step()
        for t, run in enumerate(stages):

            @pl.when(base >= 2 * t + 2)
            def _():
                run(base, None)

        @pl.when(base >= 14)
        def _():
            last_stage(base - 7)

        return carry

    def steady(pair, carry):
        base = 2 * pair - 2
        done = pair - 1 - HB

        @pl.when(((done & 3) == 0) & (done >= 8))
        def _():
            page_copy((done >> 2) - 2).wait()

        commit(pair)
        pending = []
        making, turning = produce(pair + 1), finish(pair - 1)
        while making or turning:
            if turning:
                pending.append(turning.pop(0))
            if making:
                pending.append(making.pop(0))
        slots = 12 * seglen
        count_of = len(pending)
        seen = [0]

        def between():
            seen[0] += 1
            while pending and (count_of - len(pending)) * slots < seen[0] * count_of:
                pending.pop(0)()

        for run in stages:
            run(base, between)
        while pending:
            pending.pop(0)()
        last_stage(base - 7)

        @pl.when((done & 3) == 3)
        def _():
            page_copy(done >> 2).start()

        return carry

    gather(spots, pieces, planes, sems)
    for ring in (a1, a2, a3, wide, b1, b2):
        for q in range(6):
            ring[4, q, :, :] = jnp.zeros(ring.shape[2:], jnp.float32)
    for step in produce(0):
        step()
    final = HB + ny // 2 - 1
    lax.fori_loop(0, HB + 1, ramp, 0)
    lax.fori_loop(HB + 1, final + 1, steady, 0)
    for step in finish(final):
        step()
    blocks = ny // 8
    page_copy(blocks - 1).start()
    for block in range(max(blocks - 2, 0), blocks):
        page_copy(block).wait()


def solve_field(spots, pieces, flags, left, right, tw, tc, vectors, edge, sleepers, count):
    height, _, width = left.shape
    depth = pieces[0].shape[2]
    ny = height - 2 * HB
    seglen = (depth + 2 * HB) // SEGS
    cells = 8 * seglen
    chunks = width // LANES
    ring = pltpu.VMEM((5, 6, 8 * (seglen + 2), LANES), jnp.float32)
    whole = pl.BlockSpec(memory_space=pltpu.VMEM)
    scratch = (
        pltpu.VMEM((3 * sleepers + 1, height, depth), jnp.float32),
        pltpu.SemaphoreType.DMA((len(spots),)),
        pltpu.VMEM((16 * cells, 6 * LANES), jnp.float32),
        pltpu.VMEM((16, 6, 16, LANES), jnp.float32),
        pltpu.VMEM((16 * cells, 7 * LANES), jnp.float32),
        pltpu.VMEM((2 * cells, 6 * LANES), jnp.float32),
        pltpu.VMEM((2 * cells, 8 * LANES), jnp.float32),
        pltpu.VMEM((2 * cells, 6 * width), jnp.bfloat16),
        pltpu.VMEM((2 * chunks, 2 * cells, LANES), jnp.float32),
        ring, ring, ring, ring, ring, ring,
        pltpu.VMEM((6, 2 * cells, LANES), jnp.float32),
        pltpu.VMEM((2, count, 2, 3, 8, depth), jnp.float32),
        pltpu.SemaphoreType.DMA((2,)),
    )
    return pl.pallas_call(
        functools.partial(field_kernel, sleepers, count, seglen, spots, scratch),
        out_shape=jax.ShapeDtypeStruct((count, 2, 3, ny, depth), jnp.float32),
        in_specs=[pl.BlockSpec(memory_space=pltpu.SMEM)]
        + [whole] * 6
        + [pl.BlockSpec(memory_space=pltpu.HBM)]
        + [pl.BlockSpec(memory_space=pl.ANY)] * (len(pieces) - 1),
        out_specs=pl.BlockSpec(memory_space=pl.ANY),
        compiler_params=pltpu.CompilerParams(vmem_limit_bytes=40 * 1024 * 1024),
        name="adjoint_field",
    )(flags, left, right, tw, tc, vectors, edge, *pieces)


def local(loads, sleeper_pos, material, material_table):
    ka = lax.axis_size("ka")
    gy, gz = lax.axis_size("gy"), lax.axis_size("gz")
    count = KW // ka
    wave_start = lax.axis_index("ka") * count
    sleepers = ka * loads.shape[0]
    own = 3 * loads.shape[0]
    ny, depth = material.shape
    height = ny + 2 * HB
    loads = loads.reshape(own, ny, depth)
    material = material.astype(jnp.float32)[None]

    def shift(array, axis, size, by):
        pairs = [(i, i + by) for i in range(size) if 0 <= i + by < size]
        return lax.ppermute(array, axis, pairs)

    turns = [[(i, (i + step) % ka) for i in range(ka)] for step in range(1, ka)]
    ends = jnp.concatenate([loads[:, :HB], loads[:, ny - HB :]], axis=1)
    got_ends = [lax.ppermute(ends, "ka", turn) for turn in turns]
    inner = loads[:, HB : ny - HB]
    got_inner = [lax.ppermute(inner, "ka", turn) for turn in turns]
    all_pos = [sleeper_pos] + [lax.ppermute(sleeper_pos, "ka", turn) for turn in turns]
    tw, tc, vectors = tables(
        jnp.concatenate(all_pos), material_table, wave_start, count, lanes_for(sleepers)
    )
    tw, tc, vectors, tied = lax.optimization_barrier((tw, tc, vectors, loads))
    low = jnp.concatenate([tied[:, :HB], material[:, :HB]], axis=0)
    high = jnp.concatenate([tied[:, ny - HB :], material[:, ny - HB :]], axis=0)
    above, below = shift(high, "gy", gy, 1), shift(low, "gy", gy, -1)

    pieces = [loads, material, above, below]
    spots = [
        (0, 0, own, 0, (0, ny), HB),
        (1, 3 * sleepers, 1, 0, (0, ny), HB),
        (2, 0, own, 0, (0, HB), 0),
        (2, 3 * sleepers, 1, own, (0, HB), 0),
        (3, 0, own, 0, (0, HB), HB + ny),
        (3, 3 * sleepers, 1, own, (0, HB), HB + ny),
    ]
    for step, (outer, middle) in enumerate(zip(got_ends, got_inner)):
        first = own * (step + 1)
        number = len(pieces)
        pieces += [
            outer,
            middle,
            shift(outer[:, HB:], "gy", gy, 1),
            shift(outer[:, :HB], "gy", gy, -1),
        ]
        spots += [
            (number, first, own, 0, (0, HB), HB),
            (number, first, own, 0, (HB, HB), ny),
            (number + 1, first, own, 0, (0, ny - 2 * HB), 2 * HB),
            (number + 2, first, own, 0, (0, HB), 0),
            (number + 3, first, own, 0, (0, HB), HB + ny),
        ]

    y_at, z_at = lax.axis_index("gy"), lax.axis_index("gz")
    flags = jnp.stack([y_at == 0, y_at == gy - 1]).astype(jnp.int32)
    sub = jnp.arange(8)[:, None]
    lane = jnp.arange(LANES)[None, :]
    edge = jnp.stack(
        [
            jnp.where((z_at == 0) & (sub == 0) & (lane < HALF), 0.0, 1.0),
            jnp.where((z_at == gz - 1) & (sub == 7) & (lane >= HALF), 0.0, 1.0),
        ]
    ).astype(jnp.float32)
    pieces[-1], flags, edge = lax.optimization_barrier((pieces[-1], flags, edge))

    columns = edges_of(spots, pieces, sleepers, height, depth)
    left = shift(columns[:, HB:], "gz", gz, 1)
    right = shift(columns[:, :HB], "gz", gz, -1)
    return solve_field(
        spots, pieces, flags, left, right, tw, tc, vectors, edge, sleepers, count
    )


def solution(mesh):
    return jax.shard_map(
        local,
        mesh=mesh,
        in_specs=(P("ka", None, "gy", "gz"), P("ka"), P("gy", "gz"), P()),
        out_specs=P("ka", None, None, "gy", "gz"),
        check_vma=False,
    )
```

```python
import functools
import math

import jax
import jax.numpy as jnp
from jax import lax
from jax.experimental import pallas as pl
from jax.experimental.pallas import tpu as pltpu
from jax.sharding import PartitionSpec as P

KW = 128
NMAT = 8
DEG = 4
LANES = 128
HALF = 64
SEGS = 16
HY = 7
HB = 8
RING = 12


def lanes_for(sleepers):
    return -(-(3 * sleepers + 3 * NMAT) // LANES) * LANES


def two_parts(values):
    high = values.astype(jnp.bfloat16)
    low = (values - high.astype(jnp.float32)).astype(jnp.bfloat16)
    return high, low


def dot(a, b):
    return lax.dot_general(a, b, (((1,), (0,)), ((), ())), preferred_element_type=jnp.float32)


def dot_t(a, b):
    return lax.dot_general(a, b, (((1,), (1,)), ((), ())), preferred_element_type=jnp.float32)


def table_kernel(sleepers, count, start, table, cells, positions, tw, tc, vectors):
    width = tc.shape[0] // 2
    lane = lax.broadcasted_iota(jnp.int32, (8, LANES), 1)
    wave = lane % HALF
    live = wave < count
    wave = wave + start[0]
    q = (2.0 * jnp.sin(wave.astype(jnp.float32) * (math.pi / KW))) ** 2
    lowest = highest = None
    for m in range(NMAT):
        s, xx, yy, zz, xy, xz, yz = (jnp.full((8, LANES), table[m, f]) for f in range(7))
        xy, xz, yz = jnp.abs(xy), jnp.abs(xz), jnp.abs(yz)
        sums = (xy + xz, xy + yz, xz + yz)
        low = s + q * functools.reduce(jnp.minimum, [d - r for d, r in zip((xx, yy, zz), sums)])
        high = s + q * functools.reduce(jnp.maximum, [d + r for d, r in zip((xx, yy, zz), sums)])
        lowest = low if m == 0 else jnp.minimum(lowest, low)
        highest = high if m == 0 else jnp.maximum(highest, high)
    highest = 8.0 + highest
    center = 0.5 * (highest + lowest)
    half_width = 0.5 * (highest - lowest)
    ratio2 = (center / half_width) ** 2
    top = 8.0 * ratio2 * (ratio2 - 1.0) + 1.0
    h2 = half_width * half_width
    h4 = h2 * h2
    scale = 8.0 / (top * h4)
    scale = jnp.where(live, scale * scale, 0.0)
    for n, vector in enumerate((-h2, (top + 1.0) * h4 * 0.125, lowest * highest, center)):
        vectors[n, :, :] = jnp.where(live, vector, 0.0)

    tc[...] = jnp.zeros(tc.shape, jnp.bfloat16)
    tw[...] = jnp.zeros(tw.shape, jnp.bfloat16)
    column = [jnp.broadcast_to(cells[:, f : f + 1], (8, LANES)) for f in range(8)]
    fields = [center - 4.0 - column[0] - q * column[c] for c in (1, 2, 3)]
    fields += [-q * column[c] for c in (4, 5, 6)] + [q * column[7]]
    rounded = lambda values: values.astype(jnp.bfloat16).astype(jnp.float32)
    for f, field in enumerate(fields):
        field = jnp.where(live, field, 0.0)
        first = rounded(field)
        second = rounded(field - first)
        third = field - first - second
        rows = jnp.concatenate([first, second, third, jnp.zeros_like(first)], axis=0)
        lanes = lax.broadcasted_iota(jnp.int32, rows.shape, 1)
        for half in range(2):
            kept = jnp.where(lanes // HALF == half, rows, 0.0).astype(jnp.bfloat16)
            at = half * width + 3 * sleepers
            tc[at : at + 32, f * LANES : (f + 1) * LANES] = kept

    turns = (positions[...] * wave[:1]) & (KW - 1)
    angles = turns.astype(jnp.float32) * (2.0 * math.pi / KW)
    lanes = lax.broadcasted_iota(jnp.int32, turns.shape, 1)
    for part, phase in enumerate((jnp.cos(angles), -jnp.sin(angles))):
        phase = phase * scale[:1]
        high = rounded(phase)
        for segment, values in enumerate((high, high, phase - high)):
            for half in range(2):
                kept = jnp.where(lanes // HALF == half, values, 0.0).astype(jnp.bfloat16)
                for c in range(3):
                    at = (2 * segment + half) * width + c * sleepers
                    to = (2 * c + part) * LANES
                    tw[at : at + sleepers, to : to + LANES] = kept


def tables(positions, material_table, start, count, width):
    sleepers = positions.shape[0]
    spots = jnp.broadcast_to(positions[:, None], (sleepers, LANES))
    return pl.pallas_call(
        functools.partial(table_kernel, sleepers, count),
        out_shape=(
            jax.ShapeDtypeStruct((6 * width, 6 * LANES), jnp.bfloat16),
            jax.ShapeDtypeStruct((2 * width, 8 * LANES), jnp.bfloat16),
            jax.ShapeDtypeStruct((4, 8, LANES), jnp.float32),
        ),
        in_specs=[pl.BlockSpec(memory_space=pltpu.SMEM)] * 2
        + [pl.BlockSpec(memory_space=pltpu.VMEM)] * 2,
        out_specs=(pl.BlockSpec(memory_space=pltpu.VMEM),) * 3,
        compiler_params=pltpu.CompilerParams(vmem_limit_bytes=32 * 1024 * 1024),
        name="tables",
    )(start.reshape(1), material_table, material_table, spots)


def row_values(planes, row, height, sleepers, width):
    depth = planes.shape[1]
    parts = [planes[pl.ds(c * height + row, sleepers, stride=3 * height), :] for c in range(3)]
    material = planes[pl.ds(3 * sleepers * height + row, 1), :]
    number = lax.broadcasted_iota(jnp.int32, (width - 3 * sleepers, depth), 0)
    kind = jnp.where(number < 3 * NMAT, number % NMAT, -1).astype(jnp.float32)
    parts.append((kind == material).astype(jnp.float32))
    return jnp.concatenate(parts, axis=0)


def gather(spots, pieces, planes, sems):
    copies = []
    for n, (piece, first, count, plane, row, target) in enumerate(spots):
        src = pieces[piece]
        copies.append(
            pltpu.make_async_copy(
                src.at[plane : plane + count, row[0] : row[0] + row[1], :],
                planes.at[first : first + count, target : target + row[1], :],
                sems.at[n],
            )
        )
    for copy in copies:
        copy.start()
    for copy in copies:
        copy.wait()


def edge_kernel(sleepers, spots, *refs):
    *pieces, out, planes, sems = refs
    gather(spots, pieces, planes, sems)
    height, depth = planes.shape[1:]
    width = out.shape[2]
    spot = lax.broadcasted_iota(jnp.int32, (2 * HB, depth), 0)
    at = lax.broadcasted_iota(jnp.int32, (2 * HB, depth), 1)
    pick = (at == jnp.where(spot < HB, spot, spot + (depth - 2 * HB))).astype(jnp.bfloat16)
    flat = planes.reshape(planes.shape[0] * height, depth)

    def some_rows(block, carry):
        for line in range(8):
            row = 8 * block + line
            high, low = two_parts(row_values(flat, row, height, sleepers, width))
            out[row, :, :] = dot_t(pick, high) + dot_t(pick, low)
        return carry

    lax.fori_loop(0, height // 8, some_rows, 0)


def edges_of(spots, pieces, sleepers, height, depth):
    return pl.pallas_call(
        functools.partial(edge_kernel, sleepers, spots),
        out_shape=jax.ShapeDtypeStruct((height, 2 * HB, lanes_for(sleepers)), jnp.float32),
        in_specs=[pl.BlockSpec(memory_space=pltpu.HBM)]
        + [pl.BlockSpec(memory_space=pl.ANY)] * (len(pieces) - 1),
        out_specs=pl.BlockSpec(memory_space=pltpu.VMEM),
        scratch_shapes=[
            pltpu.VMEM((3 * sleepers + 1, height, depth), jnp.float32),
            pltpu.SemaphoreType.DMA((len(spots),)),
        ],
        compiler_params=pltpu.CompilerParams(vmem_limit_bytes=32 * 1024 * 1024),
        name="edge_columns",
    )(*pieces)


def field_kernel(sleepers, count, seglen, spots, scratch, *refs):
    pl.run_scoped(functools.partial(field_body, sleepers, count, seglen, spots, refs), *scratch)


def field_body(sleepers, count, seglen, spots, refs, *scratch):
    flags, left, right, tw, tc, vectors, edge, *pieces, out = refs
    (planes, sems, source, ghosts, coefs, lhs, lay,
     a1, a2, a3, wide, b1, b2, turn, pages, page_sems) = scratch
    height, depth = planes.shape[1:]
    flat = planes.reshape(planes.shape[0] * height, depth)
    ny = height - 2 * HB
    width = left.shape[2]
    chunks = width // LANES
    cells = 8 * seglen
    page_rows = pages.reshape(2 * count * 48, depth)
    lane = lax.broadcasted_iota(jnp.int32, (8, LANES), 1)
    sub = lax.broadcasted_iota(jnp.int32, (8, LANES), 0)

    def at(zm):
        return pl.ds(8 * (zm + 1), 8)

    def around(first, last):
        before = pltpu.roll(last, 1, 0)
        after = pltpu.roll(first, 7, 0)
        return (
            jnp.where(sub == 0, pltpu.roll(before, HALF, 1), before),
            jnp.where(sub == 7, pltpu.roll(after, HALF, 1), after),
        )

    def line_at(row, zm):
        return pl.ds(pl.multiple_of(((row + 2) & 15) * cells, 8) + 8 * zm, 8)

    def column(q):
        part, c = divmod(q, 3)
        return slice((2 * c + part) * LANES, (2 * c + part + 1) * LANES)

    def read_source(row, q, zm):
        if zm == -1:
            return ghosts[(row + 2) & 15, q, :8, :]
        if zm == seglen:
            return ghosts[(row + 2) & 15, q, 8:, :]
        return source[line_at(row, zm), column(q)]

    def reader(ring):
        def read(row, q, zm):
            outside = ((row < HY) & (flags[0] == 1)) | ((row >= HY + ny) & (flags[1] == 1))
            return ring[jnp.where(outside, RING, lax.rem(row, RING)), q, at(zm), :]

        return read

    def produce(block):
        def two_lines(pair, carry):
            for k in range(2):
                srow = jnp.maximum(8 * block + 2 * pair + k - 2 + (HB - HY), 0)
                values = row_values(flat, srow, height, sleepers, width)
                for n in range(chunks):
                    span = slice(n * LANES, (n + 1) * LANES)
                    lay[k * chunks + n, HB : HB + depth, :] = jnp.transpose(values[span])
                    lay[k * chunks + n, :HB, :] = left[srow, :, span]
                    lay[k * chunks + n, HB + depth :, :] = right[srow, :, span]
            halves = [[], []]
            for k in range(2):
                for half in range(2):
                    for zm in range(seglen):
                        spot = pl.ds(half * cells + zm, 8, stride=seglen)
                        pieces_at = [lay[k * chunks + n, spot, :] for n in range(chunks)]
                        halves[half].append(jnp.concatenate(pieces_at, axis=1))
            values = jnp.concatenate(
                [jnp.concatenate(half, axis=0) for half in halves], axis=1
            )
            high, low = two_parts(values)
            rows = pl.ds(pl.multiple_of(2 * cells * pair, 16), 2 * cells)
            lhs[rows, : 2 * width] = high
            lhs[rows, 2 * width : 4 * width] = low
            lhs[rows, 4 * width :] = high
            return carry

        lax.fori_loop(0, 4, two_lines, 0)
        target = pl.ds(pl.multiple_of((block & 1) * (8 * cells), 8), 8 * cells)
        for c in range(3):
            span = slice(2 * c * LANES, 2 * (c + 1) * LANES)
            source[target, span] = dot(lhs[...], tw[:, span])
        for f in range(0, 8, 2):
            span = slice(f * LANES, (f + 2) * LANES)
            coefs[target, span] = dot(lhs[:, : 2 * width], tc[:, span])

        def one_line(line, carry):
            row = 8 * block - 2 + line
            for q in range(6):
                first = read_source(row, q, 0)
                last = read_source(row, q, seglen - 1)
                ghosts[(row + 2) & 15, q, :8, :], ghosts[(row + 2) & 15, q, 8:, :] = around(
                    first, last
                )
            return carry

        lax.fori_loop(0, 8, one_line, 0)

    def apply(src, row, emit, shift=None, extra=None):
        cur = [[src(row + k, q, 0) for q in range(6)] for k in range(2)]
        behind = [
            [src(row + k, q, -1) + (cur[1][q] if k == 0 else src(row + 2, q, 0)) for q in range(6)]
            for k in range(2)
        ]
        for zm in range(seglen):
            nxt = [[src(row + k, q, zm + 1) for q in range(6)] for k in range(2)]
            ahead = [
                [src(row - 1, q, zm) + nxt[0][q] for q in range(6)],
                [cur[0][q] + nxt[1][q] for q in range(6)],
            ]
            if zm + 1 < seglen:
                below = [cur[1][q] + src(row + 2, q, zm + 1) for q in range(6)]
            for k in range(2):
                f = [
                    coefs[line_at(row + k, zm), n * LANES : (n + 1) * LANES] for n in range(7)
                ]
                diagonal = f[:3]
                if shift is not None:
                    diagonal = [d + shift for d in diagonal]
                matrix = (
                    (diagonal[0], f[3], f[4]),
                    (f[3], diagonal[1], f[5]),
                    (f[4], f[5], diagonal[2]),
                )
                results = []
                for q in range(6):
                    part, c = divmod(q, 3)
                    mine = cur[k][3 * part : 3 * part + 3]
                    own = matrix[c][0] * mine[0] + matrix[c][1] * mine[1] + matrix[c][2] * mine[2]
                    damp = f[6] * cur[k][3 * (1 - part) + c]
                    total = (ahead[k][q] + behind[k][q]) + own
                    total = total + damp if part == 0 else total - damp
                    if extra is not None:
                        total = total + extra[1] * extra[0](row + k, q, zm)
                    results.append(total)
                emit(k, zm, results)
            if zm + 1 < seglen:
                behind = [ahead[1], below]
            cur = nxt

    def stage(src, dst, row, extra=None):
        ends = {}

        def emit(k, zm, results):
            if zm == HB - 1:
                results = [value * edge[0] for value in results]
            if zm == (HB + depth) % seglen:
                results = [value * edge[1] for value in results]
            slot = lax.rem(row + k, RING)
            for q in range(6):
                dst[slot, q, at(zm), :] = results[q]
            if zm in (0, seglen - 1):
                ends[k, zm] = results
            if zm == seglen - 1:
                for q in range(6):
                    dst[slot, q, at(-1), :], dst[slot, q, at(seglen), :] = around(
                        ends[k, 0][q], results[q]
                    )

        apply(src, row, emit, extra=extra)

    def finish(row, start):
        def emit(k, zm, results):
            for c in range(3):
                real, imag = results[c], results[3 + c]
                first = jnp.where(lane < HALF, real, pltpu.roll(imag, HALF, 1))
                second = jnp.where(lane < HALF, pltpu.roll(real, HALF, 1), imag)
                turn[3 * k + c, pl.ds(zm, 8, stride=seglen), :] = first
                turn[3 * k + c, pl.ds(cells + zm, 8, stride=seglen), :] = second

        apply(reader(b2), row, emit, shift=vectors[3])
        for k in range(2):
            for c in range(3):
                turned = jnp.transpose(turn[3 * k + c, HB : HB + depth, :])
                for part in range(2):
                    rows = pl.ds(start + (part * 3 + c) * 8 + k, count, stride=48)
                    page_rows[rows, :] = turned[part * HALF : part * HALF + count]

    stages = (
        lambda row: stage(read_source, a1, row),
        lambda row: stage(reader(a1), a2, row, (read_source, vectors[0])),
        lambda row: stage(reader(a2), a3, row),
        lambda row: stage(reader(a3), wide, row, (read_source, vectors[1])),
        lambda row: stage(reader(wide), b1, row),
        lambda row: stage(reader(b1), b2, row, (reader(wide), vectors[2])),
    )

    def page_copy(block):
        return pltpu.make_async_copy(
            pages.at[block & 1],
            out.at[:, :, :, pl.ds(pl.multiple_of(8 * block, 8), 8), :],
            page_sems.at[block & 1],
        )

    def one_block(block, carry):
        produce(block)
        for t, run in enumerate(stages, 1):

            def two_rows(pair, carry):
                run(8 * block + 2 * pair - 2 - t)
                return carry

            lax.fori_loop(jnp.clip(t + 1 - 4 * block, 0, 4), 4, two_rows, 0)

        @pl.when(block >= 2)
        def _():
            done = block - 2

            @pl.when(done >= 2)
            def _():
                page_copy(done - 2).wait()

            def two_rows(pair, carry):
                start = pl.multiple_of((done & 1) * (count * 48), 8) + 2 * pair
                finish(8 * block + 2 * pair - 9, start)
                return carry

            lax.fori_loop(0, 4, two_rows, 0)
            page_copy(done).start()

        return carry

    gather(spots, pieces, planes, sems)
    for ring in (a1, a2, a3, wide, b1, b2):
        for q in range(6):
            ring[RING, q, :, :] = jnp.zeros(ring.shape[2:], jnp.float32)
    blocks = ny // 8
    lax.fori_loop(0, blocks + 2, one_block, 0)
    for block in range(max(blocks - 2, 0), blocks):
        page_copy(block).wait()


def solve_field(spots, pieces, flags, left, right, tw, tc, vectors, edge, sleepers, count):
    height, _, width = left.shape
    depth = pieces[0].shape[2]
    ny = height - 2 * HB
    seglen = (depth + 2 * HB) // SEGS
    cells = 8 * seglen
    chunks = width // LANES
    ring = pltpu.VMEM((RING + 1, 6, 8 * (seglen + 2), LANES), jnp.float32)
    whole = pl.BlockSpec(memory_space=pltpu.VMEM)
    scratch = (
        pltpu.VMEM((3 * sleepers + 1, height, depth), jnp.float32),
        pltpu.SemaphoreType.DMA((len(spots),)),
        pltpu.VMEM((16 * cells, 6 * LANES), jnp.float32),
        pltpu.VMEM((16, 6, 16, LANES), jnp.float32),
        pltpu.VMEM((16 * cells, 8 * LANES), jnp.float32),
        pltpu.VMEM((8 * cells, 6 * width), jnp.bfloat16),
        pltpu.VMEM((2 * chunks, 2 * cells, LANES), jnp.float32),
        ring, ring, ring, ring, ring, ring,
        pltpu.VMEM((6, 2 * cells, LANES), jnp.float32),
        pltpu.VMEM((2, count, 2, 3, 8, depth), jnp.float32),
        pltpu.SemaphoreType.DMA((2,)),
    )
    return pl.pallas_call(
        functools.partial(field_kernel, sleepers, count, seglen, spots, scratch),
        out_shape=jax.ShapeDtypeStruct((count, 2, 3, ny, depth), jnp.float32),
        in_specs=[pl.BlockSpec(memory_space=pltpu.SMEM)]
        + [whole] * 6
        + [pl.BlockSpec(memory_space=pltpu.HBM)]
        + [pl.BlockSpec(memory_space=pl.ANY)] * (len(pieces) - 1),
        out_specs=pl.BlockSpec(memory_space=pl.ANY),
        compiler_params=pltpu.CompilerParams(vmem_limit_bytes=(38 + 4 * chunks) * 1024 * 1024),
        name="adjoint_field",
    )(flags, left, right, tw, tc, vectors, edge, *pieces)


def local(loads, sleeper_pos, material, material_table):
    ka = lax.axis_size("ka")
    gy, gz = lax.axis_size("gy"), lax.axis_size("gz")
    count = KW // ka
    wave_start = lax.axis_index("ka") * count
    sleepers = ka * loads.shape[0]
    own = 3 * loads.shape[0]
    ny, depth = material.shape
    height = ny + 2 * HB
    loads = loads.reshape(own, ny, depth)
    material = material.astype(jnp.float32)[None]

    def shift(array, axis, size, by):
        pairs = [(i, i + by) for i in range(size) if 0 <= i + by < size]
        return lax.ppermute(array, axis, pairs)

    turns = [[(i, (i + step) % ka) for i in range(ka)] for step in range(1, ka)]
    ends = jnp.concatenate([loads[:, :HB], loads[:, ny - HB :]], axis=1)
    got_ends = [lax.ppermute(ends, "ka", turn) for turn in turns]
    inner = loads[:, HB : ny - HB]
    got_inner = [lax.ppermute(inner, "ka", turn) for turn in turns]
    all_pos = [sleeper_pos] + [lax.ppermute(sleeper_pos, "ka", turn) for turn in turns]
    tw, tc, vectors = tables(
        jnp.concatenate(all_pos), material_table, wave_start, count, lanes_for(sleepers)
    )
    tw, tc, vectors, tied = lax.optimization_barrier((tw, tc, vectors, loads))
    low = jnp.concatenate([tied[:, :HB], material[:, :HB]], axis=0)
    high = jnp.concatenate([tied[:, ny - HB :], material[:, ny - HB :]], axis=0)
    above, below = shift(high, "gy", gy, 1), shift(low, "gy", gy, -1)

    pieces = [loads, material, above, below]
    spots = [
        (0, 0, own, 0, (0, ny), HB),
        (1, 3 * sleepers, 1, 0, (0, ny), HB),
        (2, 0, own, 0, (0, HB), 0),
        (2, 3 * sleepers, 1, own, (0, HB), 0),
        (3, 0, own, 0, (0, HB), HB + ny),
        (3, 3 * sleepers, 1, own, (0, HB), HB + ny),
    ]
    for step, (outer, middle) in enumerate(zip(got_ends, got_inner)):
        first = own * (step + 1)
        number = len(pieces)
        pieces += [
            outer,
            middle,
            shift(outer[:, HB:], "gy", gy, 1),
            shift(outer[:, :HB], "gy", gy, -1),
        ]
        spots += [
            (number, first, own, 0, (0, HB), HB),
            (number, first, own, 0, (HB, HB), ny),
            (number + 1, first, own, 0, (0, ny - 2 * HB), 2 * HB),
            (number + 2, first, own, 0, (0, HB), 0),
            (number + 3, first, own, 0, (0, HB), HB + ny),
        ]

    y_at, z_at = lax.axis_index("gy"), lax.axis_index("gz")
    flags = jnp.stack([y_at == 0, y_at == gy - 1]).astype(jnp.int32)
    sub = jnp.arange(8)[:, None]
    lane = jnp.arange(LANES)[None, :]
    edge = jnp.stack(
        [
            jnp.where((z_at == 0) & (sub == 0) & (lane < HALF), 0.0, 1.0),
            jnp.where((z_at == gz - 1) & (sub == 7) & (lane >= HALF), 0.0, 1.0),
        ]
    ).astype(jnp.float32)
    pieces[-1], flags, edge = lax.optimization_barrier((pieces[-1], flags, edge))

    columns = edges_of(spots, pieces, sleepers, height, depth)
    left = shift(columns[:, HB:], "gz", gz, 1)
    right = shift(columns[:, :HB], "gz", gz, -1)
    return solve_field(
        spots, pieces, flags, left, right, tw, tc, vectors, edge, sleepers, count
    )


def solution(mesh):
    return jax.shard_map(
        local,
        mesh=mesh,
        in_specs=(P("ka", None, "gy", "gz"), P("ka"), P("gy", "gz"), P()),
        out_specs=P("ka", None, None, "gy", "gz"),
        check_vma=False,
    )
```

```python
import functools
import math

import jax
import jax.numpy as jnp
from jax import lax
from jax.experimental import pallas as pl
from jax.experimental.pallas import tpu as pltpu
from jax.sharding import PartitionSpec as P

KW = 128
NMAT = 8
DEG = 4
LANES = 128
HALF = 64
SEGS = 16
HY = 7
HB = 8


def lanes_for(sleepers):
    return -(-(3 * sleepers + 3 * NMAT) // LANES) * LANES


def two_parts(values):
    high = values.astype(jnp.bfloat16)
    low = (values - high.astype(jnp.float32)).astype(jnp.bfloat16)
    return high, low


def dot(a, b):
    return lax.dot_general(a, b, (((1,), (0,)), ((), ())), preferred_element_type=jnp.float32)


def dot_t(a, b):
    return lax.dot_general(a, b, (((1,), (1,)), ((), ())), preferred_element_type=jnp.float32)


def table_kernel(sleepers, count, start, table, cells, positions, tw, tc, vectors):
    width = tc.shape[0] // 2
    lane = lax.broadcasted_iota(jnp.int32, (8, LANES), 1)
    wave = lane % HALF
    live = wave < count
    wave = wave + start[0]
    q = (2.0 * jnp.sin(wave.astype(jnp.float32) * (math.pi / KW))) ** 2
    lowest = highest = None
    for m in range(NMAT):
        s, xx, yy, zz, xy, xz, yz = (jnp.full((8, LANES), table[m, f]) for f in range(7))
        xy, xz, yz = jnp.abs(xy), jnp.abs(xz), jnp.abs(yz)
        sums = (xy + xz, xy + yz, xz + yz)
        low = s + q * functools.reduce(jnp.minimum, [d - r for d, r in zip((xx, yy, zz), sums)])
        high = s + q * functools.reduce(jnp.maximum, [d + r for d, r in zip((xx, yy, zz), sums)])
        lowest = low if m == 0 else jnp.minimum(lowest, low)
        highest = high if m == 0 else jnp.maximum(highest, high)
    highest = 8.0 + highest
    center = 0.5 * (highest + lowest)
    half_width = 0.5 * (highest - lowest)
    ratio2 = (center / half_width) ** 2
    top = 8.0 * ratio2 * (ratio2 - 1.0) + 1.0
    h2 = half_width * half_width
    h4 = h2 * h2
    scale = 8.0 / (top * h4)
    scale = jnp.where(live, scale * scale, 0.0)
    twice = h2 * jnp.sqrt(0.5 * (top + 1.0))
    shift = 0.5 * jnp.sqrt(twice + h2)
    tilt = 0.5 * jnp.sqrt(jnp.maximum(twice - h2, 0.0))
    for n, vector in enumerate((shift, tilt, jnp.sqrt(lowest * highest), center)):
        vectors[n, :, :] = jnp.where(live, vector, 0.0)

    tc[...] = jnp.zeros(tc.shape, jnp.bfloat16)
    tw[...] = jnp.zeros(tw.shape, jnp.bfloat16)
    column = [jnp.broadcast_to(cells[:, f : f + 1], (8, LANES)) for f in range(8)]
    fields = [center - 4.0 - column[0] - q * column[c] for c in (1, 2, 3)]
    fields += [-q * column[c] for c in (4, 5, 6)] + [q * column[7]]
    rounded = lambda values: values.astype(jnp.bfloat16).astype(jnp.float32)
    for f, field in enumerate(fields):
        field = jnp.where(live, field, 0.0)
        first = rounded(field)
        second = rounded(field - first)
        third = field - first - second
        rows = jnp.concatenate([first, second, third, jnp.zeros_like(first)], axis=0)
        lanes = lax.broadcasted_iota(jnp.int32, rows.shape, 1)
        for half in range(2):
            kept = jnp.where(lanes // HALF == half, rows, 0.0).astype(jnp.bfloat16)
            at = half * width + 3 * sleepers
            tc[at : at + 32, f * LANES : (f + 1) * LANES] = kept

    turns = (positions[...] * wave[:1]) & (KW - 1)
    angles = turns.astype(jnp.float32) * (2.0 * math.pi / KW)
    lanes = lax.broadcasted_iota(jnp.int32, turns.shape, 1)
    for part, phase in enumerate((jnp.cos(angles), -jnp.sin(angles))):
        phase = phase * scale[:1]
        high = rounded(phase)
        for segment, values in enumerate((high, high, phase - high)):
            for half in range(2):
                kept = jnp.where(lanes // HALF == half, values, 0.0).astype(jnp.bfloat16)
                for c in range(3):
                    at = (2 * segment + half) * width + c * sleepers
                    to = (2 * c + part) * LANES
                    tw[at : at + sleepers, to : to + LANES] = kept


def tables(positions, material_table, start, count, width):
    sleepers = positions.shape[0]
    spots = jnp.broadcast_to(positions[:, None], (sleepers, LANES))
    return pl.pallas_call(
        functools.partial(table_kernel, sleepers, count),
        out_shape=(
            jax.ShapeDtypeStruct((6 * width, 6 * LANES), jnp.bfloat16),
            jax.ShapeDtypeStruct((2 * width, 8 * LANES), jnp.bfloat16),
            jax.ShapeDtypeStruct((4, 8, LANES), jnp.float32),
        ),
        in_specs=[pl.BlockSpec(memory_space=pltpu.SMEM)] * 2
        + [pl.BlockSpec(memory_space=pltpu.VMEM)] * 2,
        out_specs=(pl.BlockSpec(memory_space=pltpu.VMEM),) * 3,
        compiler_params=pltpu.CompilerParams(vmem_limit_bytes=32 * 1024 * 1024),
        name="tables",
    )(start.reshape(1), material_table, material_table, spots)


def row_values(planes, row, height, sleepers, width):
    depth = planes.shape[1]
    parts = [planes[pl.ds(c * height + row, sleepers, stride=3 * height), :] for c in range(3)]
    material = planes[pl.ds(3 * sleepers * height + row, 1), :]
    number = lax.broadcasted_iota(jnp.int32, (width - 3 * sleepers, depth), 0)
    kind = jnp.where(number < 3 * NMAT, number % NMAT, -1).astype(jnp.float32)
    parts.append((kind == material).astype(jnp.float32))
    return jnp.concatenate(parts, axis=0)


def gather(spots, pieces, planes, sems):
    copies = []
    for n, (piece, first, count, plane, row, target) in enumerate(spots):
        src = pieces[piece]
        copies.append(
            pltpu.make_async_copy(
                src.at[plane : plane + count, row[0] : row[0] + row[1], :],
                planes.at[first : first + count, target : target + row[1], :],
                sems.at[n],
            )
        )
    for copy in copies:
        copy.start()
    for copy in copies:
        copy.wait()


def edge_kernel(sleepers, spots, *refs):
    *pieces, out, planes, sems = refs
    gather(spots, pieces, planes, sems)
    height, depth = planes.shape[1:]
    width = out.shape[2]
    spot = lax.broadcasted_iota(jnp.int32, (2 * HB, depth), 0)
    at = lax.broadcasted_iota(jnp.int32, (2 * HB, depth), 1)
    pick = (at == jnp.where(spot < HB, spot, spot + (depth - 2 * HB))).astype(jnp.bfloat16)
    flat = planes.reshape(planes.shape[0] * height, depth)

    def some_rows(block, carry):
        for line in range(8):
            row = 8 * block + line
            high, low = two_parts(row_values(flat, row, height, sleepers, width))
            out[row, :, :] = dot_t(pick, high) + dot_t(pick, low)
        return carry

    lax.fori_loop(0, height // 8, some_rows, 0)


def edges_of(spots, pieces, sleepers, height, depth):
    return pl.pallas_call(
        functools.partial(edge_kernel, sleepers, spots),
        out_shape=jax.ShapeDtypeStruct((height, 2 * HB, lanes_for(sleepers)), jnp.float32),
        in_specs=[pl.BlockSpec(memory_space=pl.ANY)] * len(pieces),
        out_specs=pl.BlockSpec(memory_space=pltpu.VMEM),
        scratch_shapes=[
            pltpu.VMEM((3 * sleepers + 1, height, depth), jnp.float32),
            pltpu.SemaphoreType.DMA((len(spots),)),
        ],
        compiler_params=pltpu.CompilerParams(vmem_limit_bytes=32 * 1024 * 1024),
        name="edge_columns",
    )(*pieces)


def field_kernel(sleepers, count, seglen, spots, scratch, *refs):
    pl.run_scoped(functools.partial(field_body, sleepers, count, seglen, spots, refs), *scratch)


def field_body(sleepers, count, seglen, spots, refs, *scratch):
    flags, left, right, tw, tc, vectors, edge, *pieces, out = refs
    planes, sems, source, ghosts, coefs, made, lhs, lay, *rings = scratch[:14]
    turn, pages, page_sems = scratch[14:]
    height, depth = planes.shape[1:]
    flat = planes.reshape(planes.shape[0] * height, depth)
    ny = height - 2 * HB
    width = left.shape[2]
    chunks = width // LANES
    cells = 8 * seglen
    page_rows = pages.reshape(2 * count * 48, depth)
    lane = lax.broadcasted_iota(jnp.int32, (8, LANES), 1)
    sub = lax.broadcasted_iota(jnp.int32, (8, LANES), 0)

    def at(zm):
        return pl.ds(8 * (zm + 1), 8)

    def around(first, last):
        before = pltpu.roll(last, 1, 0)
        after = pltpu.roll(first, 7, 0)
        return (
            jnp.where(sub == 0, pltpu.roll(before, HALF, 1), before),
            jnp.where(sub == 7, pltpu.roll(after, HALF, 1), after),
        )

    def line_at(row, zm):
        return pl.ds(pl.multiple_of((row & 15) * cells, 8) + 8 * zm, 8)

    def column(q):
        part, c = divmod(q, 3)
        return slice((2 * c + part) * LANES, (2 * c + part + 1) * LANES)

    def read_source(row, q, zm):
        if zm == -1:
            return ghosts[row & 3, q, :8, :]
        if zm == seglen:
            return ghosts[row & 3, q, 8:, :]
        rows = pl.ds(pl.multiple_of((row & 3) * cells, 8) + 8 * zm, 8)
        return source[rows, column(q)]

    def reader(ring):
        def read(row, q, zm):
            outside = ((row < HY) & (flags[0] == 1)) | ((row >= HY + ny) & (flags[1] == 1))
            return ring[jnp.where(outside, 4, row & 3), q, at(zm), :]

        return read

    def produce(pair):
        def lay_out(k):
            srow = jnp.clip(2 * pair - 2 + k + (HB - HY), 0, height - 1)
            values = row_values(flat, srow, height, sleepers, width)
            for n in range(chunks):
                span = slice(n * LANES, (n + 1) * LANES)
                lay[k * chunks + n, HB : HB + depth, :] = jnp.transpose(values[span])
                lay[k * chunks + n, :HB, :] = left[srow, :, span]
                lay[k * chunks + n, HB + depth :, :] = right[srow, :, span]

        def split():
            halves = [[], []]
            for k in range(2):
                for half in range(2):
                    for zm in range(seglen):
                        spot = pl.ds(half * cells + zm, 8, stride=seglen)
                        pieces_at = [lay[k * chunks + n, spot, :] for n in range(chunks)]
                        halves[half].append(jnp.concatenate(pieces_at, axis=1))
            values = jnp.concatenate(
                [jnp.concatenate(half, axis=0) for half in halves], axis=1
            )
            high, low = two_parts(values)
            lhs[:, : 2 * width] = high
            lhs[:, 2 * width : 4 * width] = low
            lhs[:, 4 * width :] = high

        first_row = 2 * pair - 2
        target = pl.ds(pl.multiple_of((first_row & 3) * cells, 8), 2 * cells)

        def spectrum(c):
            span = slice(2 * c * LANES, 2 * (c + 1) * LANES)
            source[target, span] = dot(lhs[...], tw[:, span])

        def fields(f):
            span = slice(f * LANES, (f + 2) * LANES)
            made[:, span] = dot(lhs[:, : 2 * width], tc[:, span])

        def wrap(k):
            row = first_row + k
            for q in range(6):
                ghosts[row & 3, q, :8, :], ghosts[row & 3, q, 8:, :] = around(
                    read_source(row, q, 0), read_source(row, q, seglen - 1)
                )

        return (
            [functools.partial(lay_out, 0), functools.partial(lay_out, 1), split],
            [functools.partial(spectrum, c) for c in range(3)]
            + [functools.partial(fields, f) for f in range(0, 8, 2)]
            + [functools.partial(wrap, k) for k in range(2)],
        )

    def commit(pair):
        def move(k, zm):
            rows = slice(k * cells + 8 * zm, k * cells + 8 * zm + 8)
            for n in range(7):
                span = slice(n * LANES, (n + 1) * LANES)
                coefs[line_at(2 * pair - 2 + k, zm), span] = made[rows, span]

        return [functools.partial(move, k, zm) for k in range(2) for zm in range(seglen)]

    def apply(src, row, emit, shift=None, tilt=None):
        cur = [[src(row + k, q, 0) for q in range(6)] for k in range(2)]
        behind = [
            [src(row + k, q, -1) + (cur[1][q] if k == 0 else src(row + 2, q, 0)) for q in range(6)]
            for k in range(2)
        ]
        for zm in range(seglen):
            nxt = [[src(row + k, q, zm + 1) for q in range(6)] for k in range(2)]
            ahead = [
                [src(row - 1, q, zm) + nxt[0][q] for q in range(6)],
                [cur[0][q] + nxt[1][q] for q in range(6)],
            ]
            if zm + 1 < seglen:
                below = [cur[1][q] + src(row + 2, q, zm + 1) for q in range(6)]
            for k in range(2):
                f = [
                    coefs[line_at(row + k, zm), n * LANES : (n + 1) * LANES] for n in range(7)
                ]
                diagonal, damping = f[:3], f[6]
                if shift is not None:
                    diagonal = [d + shift for d in diagonal]
                if tilt is not None:
                    damping = damping - tilt
                matrix = (
                    (diagonal[0], f[3], f[4]),
                    (f[3], diagonal[1], f[5]),
                    (f[4], f[5], diagonal[2]),
                )
                results = []
                for q in range(6):
                    part, c = divmod(q, 3)
                    mine = cur[k][3 * part : 3 * part + 3]
                    own = matrix[c][0] * mine[0] + matrix[c][1] * mine[1] + matrix[c][2] * mine[2]
                    damp = damping * cur[k][3 * (1 - part) + c]
                    total = (ahead[k][q] + behind[k][q]) + own
                    total = total + damp if part == 0 else total - damp
                    results.append(total)
                emit(k, zm, results)
            if zm + 1 < seglen:
                behind = [ahead[1], below]
            cur = nxt

    def stage(src, dst, row, shift, tilt, between=None):
        ends = {}

        def emit(k, zm, results):
            if zm == HB - 1:
                results = [value * edge[0] for value in results]
            if zm == (HB + depth) % seglen:
                results = [value * edge[1] for value in results]
            slot = (row + k) & 3
            for q in range(6):
                dst[slot, q, at(zm), :] = results[q]
            if zm in (0, seglen - 1):
                ends[k, zm] = results
            if zm == seglen - 1:
                for q in range(6):
                    dst[slot, q, at(-1), :], dst[slot, q, at(seglen), :] = around(
                        ends[k, 0][q], results[q]
                    )
            if between is not None:
                between()

        apply(src, row, emit, shift, tilt)

    def last_stage(row, between=None):
        def emit(k, zm, results):
            for c in range(3):
                real, imag = results[c], results[3 + c]
                first = jnp.where(lane < HALF, real, pltpu.roll(imag, HALF, 1))
                second = jnp.where(lane < HALF, pltpu.roll(real, HALF, 1), imag)
                turn[3 * k + c, pl.ds(zm, 8, stride=seglen), :] = first
                turn[3 * k + c, pl.ds(cells + zm, 8, stride=seglen), :] = second
            if between is not None:
                between()

        apply(reader(rings[5]), row, emit, shift=vectors[3])

    def run_stage(t, base, between=None):
        shift = (1, 1, -1, -1, 0, 0)[t - 1]
        shift = shift * vectors[0] if shift else None
        tilt = (vectors[1] if t <= 4 else vectors[2]) * (1 if t % 2 else -1)
        src = read_source if t == 1 else reader(rings[t - 2])
        stage(src, rings[t - 1], base - t, shift, tilt, between)

    def spread(tasks, slots):
        total, seen, left_over = len(tasks), [0], list(tasks)

        def between():
            seen[0] += 1
            while left_over and (total - len(left_over)) * slots < seen[0] * total:
                left_over.pop(0)()

        return between

    def mixed(first, second):
        tasks = []
        for n in range(max(len(first), len(second))):
            tasks += first[n : n + 1] + second[n : n + 1]
        return tasks

    def finish(pair):
        done = pair - HB
        block = done >> 2
        start = pl.multiple_of((block & 1) * (count * 48), 8) + 2 * (done & 3)

        def page(k, c):
            turned = jnp.transpose(turn[3 * k + c, HB : HB + depth, :])
            for part in range(2):
                rows = pl.ds(start + (part * 3 + c) * 8 + k, count, stride=48)
                page_rows[rows, :] = turned[part * HALF : part * HALF + count]

        return [functools.partial(page, k, c) for k in range(2) for c in range(3)]

    def page_copy(block):
        return pltpu.make_async_copy(
            pages.at[block & 1],
            out.at[:, :, :, pl.ds(pl.multiple_of(8 * block, 8), 8), :],
            page_sems.at[block & 1],
        )

    def ramp(pair, carry):
        base = 2 * pair - 2
        early, late = produce(pair + 1)
        for t, tasks in ((1, early), (2, late)):

            @pl.when(base >= 2 * t)
            def _():
                run_stage(t, base, spread(tasks, 2 * seglen))

            @pl.when(base < 2 * t)
            def _():
                for task in tasks:
                    task()

        for t in range(3, 7):

            @pl.when(base >= 2 * t)
            def _():
                run_stage(t, base)

        @pl.when(base >= 14)
        def _():
            last_stage(base - 7)

        for task in commit(pair + 1):
            task()
        return carry

    def steady(pair, carry):
        base = 2 * pair - 2
        done = pair - 1 - HB

        @pl.when(((done & 3) == 0) & (done >= 8))
        def _():
            page_copy((done >> 2) - 2).wait()

        early, late = produce(pair + 1)
        turning = finish(pair - 1)
        run_stage(1, base, spread(mixed(early, turning[:2]), 2 * seglen))
        between = spread(mixed(late, turning[2:]), 10 * seglen)
        for t in range(2, 7):
            run_stage(t, base, between)
        last_stage(base - 7, spread(commit(pair + 1), 2 * seglen))

        @pl.when((done & 3) == 3)
        def _():
            page_copy(done >> 2).start()

        return carry

    gather(spots, pieces, planes, sems)
    for ring in rings:
        for q in range(6):
            ring[4, q, :, :] = jnp.zeros(ring.shape[2:], jnp.float32)
    early, late = produce(0)
    for task in early + late + commit(0):
        task()
    final = HB + ny // 2 - 1
    lax.fori_loop(0, HB + 1, ramp, 0)
    lax.fori_loop(HB + 1, final + 1, steady, 0)
    for step in finish(final):
        step()
    blocks = ny // 8
    page_copy(blocks - 1).start()
    for block in range(max(blocks - 2, 0), blocks):
        page_copy(block).wait()


def solve_field(spots, pieces, flags, left, right, tw, tc, vectors, edge, sleepers, count):
    height, _, width = left.shape
    depth = pieces[0].shape[2]
    ny = height - 2 * HB
    seglen = (depth + 2 * HB) // SEGS
    cells = 8 * seglen
    chunks = width // LANES
    ring = pltpu.VMEM((5, 6, 8 * (seglen + 2), LANES), jnp.float32)
    whole = pl.BlockSpec(memory_space=pltpu.VMEM)
    scratch = (
        pltpu.VMEM((3 * sleepers + 1, height, depth), jnp.float32),
        pltpu.SemaphoreType.DMA((len(spots),)),
        pltpu.VMEM((4 * cells, 6 * LANES), jnp.float32),
        pltpu.VMEM((4, 6, 16, LANES), jnp.float32),
        pltpu.VMEM((16 * cells, 7 * LANES), jnp.float32),
        pltpu.VMEM((2 * cells, 8 * LANES), jnp.float32),
        pltpu.VMEM((2 * cells, 6 * width), jnp.bfloat16),
        pltpu.VMEM((2 * chunks, 2 * cells, LANES), jnp.float32),
        ring, ring, ring, ring, ring, ring,
        pltpu.VMEM((6, 2 * cells, LANES), jnp.float32),
        pltpu.VMEM((2, count, 2, 3, 8, depth), jnp.float32),
        pltpu.SemaphoreType.DMA((2,)),
    )
    return pl.pallas_call(
        functools.partial(field_kernel, sleepers, count, seglen, spots, scratch),
        out_shape=jax.ShapeDtypeStruct((count, 2, 3, ny, depth), jnp.float32),
        in_specs=[pl.BlockSpec(memory_space=pltpu.SMEM)]
        + [whole] * 6
        + [pl.BlockSpec(memory_space=pl.ANY)] * len(pieces),
        out_specs=pl.BlockSpec(memory_space=pl.ANY),
        compiler_params=pltpu.CompilerParams(vmem_limit_bytes=40 * 1024 * 1024),
        name="adjoint_field",
    )(flags, left, right, tw, tc, vectors, edge, *pieces)


def local(loads, sleeper_pos, material, material_table):
    ka = lax.axis_size("ka")
    gy, gz = lax.axis_size("gy"), lax.axis_size("gz")
    count = KW // ka
    wave_start = lax.axis_index("ka") * count
    sleepers = ka * loads.shape[0]
    own = 3 * loads.shape[0]
    ny, depth = material.shape
    height = ny + 2 * HB
    loads = loads.reshape(own, ny, depth)
    material = material.astype(jnp.float32)[None]

    def shift(array, axis, size, by):
        pairs = [(i, i + by) for i in range(size) if 0 <= i + by < size]
        return lax.ppermute(array, axis, pairs)

    turns = [[(i, (i + step) % ka) for i in range(ka)] for step in range(1, ka)]
    ends = jnp.concatenate([loads[:, :HB], loads[:, ny - HB :]], axis=1)
    got_ends = [lax.ppermute(ends, "ka", turn) for turn in turns]
    inner = loads[:, HB : ny - HB]
    got_inner = [lax.ppermute(inner, "ka", turn) for turn in turns]
    all_pos = [sleeper_pos] + [lax.ppermute(sleeper_pos, "ka", turn) for turn in turns]
    met, tied = lax.optimization_barrier((all_pos, loads))
    low = jnp.concatenate([tied[:, :HB], material[:, :HB]], axis=0)
    high = jnp.concatenate([tied[:, ny - HB :], material[:, ny - HB :]], axis=0)
    above, below = shift(high, "gy", gy, 1), shift(low, "gy", gy, -1)

    pieces, spots = [], []

    def place(array, *where):
        pieces.append(array)
        spots.extend((len(pieces) - 1, *spot) for spot in where)

    def place_middle(first, outer, middle):
        place(outer, (first, own, 0, (0, HB), HB), (first, own, 0, (HB, HB), ny))
        place(middle, (first, own, 0, (0, ny - 2 * HB), 2 * HB))

    place_middle(0, ends, inner)
    place(material, (3 * sleepers, 1, 0, (0, ny), HB))
    for array, row in ((above, 0), (below, HB + ny)):
        place(array, (0, own, 0, (0, HB), row), (3 * sleepers, 1, own, (0, HB), row))
    for step, (outer, middle) in enumerate(zip(got_ends, got_inner), 1):
        place_middle(own * step, outer, middle)
        place(shift(outer[:, HB:], "gy", gy, 1), (own * step, own, 0, (0, HB), 0))
        place(shift(outer[:, :HB], "gy", gy, -1), (own * step, own, 0, (0, HB), HB + ny))

    met, _ = lax.optimization_barrier((met, got_ends))
    tw, tc, vectors = tables(
        jnp.concatenate(met), material_table, wave_start, count, lanes_for(sleepers)
    )
    y_at, z_at = lax.axis_index("gy"), lax.axis_index("gz")
    flags = jnp.stack([y_at == 0, y_at == gy - 1]).astype(jnp.int32)
    sub = jnp.arange(8)[:, None]
    lane = jnp.arange(LANES)[None, :]
    edge = jnp.stack(
        [
            jnp.where((z_at == 0) & (sub == 0) & (lane < HALF), 0.0, 1.0),
            jnp.where((z_at == gz - 1) & (sub == 7) & (lane >= HALF), 0.0, 1.0),
        ]
    ).astype(jnp.float32)
    pieces[-1], flags, edge = lax.optimization_barrier((pieces[-1], flags, edge))

    columns = edges_of(spots, pieces, sleepers, height, depth)
    left = shift(columns[:, HB:], "gz", gz, 1)
    right = shift(columns[:, :HB], "gz", gz, -1)
    return solve_field(
        spots, pieces, flags, left, right, tw, tc, vectors, edge, sleepers, count
    )


def solution(mesh):
    return jax.shard_map(
        local,
        mesh=mesh,
        in_specs=(P("ka", None, "gy", "gz"), P("ka"), P("gy", "gz"), P()),
        out_specs=P("ka", None, None, "gy", "gz"),
        check_vma=False,
    )
```

```python
import functools
import math

import jax
import jax.numpy as jnp
from jax import lax
from jax.experimental import pallas as pl
from jax.experimental.pallas import tpu as pltpu
from jax.sharding import PartitionSpec as P

KW = 128
NMAT = 8
DEG = 4
LANES = 128
HALF = 64
SEGS = 16
HY = 7
HB = 8


def lanes_for(sleepers):
    return -(-(3 * sleepers + 3 * NMAT) // LANES) * LANES


def two_parts(values):
    high = values.astype(jnp.bfloat16)
    low = (values - high.astype(jnp.float32)).astype(jnp.bfloat16)
    return high, low


def dot(a, b):
    return lax.dot_general(a, b, (((1,), (0,)), ((), ())), preferred_element_type=jnp.float32)


def dot_t(a, b):
    return lax.dot_general(a, b, (((1,), (1,)), ((), ())), preferred_element_type=jnp.float32)


def table_kernel(sleepers, count, start, table, cells, positions, tw, tc, vectors):
    width = tc.shape[0] // 2
    lane = lax.broadcasted_iota(jnp.int32, (8, LANES), 1)
    wave = lane % HALF
    live = wave < count
    wave = wave + start[0]
    q = (2.0 * jnp.sin(wave.astype(jnp.float32) * (math.pi / KW))) ** 2
    lowest = highest = None
    for m in range(NMAT):
        s, xx, yy, zz, xy, xz, yz = (jnp.full((8, LANES), table[m, f]) for f in range(7))
        xy, xz, yz = jnp.abs(xy), jnp.abs(xz), jnp.abs(yz)
        sums = (xy + xz, xy + yz, xz + yz)
        low = s + q * functools.reduce(jnp.minimum, [d - r for d, r in zip((xx, yy, zz), sums)])
        high = s + q * functools.reduce(jnp.maximum, [d + r for d, r in zip((xx, yy, zz), sums)])
        lowest = low if m == 0 else jnp.minimum(lowest, low)
        highest = high if m == 0 else jnp.maximum(highest, high)
    highest = 8.0 + highest
    center = 0.5 * (highest + lowest)
    half_width = 0.5 * (highest - lowest)
    ratio2 = (center / half_width) ** 2
    top = 8.0 * ratio2 * (ratio2 - 1.0) + 1.0
    h2 = half_width * half_width
    h4 = h2 * h2
    scale = 8.0 / (top * h4)
    scale = jnp.where(live, scale * scale, 0.0)
    twice = h2 * jnp.sqrt(0.5 * (top + 1.0))
    shift = 0.5 * jnp.sqrt(twice + h2)
    tilt = 0.5 * jnp.sqrt(jnp.maximum(twice - h2, 0.0))
    for n, vector in enumerate((shift, tilt, jnp.sqrt(lowest * highest), center)):
        vectors[n, :, :] = jnp.where(live, vector, 0.0)

    tc[...] = jnp.zeros(tc.shape, jnp.bfloat16)
    tw[...] = jnp.zeros(tw.shape, jnp.bfloat16)
    column = [jnp.broadcast_to(cells[:, f : f + 1], (8, LANES)) for f in range(8)]
    fields = [center - 4.0 - column[0] - q * column[c] for c in (1, 2, 3)]
    fields += [-q * column[c] for c in (4, 5, 6)] + [q * column[7]]
    rounded = lambda values: values.astype(jnp.bfloat16).astype(jnp.float32)
    for f, field in enumerate(fields):
        field = jnp.where(live, field, 0.0)
        first = rounded(field)
        second = rounded(field - first)
        third = field - first - second
        rows = jnp.concatenate([first, second, third, jnp.zeros_like(first)], axis=0)
        lanes = lax.broadcasted_iota(jnp.int32, rows.shape, 1)
        for half in range(2):
            kept = jnp.where(lanes // HALF == half, rows, 0.0).astype(jnp.bfloat16)
            at = half * width + 3 * sleepers
            tc[at : at + 32, f * LANES : (f + 1) * LANES] = kept

    turns = (positions[...] * wave[:1]) & (KW - 1)
    angles = turns.astype(jnp.float32) * (2.0 * math.pi / KW)
    lanes = lax.broadcasted_iota(jnp.int32, turns.shape, 1)
    for part, phase in enumerate((jnp.cos(angles), -jnp.sin(angles))):
        phase = phase * scale[:1]
        high = rounded(phase)
        for segment, values in enumerate((high, high, phase - high)):
            for half in range(2):
                kept = jnp.where(lanes // HALF == half, values, 0.0).astype(jnp.bfloat16)
                for c in range(3):
                    at = (2 * segment + half) * width + c * sleepers
                    to = (2 * c + part) * LANES
                    tw[at : at + sleepers, to : to + LANES] = kept


def tables(positions, material_table, start, count, width):
    sleepers = positions.shape[0]
    spots = jnp.broadcast_to(positions[:, None], (sleepers, LANES))
    return pl.pallas_call(
        functools.partial(table_kernel, sleepers, count),
        out_shape=(
            jax.ShapeDtypeStruct((6 * width, 6 * LANES), jnp.bfloat16),
            jax.ShapeDtypeStruct((2 * width, 8 * LANES), jnp.bfloat16),
            jax.ShapeDtypeStruct((4, 8, LANES), jnp.float32),
        ),
        in_specs=[pl.BlockSpec(memory_space=pltpu.SMEM)] * 2
        + [pl.BlockSpec(memory_space=pltpu.VMEM)] * 2,
        out_specs=(pl.BlockSpec(memory_space=pltpu.VMEM),) * 3,
        compiler_params=pltpu.CompilerParams(vmem_limit_bytes=32 * 1024 * 1024),
        name="tables",
    )(start.reshape(1), material_table, material_table, spots)


def row_values(planes, row, height, sleepers, width):
    depth = planes.shape[1]
    parts = [planes[pl.ds(c * height + row, sleepers, stride=3 * height), :] for c in range(3)]
    material = planes[pl.ds(3 * sleepers * height + row, 1), :]
    number = lax.broadcasted_iota(jnp.int32, (width - 3 * sleepers, depth), 0)
    kind = jnp.where(number < 3 * NMAT, number % NMAT, -1).astype(jnp.float32)
    parts.append((kind == material).astype(jnp.float32))
    return jnp.concatenate(parts, axis=0)


def gather(spots, flags, pieces, planes, sems):
    copies = []
    for n, (piece, first, count, plane, row, target) in enumerate(spots):
        src = pieces[piece]
        if isinstance(target, tuple):
            target = pl.multiple_of(jnp.where(flags[2] == 1, target[1], target[0]), 8)
        copies.append(
            pltpu.make_async_copy(
                src.at[plane : plane + count, row[0] : row[0] + row[1], :],
                planes.at[first : first + count, pl.ds(target, row[1]), :],
                sems.at[n],
            )
        )
    for copy in copies:
        copy.start()
    for copy in copies:
        copy.wait()


def edge_kernel(sleepers, spots, *refs):
    flags, *pieces, out, planes, sems = refs
    gather(spots, flags, pieces, planes, sems)
    height, depth = planes.shape[1:]
    width = out.shape[2]
    spot = lax.broadcasted_iota(jnp.int32, (2 * HB, depth), 0)
    at = lax.broadcasted_iota(jnp.int32, (2 * HB, depth), 1)
    pick = (at == jnp.where(spot < HB, spot, spot + (depth - 2 * HB))).astype(jnp.bfloat16)
    flat = planes.reshape(planes.shape[0] * height, depth)

    def some_rows(block, carry):
        for line in range(8):
            row = 8 * block + line
            high, low = two_parts(row_values(flat, row, height, sleepers, width))
            out[row, :, :] = dot_t(pick, high) + dot_t(pick, low)
        return carry

    lax.fori_loop(0, height // 8, some_rows, 0)


def edges_of(spots, flags, pieces, sleepers, height, depth):
    return pl.pallas_call(
        functools.partial(edge_kernel, sleepers, spots),
        out_shape=jax.ShapeDtypeStruct((height, 2 * HB, lanes_for(sleepers)), jnp.float32),
        in_specs=[pl.BlockSpec(memory_space=pltpu.SMEM)]
        + [pl.BlockSpec(memory_space=pl.ANY)] * len(pieces),
        out_specs=pl.BlockSpec(memory_space=pltpu.VMEM),
        scratch_shapes=[
            pltpu.VMEM((3 * sleepers + 1, height, depth), jnp.float32),
            pltpu.SemaphoreType.DMA((len(spots),)),
        ],
        compiler_params=pltpu.CompilerParams(vmem_limit_bytes=32 * 1024 * 1024),
        name="edge_columns",
    )(flags, *pieces)


def field_kernel(sleepers, count, seglen, spots, scratch, *refs):
    pl.run_scoped(functools.partial(field_body, sleepers, count, seglen, spots, refs), *scratch)


def field_body(sleepers, count, seglen, spots, refs, *scratch):
    flags, inside, across, tw, tc, vectors, edge, *pieces, out = refs
    planes, sems, source, ghosts, coefs, made, lhs, lay, *rings = scratch[:14]
    turn, pages, page_sems = scratch[14:]
    height, depth = planes.shape[1:]
    flat = planes.reshape(planes.shape[0] * height, depth)
    ny = height - 2 * HB
    width = inside.shape[2]
    chunks = width // LANES
    cells = 8 * seglen
    page_rows = pages.reshape(2 * count * 48, depth)
    lane = lax.broadcasted_iota(jnp.int32, (8, LANES), 1)
    sub = lax.broadcasted_iota(jnp.int32, (8, LANES), 0)

    def at(zm):
        return pl.ds(8 * (zm + 1), 8)

    def around(first, last):
        before = pltpu.roll(last, 1, 0)
        after = pltpu.roll(first, 7, 0)
        return (
            jnp.where(sub == 0, pltpu.roll(before, HALF, 1), before),
            jnp.where(sub == 7, pltpu.roll(after, HALF, 1), after),
        )

    def line_at(row, zm):
        return pl.ds(pl.multiple_of((row & 15) * cells, 8) + 8 * zm, 8)

    def column(q):
        part, c = divmod(q, 3)
        return slice((2 * c + part) * LANES, (2 * c + part + 1) * LANES)

    def read_source(row, q, zm):
        if zm == -1:
            return ghosts[row & 3, q, :8, :]
        if zm == seglen:
            return ghosts[row & 3, q, 8:, :]
        rows = pl.ds(pl.multiple_of((row & 3) * cells, 8) + 8 * zm, 8)
        return source[rows, column(q)]

    def reader(ring):
        def read(row, q, zm):
            outside = ((row < HY) & (flags[0] == 1)) | ((row >= HY + ny) & (flags[1] == 1))
            return ring[jnp.where(outside, 4, row & 3), q, at(zm), :]

        return read

    def produce(pair):
        def lay_out(k):
            srow = jnp.clip(2 * pair - 2 + k + (HB - HY), 0, height - 1)
            values = row_values(flat, srow, height, sleepers, width)
            odd = flags[3] == 1
            for n in range(chunks):
                span = slice(n * LANES, (n + 1) * LANES)
                lay[k * chunks + n, HB : HB + depth, :] = jnp.transpose(values[span])
                first, second = inside[srow, :, span], across[srow, :, span]
                lay[k * chunks + n, :HB, :] = jnp.where(odd, first, second)
                lay[k * chunks + n, HB + depth :, :] = jnp.where(odd, second, first)

        def split():
            halves = [[], []]
            for k in range(2):
                for half in range(2):
                    for zm in range(seglen):
                        spot = pl.ds(half * cells + zm, 8, stride=seglen)
                        pieces_at = [lay[k * chunks + n, spot, :] for n in range(chunks)]
                        halves[half].append(jnp.concatenate(pieces_at, axis=1))
            values = jnp.concatenate(
                [jnp.concatenate(half, axis=0) for half in halves], axis=1
            )
            high, low = two_parts(values)
            lhs[:, : 2 * width] = high
            lhs[:, 2 * width : 4 * width] = low
            lhs[:, 4 * width :] = high

        first_row = 2 * pair - 2
        target = pl.ds(pl.multiple_of((first_row & 3) * cells, 8), 2 * cells)

        def spectrum(c):
            span = slice(2 * c * LANES, 2 * (c + 1) * LANES)
            source[target, span] = dot(lhs[...], tw[:, span])

        def fields(f):
            span = slice(f * LANES, (f + 2) * LANES)
            made[:, span] = dot(lhs[:, : 2 * width], tc[:, span])

        def wrap(k):
            row = first_row + k
            for q in range(6):
                ghosts[row & 3, q, :8, :], ghosts[row & 3, q, 8:, :] = around(
                    read_source(row, q, 0), read_source(row, q, seglen - 1)
                )

        return (
            [functools.partial(lay_out, 0), functools.partial(lay_out, 1), split],
            [functools.partial(spectrum, c) for c in range(3)]
            + [functools.partial(fields, f) for f in range(0, 8, 2)]
            + [functools.partial(wrap, k) for k in range(2)],
        )

    def commit(pair):
        def move(k, zm):
            rows = slice(k * cells + 8 * zm, k * cells + 8 * zm + 8)
            for n in range(7):
                span = slice(n * LANES, (n + 1) * LANES)
                coefs[line_at(2 * pair - 2 + k, zm), span] = made[rows, span]

        return [functools.partial(move, k, zm) for k in range(2) for zm in range(seglen)]

    def apply(src, row, emit, shift=None, tilt=None):
        cur = [[src(row + k, q, 0) for q in range(6)] for k in range(2)]
        behind = [
            [src(row + k, q, -1) + (cur[1][q] if k == 0 else src(row + 2, q, 0)) for q in range(6)]
            for k in range(2)
        ]
        for zm in range(seglen):
            nxt = [[src(row + k, q, zm + 1) for q in range(6)] for k in range(2)]
            ahead = [
                [src(row - 1, q, zm) + nxt[0][q] for q in range(6)],
                [cur[0][q] + nxt[1][q] for q in range(6)],
            ]
            if zm + 1 < seglen:
                below = [cur[1][q] + src(row + 2, q, zm + 1) for q in range(6)]
            for k in range(2):
                f = [
                    coefs[line_at(row + k, zm), n * LANES : (n + 1) * LANES] for n in range(7)
                ]
                diagonal, damping = f[:3], f[6]
                if shift is not None:
                    diagonal = [d + shift for d in diagonal]
                if tilt is not None:
                    damping = damping - tilt
                matrix = (
                    (diagonal[0], f[3], f[4]),
                    (f[3], diagonal[1], f[5]),
                    (f[4], f[5], diagonal[2]),
                )
                results = []
                for q in range(6):
                    part, c = divmod(q, 3)
                    mine = cur[k][3 * part : 3 * part + 3]
                    own = matrix[c][0] * mine[0] + matrix[c][1] * mine[1] + matrix[c][2] * mine[2]
                    damp = damping * cur[k][3 * (1 - part) + c]
                    total = (ahead[k][q] + behind[k][q]) + own
                    total = total + damp if part == 0 else total - damp
                    results.append(total)
                emit(k, zm, results)
            if zm + 1 < seglen:
                behind = [ahead[1], below]
            cur = nxt

    def stage(src, dst, row, shift, tilt, between=None):
        ends = {}

        def emit(k, zm, results):
            if zm == HB - 1:
                results = [value * edge[0] for value in results]
            if zm == (HB + depth) % seglen:
                results = [value * edge[1] for value in results]
            slot = (row + k) & 3
            for q in range(6):
                dst[slot, q, at(zm), :] = results[q]
            if zm in (0, seglen - 1):
                ends[k, zm] = results
            if zm == seglen - 1:
                for q in range(6):
                    dst[slot, q, at(-1), :], dst[slot, q, at(seglen), :] = around(
                        ends[k, 0][q], results[q]
                    )
            if between is not None:
                between()

        apply(src, row, emit, shift, tilt)

    def last_stage(row, between=None):
        def emit(k, zm, results):
            for c in range(3):
                real, imag = results[c], results[3 + c]
                first = jnp.where(lane < HALF, real, pltpu.roll(imag, HALF, 1))
                second = jnp.where(lane < HALF, pltpu.roll(real, HALF, 1), imag)
                turn[3 * k + c, pl.ds(zm, 8, stride=seglen), :] = first
                turn[3 * k + c, pl.ds(cells + zm, 8, stride=seglen), :] = second
            if between is not None:
                between()

        apply(reader(rings[5]), row, emit, shift=vectors[3])

    def run_stage(t, base, between=None):
        shift = (1, 1, -1, -1, 0, 0)[t - 1]
        shift = shift * vectors[0] if shift else None
        tilt = (vectors[1] if t <= 4 else vectors[2]) * (1 if t % 2 else -1)
        src = read_source if t == 1 else reader(rings[t - 2])
        stage(src, rings[t - 1], base - t, shift, tilt, between)

    def spread(tasks, slots):
        total, seen, left_over = len(tasks), [0], list(tasks)

        def between():
            seen[0] += 1
            while left_over and (total - len(left_over)) * slots < seen[0] * total:
                left_over.pop(0)()

        return between

    def mixed(first, second):
        tasks = []
        for n in range(max(len(first), len(second))):
            tasks += first[n : n + 1] + second[n : n + 1]
        return tasks

    def finish(pair):
        done = pair - HB
        block = done >> 2
        start = pl.multiple_of((block & 1) * (count * 48), 8) + 2 * (done & 3)

        def page(k, c):
            turned = jnp.transpose(turn[3 * k + c, HB : HB + depth, :])
            for part in range(2):
                rows = pl.ds(start + (part * 3 + c) * 8 + k, count, stride=48)
                page_rows[rows, :] = turned[part * HALF : part * HALF + count]

        return [functools.partial(page, k, c) for k in range(2) for c in range(3)]

    def page_copy(block):
        return pltpu.make_async_copy(
            pages.at[block & 1],
            out.at[:, :, :, pl.ds(pl.multiple_of(8 * block, 8), 8), :],
            page_sems.at[block & 1],
        )

    def ramp(pair, carry):
        base = 2 * pair - 2
        early, late = produce(pair + 1)
        for t, tasks in ((1, early), (2, late)):

            @pl.when(base >= 2 * t)
            def _():
                run_stage(t, base, spread(tasks, 2 * seglen))

            @pl.when(base < 2 * t)
            def _():
                for task in tasks:
                    task()

        for t in range(3, 7):

            @pl.when(base >= 2 * t)
            def _():
                run_stage(t, base)

        @pl.when(base >= 14)
        def _():
            last_stage(base - 7)

        for task in commit(pair + 1):
            task()
        return carry

    def steady(pair, carry):
        base = 2 * pair - 2
        done = pair - 1 - HB

        @pl.when(((done & 3) == 0) & (done >= 8))
        def _():
            page_copy((done >> 2) - 2).wait()

        early, late = produce(pair + 1)
        turning = finish(pair - 1)
        run_stage(1, base, spread(mixed(early, turning[:2]), 2 * seglen))
        between = spread(mixed(late, turning[2:]), 10 * seglen)
        for t in range(2, 7):
            run_stage(t, base, between)
        last_stage(base - 7, spread(commit(pair + 1), 2 * seglen))

        @pl.when((done & 3) == 3)
        def _():
            page_copy(done >> 2).start()

        return carry

    gather(spots, flags, pieces, planes, sems)
    for ring in rings:
        for q in range(6):
            ring[4, q, :, :] = jnp.zeros(ring.shape[2:], jnp.float32)
    early, late = produce(0)
    for task in early + late + commit(0):
        task()
    final = HB + ny // 2 - 1
    lax.fori_loop(0, HB + 1, ramp, 0)
    lax.fori_loop(HB + 1, final + 1, steady, 0)
    for step in finish(final):
        step()
    blocks = ny // 8
    page_copy(blocks - 1).start()
    for block in range(max(blocks - 2, 0), blocks):
        page_copy(block).wait()


def solve_field(spots, pieces, flags, inside, across, tw, tc, vectors, edge, sleepers, count):
    height, _, width = inside.shape
    depth = pieces[0].shape[2]
    ny = height - 2 * HB
    seglen = (depth + 2 * HB) // SEGS
    cells = 8 * seglen
    chunks = width // LANES
    ring = pltpu.VMEM((5, 6, 8 * (seglen + 2), LANES), jnp.float32)
    whole = pl.BlockSpec(memory_space=pltpu.VMEM)
    scratch = (
        pltpu.VMEM((3 * sleepers + 1, height, depth), jnp.float32),
        pltpu.SemaphoreType.DMA((len(spots),)),
        pltpu.VMEM((4 * cells, 6 * LANES), jnp.float32),
        pltpu.VMEM((4, 6, 16, LANES), jnp.float32),
        pltpu.VMEM((16 * cells, 7 * LANES), jnp.float32),
        pltpu.VMEM((2 * cells, 8 * LANES), jnp.float32),
        pltpu.VMEM((2 * cells, 6 * width), jnp.bfloat16),
        pltpu.VMEM((2 * chunks, 2 * cells, LANES), jnp.float32),
        ring, ring, ring, ring, ring, ring,
        pltpu.VMEM((6, 2 * cells, LANES), jnp.float32),
        pltpu.VMEM((2, count, 2, 3, 8, depth), jnp.float32),
        pltpu.SemaphoreType.DMA((2,)),
    )
    return pl.pallas_call(
        functools.partial(field_kernel, sleepers, count, seglen, spots, scratch),
        out_shape=jax.ShapeDtypeStruct((count, 2, 3, ny, depth), jnp.float32),
        in_specs=[pl.BlockSpec(memory_space=pltpu.SMEM)]
        + [whole] * 6
        + [pl.BlockSpec(memory_space=pl.ANY)] * len(pieces),
        out_specs=pl.BlockSpec(memory_space=pl.ANY),
        compiler_params=pltpu.CompilerParams(vmem_limit_bytes=40 * 1024 * 1024),
        name="adjoint_field",
    )(flags, inside, across, tw, tc, vectors, edge, *pieces)


def local(loads, sleeper_pos, material, material_table):
    ka = lax.axis_size("ka")
    gy, gz = lax.axis_size("gy"), lax.axis_size("gz")
    count = KW // ka
    wave_start = lax.axis_index("ka") * count
    sleepers = ka * loads.shape[0]
    own = 3 * loads.shape[0]
    ny, depth = material.shape
    height = ny + 2 * HB
    loads = loads.reshape(own, ny, depth)
    material = material.astype(jnp.float32)[None]

    def swap(array, axis, size, first):
        pairs = [(i, i + 1) for i in range(first, size - 1, 2)]
        return lax.ppermute(array, axis, pairs + [(high, low) for low, high in pairs])

    y_at, z_at = lax.axis_index("gy"), lax.axis_index("gz")
    y_odd, z_odd = y_at % 2 == 1, z_at % 2 == 1
    turns = [[(i, (i + step) % ka) for i in range(ka)] for step in range(1, ka)]
    ends = jnp.concatenate([loads[:, :HB], loads[:, ny - HB :]], axis=1)
    ends, sleeper_pos = lax.optimization_barrier((ends, sleeper_pos))
    got_ends = [lax.ppermute(ends, "ka", turn) for turn in turns]
    all_pos = [sleeper_pos] + [lax.ppermute(sleeper_pos, "ka", turn) for turn in turns]
    met, tied = lax.optimization_barrier((all_pos, loads))
    low = jnp.concatenate([tied[:, :HB], material[:, :HB]], axis=0)
    high = jnp.concatenate([tied[:, ny - HB :], material[:, ny - HB :]], axis=0)
    halos = (
        swap(jnp.where(y_odd, low, high), "gy", gy, 0),
        swap(jnp.where(y_odd, high, low), "gy", gy, 1),
    )
    inner, got_ends = lax.optimization_barrier((loads[:, HB : ny - HB], got_ends))
    got_inner = [lax.ppermute(inner, "ka", turn) for turn in turns]

    pieces, spots = [], []
    sides = ((HB + ny, 0), (0, HB + ny))

    def place(array, *where):
        pieces.append(array)
        spots.extend((len(pieces) - 1, *spot) for spot in where)

    def place_middle(first, outer, middle):
        place(outer, (first, own, 0, (0, HB), HB), (first, own, 0, (HB, HB), ny))
        place(middle, (first, own, 0, (0, ny - 2 * HB), 2 * HB))

    place_middle(0, ends, inner)
    place(material, (3 * sleepers, 1, 0, (0, ny), HB))
    for array, row in zip(halos, sides):
        place(array, (0, own, 0, (0, HB), row), (3 * sleepers, 1, own, (0, HB), row))
    for step, (outer, middle) in enumerate(zip(got_ends, got_inner), 1):
        place_middle(own * step, outer, middle)
        low, high = outer[:, :HB], outer[:, HB:]
        far = (
            swap(jnp.where(y_odd, low, high), "gy", gy, 0),
            swap(jnp.where(y_odd, high, low), "gy", gy, 1),
        )
        for array, row in zip(far, sides):
            place(array, (own * step, own, 0, (0, HB), row))

    met, _ = lax.optimization_barrier((met, got_ends))
    tw, tc, vectors = tables(
        jnp.concatenate(met), material_table, wave_start, count, lanes_for(sleepers)
    )
    flags = jnp.stack([y_at == 0, y_at == gy - 1, y_odd, z_odd]).astype(jnp.int32)
    sub = jnp.arange(8)[:, None]
    lane = jnp.arange(LANES)[None, :]
    edge = jnp.stack(
        [
            jnp.where((z_at == 0) & (sub == 0) & (lane < HALF), 0.0, 1.0),
            jnp.where((z_at == gz - 1) & (sub == 7) & (lane >= HALF), 0.0, 1.0),
        ]
    ).astype(jnp.float32)
    pieces[-1], flags, edge = lax.optimization_barrier((pieces[-1], flags, edge))

    columns = edges_of(spots, flags, pieces, sleepers, height, depth)
    low, high = columns[:, :HB], columns[:, HB:]
    inside = swap(jnp.where(z_odd, low, high), "gz", gz, 0)
    across = swap(jnp.where(z_odd, high, low), "gz", gz, 1)
    return solve_field(
        spots, pieces, flags, inside, across, tw, tc, vectors, edge, sleepers, count
    )


def solution(mesh):
    return jax.shard_map(
        local,
        mesh=mesh,
        in_specs=(P("ka", None, "gy", "gz"), P("ka"), P("gy", "gz"), P()),
        out_specs=P("ka", None, None, "gy", "gz"),
        check_vma=False,
    )
```

```python
import functools
import math

import jax
import jax.numpy as jnp
from jax import lax
from jax.experimental import pallas as pl
from jax.experimental.pallas import tpu as pltpu
from jax.sharding import PartitionSpec as P

KW = 128
NMAT = 8
DEG = 4
LANES = 128
HALF = 64
SEGS = 16
HY = 7
HB = 8


def lanes_for(sleepers):
    return -(-(3 * sleepers + 3 * NMAT) // LANES) * LANES


def two_parts(values):
    high = values.astype(jnp.bfloat16)
    low = (values - high.astype(jnp.float32)).astype(jnp.bfloat16)
    return high, low


def dot(a, b):
    return lax.dot_general(a, b, (((1,), (0,)), ((), ())), preferred_element_type=jnp.float32)


def dot_t(a, b):
    return lax.dot_general(a, b, (((1,), (1,)), ((), ())), preferred_element_type=jnp.float32)


def table_kernel(sleepers, count, start, table, cells, positions, tw, tc, vectors):
    width = tc.shape[0] // 2
    lane = lax.broadcasted_iota(jnp.int32, (8, LANES), 1)
    wave = lane % HALF
    live = wave < count
    wave = wave + start[0]
    q = (2.0 * jnp.sin(wave.astype(jnp.float32) * (math.pi / KW))) ** 2
    lowest = highest = None
    for m in range(NMAT):
        s, xx, yy, zz, xy, xz, yz = (jnp.full((8, LANES), table[m, f]) for f in range(7))
        xy, xz, yz = jnp.abs(xy), jnp.abs(xz), jnp.abs(yz)
        sums = (xy + xz, xy + yz, xz + yz)
        low = s + q * functools.reduce(jnp.minimum, [d - r for d, r in zip((xx, yy, zz), sums)])
        high = s + q * functools.reduce(jnp.maximum, [d + r for d, r in zip((xx, yy, zz), sums)])
        lowest = low if m == 0 else jnp.minimum(lowest, low)
        highest = high if m == 0 else jnp.maximum(highest, high)
    highest = 8.0 + highest
    center = 0.5 * (highest + lowest)
    half_width = 0.5 * (highest - lowest)
    ratio2 = (center / half_width) ** 2
    top = 8.0 * ratio2 * (ratio2 - 1.0) + 1.0
    h2 = half_width * half_width
    h4 = h2 * h2
    scale = 8.0 / (top * h4)
    scale = jnp.where(live, scale * scale, 0.0)
    twice = h2 * jnp.sqrt(0.5 * (top + 1.0))
    shift = 0.5 * jnp.sqrt(twice + h2)
    tilt = 0.5 * jnp.sqrt(jnp.maximum(twice - h2, 0.0))
    for n, vector in enumerate((shift, tilt, jnp.sqrt(lowest * highest), center)):
        vectors[n, :, :] = jnp.where(live, vector, 0.0)

    tc[...] = jnp.zeros(tc.shape, jnp.bfloat16)
    tw[...] = jnp.zeros(tw.shape, jnp.bfloat16)
    column = [jnp.broadcast_to(cells[:, f : f + 1], (8, LANES)) for f in range(8)]
    fields = [center - 4.0 - column[0] - q * column[c] for c in (1, 2, 3)]
    fields += [-q * column[c] for c in (4, 5, 6)] + [q * column[7]]
    rounded = lambda values: values.astype(jnp.bfloat16).astype(jnp.float32)
    for f, field in enumerate(fields):
        field = jnp.where(live, field, 0.0)
        first = rounded(field)
        second = rounded(field - first)
        third = field - first - second
        rows = jnp.concatenate([first, second, third, jnp.zeros_like(first)], axis=0)
        lanes = lax.broadcasted_iota(jnp.int32, rows.shape, 1)
        for half in range(2):
            kept = jnp.where(lanes // HALF == half, rows, 0.0).astype(jnp.bfloat16)
            at = half * width + 3 * sleepers
            tc[at : at + 32, f * LANES : (f + 1) * LANES] = kept

    turns = (positions[...] * wave[:1]) & (KW - 1)
    angles = turns.astype(jnp.float32) * (2.0 * math.pi / KW)
    lanes = lax.broadcasted_iota(jnp.int32, turns.shape, 1)
    for part, phase in enumerate((jnp.cos(angles), -jnp.sin(angles))):
        phase = phase * scale[:1]
        high = rounded(phase)
        for segment, values in enumerate((high, high, phase - high)):
            for half in range(2):
                kept = jnp.where(lanes // HALF == half, values, 0.0).astype(jnp.bfloat16)
                for c in range(3):
                    at = (2 * segment + half) * width + c * sleepers
                    to = (2 * c + part) * LANES
                    tw[at : at + sleepers, to : to + LANES] = kept


def tables(positions, material_table, start, count, width):
    sleepers = positions.shape[0]
    spots = jnp.broadcast_to(positions[:, None], (sleepers, LANES))
    return pl.pallas_call(
        functools.partial(table_kernel, sleepers, count),
        out_shape=(
            jax.ShapeDtypeStruct((6 * width, 6 * LANES), jnp.bfloat16),
            jax.ShapeDtypeStruct((2 * width, 8 * LANES), jnp.bfloat16),
            jax.ShapeDtypeStruct((4, 8, LANES), jnp.float32),
        ),
        in_specs=[pl.BlockSpec(memory_space=pltpu.SMEM)] * 2
        + [pl.BlockSpec(memory_space=pltpu.VMEM)] * 2,
        out_specs=(pl.BlockSpec(memory_space=pltpu.VMEM),) * 3,
        compiler_params=pltpu.CompilerParams(vmem_limit_bytes=32 * 1024 * 1024),
        name="tables",
    )(start.reshape(1), material_table, material_table, spots)


def row_values(planes, row, height, sleepers, width):
    depth = planes.shape[1]
    parts = [planes[pl.ds(c * height + row, sleepers, stride=3 * height), :] for c in range(3)]
    material = planes[pl.ds(3 * sleepers * height + row, 1), :]
    number = lax.broadcasted_iota(jnp.int32, (width - 3 * sleepers, depth), 0)
    kind = jnp.where(number < 3 * NMAT, number % NMAT, -1).astype(jnp.float32)
    parts.append((kind == material).astype(jnp.float32))
    return jnp.concatenate(parts, axis=0)


def gather(spots, flags, pieces, planes, sems):
    copies = []
    for n, (piece, first, count, plane, row, target) in enumerate(spots):
        src = pieces[piece]
        if isinstance(target, tuple):
            target = pl.multiple_of(jnp.where(flags[2] == 1, target[1], target[0]), 8)
        copies.append(
            pltpu.make_async_copy(
                src.at[plane : plane + count, row[0] : row[0] + row[1], :],
                planes.at[first : first + count, pl.ds(target, row[1]), :],
                sems.at[n],
            )
        )
    for copy in copies:
        copy.start()
    for copy in copies:
        copy.wait()


def edge_kernel(sleepers, spots, *refs):
    flags, *pieces, out, planes, sems = refs
    gather(spots, flags, pieces, planes, sems)
    height, depth = planes.shape[1:]
    width = out.shape[2]
    strip = 2 * HB
    flat = planes.reshape(planes.shape[0] * height, depth)
    group = lax.broadcasted_iota(jnp.int32, (width, depth), 1) // strip

    def eight_rows(block, carry):
        packed = None
        for line in range(8):
            values = row_values(flat, 8 * block + line, height, sleepers, width)
            moved = pltpu.roll(values, strip * line + HB, 1)
            packed = moved if line == 0 else jnp.where(group == line, moved, packed)
        for n in range(width // LANES):
            span = slice(n * LANES, (n + 1) * LANES)
            turned = jnp.transpose(packed[span])
            for line in range(8):
                out[8 * block + line, :, span] = turned[line * strip : (line + 1) * strip]
        return carry

    lax.fori_loop(0, height // 8, eight_rows, 0)


def edges_of(spots, flags, pieces, sleepers, height, depth):
    return pl.pallas_call(
        functools.partial(edge_kernel, sleepers, spots),
        out_shape=jax.ShapeDtypeStruct((height, 2 * HB, lanes_for(sleepers)), jnp.float32),
        in_specs=[pl.BlockSpec(memory_space=pltpu.SMEM)]
        + [pl.BlockSpec(memory_space=pl.ANY)] * len(pieces),
        out_specs=pl.BlockSpec(memory_space=pltpu.VMEM),
        scratch_shapes=[
            pltpu.VMEM((3 * sleepers + 1, height, depth), jnp.float32),
            pltpu.SemaphoreType.DMA((len(spots),)),
        ],
        compiler_params=pltpu.CompilerParams(vmem_limit_bytes=32 * 1024 * 1024),
        name="edge_columns",
    )(flags, *pieces)


def field_kernel(sleepers, count, seglen, spots, scratch, *refs):
    pl.run_scoped(functools.partial(field_body, sleepers, count, seglen, spots, refs), *scratch)


def field_body(sleepers, count, seglen, spots, refs, *scratch):
    flags, inside, across, tw, tc, vectors, edge, *pieces, out = refs
    planes, sems, source, ghosts, coefs, made, lhs, lay, *rings = scratch[:14]
    turn, pages, page_sems = scratch[14:]
    height, depth = planes.shape[1:]
    flat = planes.reshape(planes.shape[0] * height, depth)
    ny = height - 2 * HB
    width = inside.shape[2]
    chunks = width // LANES
    cells = 8 * seglen
    page_rows = pages.reshape(2 * count * 48, depth)
    lane = lax.broadcasted_iota(jnp.int32, (8, LANES), 1)
    sub = lax.broadcasted_iota(jnp.int32, (8, LANES), 0)

    def at(zm):
        return pl.ds(8 * (zm + 1), 8)

    def around(first, last):
        before = pltpu.roll(last, 1, 0)
        after = pltpu.roll(first, 7, 0)
        return (
            jnp.where(sub == 0, pltpu.roll(before, HALF, 1), before),
            jnp.where(sub == 7, pltpu.roll(after, HALF, 1), after),
        )

    def line_at(row, zm):
        return pl.ds(pl.multiple_of((row & 15) * cells, 8) + 8 * zm, 8)

    def column(q):
        part, c = divmod(q, 3)
        return slice((2 * c + part) * LANES, (2 * c + part + 1) * LANES)

    def read_source(row, q, zm):
        if zm == -1:
            return ghosts[row & 3, q, :8, :]
        if zm == seglen:
            return ghosts[row & 3, q, 8:, :]
        rows = pl.ds(pl.multiple_of((row & 3) * cells, 8) + 8 * zm, 8)
        return source[rows, column(q)]

    def reader(ring):
        def read(row, q, zm):
            outside = ((row < HY) & (flags[0] == 1)) | ((row >= HY + ny) & (flags[1] == 1))
            return ring[jnp.where(outside, 4, row & 3), q, at(zm), :]

        return read

    def produce(pair):
        def lay_out(k):
            srow = jnp.clip(2 * pair - 2 + k + (HB - HY), 0, height - 1)
            values = row_values(flat, srow, height, sleepers, width)
            odd = flags[3] == 1
            for n in range(chunks):
                span = slice(n * LANES, (n + 1) * LANES)
                lay[k * chunks + n, HB : HB + depth, :] = jnp.transpose(values[span])
                first, second = inside[srow, :, span], across[srow, :, span]
                lay[k * chunks + n, :HB, :] = jnp.where(odd, first, second)
                lay[k * chunks + n, HB + depth :, :] = jnp.where(odd, second, first)

        def split():
            halves = [[], []]
            for k in range(2):
                for half in range(2):
                    for zm in range(seglen):
                        spot = pl.ds(half * cells + zm, 8, stride=seglen)
                        pieces_at = [lay[k * chunks + n, spot, :] for n in range(chunks)]
                        halves[half].append(jnp.concatenate(pieces_at, axis=1))
            values = jnp.concatenate(
                [jnp.concatenate(half, axis=0) for half in halves], axis=1
            )
            high, low = two_parts(values)
            lhs[:, : 2 * width] = high
            lhs[:, 2 * width : 4 * width] = low
            lhs[:, 4 * width :] = high

        first_row = 2 * pair - 2
        target = pl.ds(pl.multiple_of((first_row & 3) * cells, 8), 2 * cells)

        def spectrum(c):
            span = slice(2 * c * LANES, 2 * (c + 1) * LANES)
            source[target, span] = dot(lhs[...], tw[:, span])

        def fields(f):
            span = slice(f * LANES, (f + 2) * LANES)
            made[:, span] = dot(lhs[:, : 2 * width], tc[:, span])

        def wrap(k):
            row = first_row + k
            for q in range(6):
                ghosts[row & 3, q, :8, :], ghosts[row & 3, q, 8:, :] = around(
                    read_source(row, q, 0), read_source(row, q, seglen - 1)
                )

        return (
            [functools.partial(lay_out, 0), functools.partial(lay_out, 1), split],
            [functools.partial(spectrum, c) for c in range(3)]
            + [functools.partial(fields, f) for f in range(0, 8, 2)]
            + [functools.partial(wrap, k) for k in range(2)],
        )

    def commit(pair):
        def move(k, zm):
            rows = slice(k * cells + 8 * zm, k * cells + 8 * zm + 8)
            for n in range(7):
                span = slice(n * LANES, (n + 1) * LANES)
                coefs[line_at(2 * pair - 2 + k, zm), span] = made[rows, span]

        return [functools.partial(move, k, zm) for k in range(2) for zm in range(seglen)]

    def apply(src, row, emit, shift=None, tilt=None):
        cur = [[src(row + k, q, 0) for q in range(6)] for k in range(2)]
        behind = [
            [src(row + k, q, -1) + (cur[1][q] if k == 0 else src(row + 2, q, 0)) for q in range(6)]
            for k in range(2)
        ]
        for zm in range(seglen):
            nxt = [[src(row + k, q, zm + 1) for q in range(6)] for k in range(2)]
            ahead = [
                [src(row - 1, q, zm) + nxt[0][q] for q in range(6)],
                [cur[0][q] + nxt[1][q] for q in range(6)],
            ]
            if zm + 1 < seglen:
                below = [cur[1][q] + src(row + 2, q, zm + 1) for q in range(6)]
            for k in range(2):
                f = [
                    coefs[line_at(row + k, zm), n * LANES : (n + 1) * LANES] for n in range(7)
                ]
                diagonal, damping = f[:3], f[6]
                if shift is not None:
                    diagonal = [d + shift for d in diagonal]
                if tilt is not None:
                    damping = damping - tilt
                matrix = (
                    (diagonal[0], f[3], f[4]),
                    (f[3], diagonal[1], f[5]),
                    (f[4], f[5], diagonal[2]),
                )
                results = []
                for q in range(6):
                    part, c = divmod(q, 3)
                    mine = cur[k][3 * part : 3 * part + 3]
                    own = matrix[c][0] * mine[0] + matrix[c][1] * mine[1] + matrix[c][2] * mine[2]
                    damp = damping * cur[k][3 * (1 - part) + c]
                    total = (ahead[k][q] + behind[k][q]) + own
                    total = total + damp if part == 0 else total - damp
                    results.append(total)
                emit(k, zm, results)
            if zm + 1 < seglen:
                behind = [ahead[1], below]
            cur = nxt

    def stage(src, dst, row, shift, tilt, between=None):
        ends = {}

        def emit(k, zm, results):
            if zm == HB - 1:
                results = [value * edge[0] for value in results]
            if zm == (HB + depth) % seglen:
                results = [value * edge[1] for value in results]
            slot = (row + k) & 3
            for q in range(6):
                dst[slot, q, at(zm), :] = results[q]
            if zm in (0, seglen - 1):
                ends[k, zm] = results
            if zm == seglen - 1:
                for q in range(6):
                    dst[slot, q, at(-1), :], dst[slot, q, at(seglen), :] = around(
                        ends[k, 0][q], results[q]
                    )
            if between is not None:
                between()

        apply(src, row, emit, shift, tilt)

    def last_stage(row, between=None):
        def emit(k, zm, results):
            for c in range(3):
                real, imag = results[c], results[3 + c]
                first = jnp.where(lane < HALF, real, pltpu.roll(imag, HALF, 1))
                second = jnp.where(lane < HALF, pltpu.roll(real, HALF, 1), imag)
                turn[3 * k + c, pl.ds(zm, 8, stride=seglen), :] = first
                turn[3 * k + c, pl.ds(cells + zm, 8, stride=seglen), :] = second
            if between is not None:
                between()

        apply(reader(rings[5]), row, emit, shift=vectors[3])

    def run_stage(t, base, between=None):
        shift = (1, 1, -1, -1, 0, 0)[t - 1]
        shift = shift * vectors[0] if shift else None
        tilt = (vectors[1] if t <= 4 else vectors[2]) * (1 if t % 2 else -1)
        src = read_source if t == 1 else reader(rings[t - 2])
        stage(src, rings[t - 1], base - t, shift, tilt, between)

    def spread(tasks, slots):
        total, seen, left_over = len(tasks), [0], list(tasks)

        def between():
            seen[0] += 1
            while left_over and (total - len(left_over)) * slots < seen[0] * total:
                left_over.pop(0)()

        return between

    def mixed(first, second):
        tasks = []
        for n in range(max(len(first), len(second))):
            tasks += first[n : n + 1] + second[n : n + 1]
        return tasks

    def finish(pair):
        done = pair - HB
        block = done >> 2
        start = pl.multiple_of((block & 1) * (count * 48), 8) + 2 * (done & 3)

        def page(k, c):
            turned = jnp.transpose(turn[3 * k + c, HB : HB + depth, :])
            for part in range(2):
                rows = pl.ds(start + (part * 3 + c) * 8 + k, count, stride=48)
                page_rows[rows, :] = turned[part * HALF : part * HALF + count]

        return [functools.partial(page, k, c) for k in range(2) for c in range(3)]

    def page_copy(block):
        return pltpu.make_async_copy(
            pages.at[block & 1],
            out.at[:, :, :, pl.ds(pl.multiple_of(8 * block, 8), 8), :],
            page_sems.at[block & 1],
        )

    def ramp(pair, carry):
        base = 2 * pair - 2
        early, late = produce(pair + 1)
        for t, tasks in ((1, early), (2, late)):

            @pl.when(base >= 2 * t)
            def _():
                run_stage(t, base, spread(tasks, 2 * seglen))

            @pl.when(base < 2 * t)
            def _():
                for task in tasks:
                    task()

        for t in range(3, 7):

            @pl.when(base >= 2 * t)
            def _():
                run_stage(t, base)

        @pl.when(base >= 14)
        def _():
            last_stage(base - 7)

        for task in commit(pair + 1):
            task()
        return carry

    def steady(pair, carry):
        base = 2 * pair - 2
        done = pair - 1 - HB

        @pl.when(((done & 3) == 0) & (done >= 8))
        def _():
            page_copy((done >> 2) - 2).wait()

        early, late = produce(pair + 1)
        turning = finish(pair - 1)
        run_stage(1, base, spread(mixed(early, turning[:2]), 2 * seglen))
        between = spread(mixed(late, turning[2:]), 10 * seglen)
        for t in range(2, 7):
            run_stage(t, base, between)
        last_stage(base - 7, spread(commit(pair + 1), 2 * seglen))

        @pl.when((done & 3) == 3)
        def _():
            page_copy(done >> 2).start()

        return carry

    gather(spots, flags, pieces, planes, sems)
    for ring in rings:
        for q in range(6):
            ring[4, q, :, :] = jnp.zeros(ring.shape[2:], jnp.float32)
    early, late = produce(0)
    for task in early + late + commit(0):
        task()
    final = HB + ny // 2 - 1
    lax.fori_loop(0, HB + 1, ramp, 0)
    lax.fori_loop(HB + 1, final + 1, steady, 0)
    for step in finish(final):
        step()
    blocks = ny // 8
    page_copy(blocks - 1).start()
    for block in range(max(blocks - 2, 0), blocks):
        page_copy(block).wait()


def solve_field(spots, pieces, flags, inside, across, tw, tc, vectors, edge, sleepers, count):
    height, _, width = inside.shape
    depth = pieces[0].shape[2]
    ny = height - 2 * HB
    seglen = (depth + 2 * HB) // SEGS
    cells = 8 * seglen
    chunks = width // LANES
    ring = pltpu.VMEM((5, 6, 8 * (seglen + 2), LANES), jnp.float32)
    whole = pl.BlockSpec(memory_space=pltpu.VMEM)
    scratch = (
        pltpu.VMEM((3 * sleepers + 1, height, depth), jnp.float32),
        pltpu.SemaphoreType.DMA((len(spots),)),
        pltpu.VMEM((4 * cells, 6 * LANES), jnp.float32),
        pltpu.VMEM((4, 6, 16, LANES), jnp.float32),
        pltpu.VMEM((16 * cells, 7 * LANES), jnp.float32),
        pltpu.VMEM((2 * cells, 8 * LANES), jnp.float32),
        pltpu.VMEM((2 * cells, 6 * width), jnp.bfloat16),
        pltpu.VMEM((2 * chunks, 2 * cells, LANES), jnp.float32),
        ring, ring, ring, ring, ring, ring,
        pltpu.VMEM((6, 2 * cells, LANES), jnp.float32),
        pltpu.VMEM((2, count, 2, 3, 8, depth), jnp.float32),
        pltpu.SemaphoreType.DMA((2,)),
    )
    return pl.pallas_call(
        functools.partial(field_kernel, sleepers, count, seglen, spots, scratch),
        out_shape=jax.ShapeDtypeStruct((count, 2, 3, ny, depth), jnp.float32),
        in_specs=[pl.BlockSpec(memory_space=pltpu.SMEM)]
        + [whole] * 6
        + [pl.BlockSpec(memory_space=pl.ANY)] * len(pieces),
        out_specs=pl.BlockSpec(memory_space=pl.ANY),
        compiler_params=pltpu.CompilerParams(vmem_limit_bytes=40 * 1024 * 1024),
        name="adjoint_field",
    )(flags, inside, across, tw, tc, vectors, edge, *pieces)


def local(loads, sleeper_pos, material, material_table):
    ka = lax.axis_size("ka")
    gy, gz = lax.axis_size("gy"), lax.axis_size("gz")
    count = KW // ka
    wave_start = lax.axis_index("ka") * count
    sleepers = ka * loads.shape[0]
    own = 3 * loads.shape[0]
    ny, depth = material.shape
    height = ny + 2 * HB
    loads = loads.reshape(own, ny, depth)
    material = material.astype(jnp.float32)[None]

    def swap(array, axis, size, first):
        pairs = [(i, i + 1) for i in range(first, size - 1, 2)]
        return lax.ppermute(array, axis, pairs + [(high, low) for low, high in pairs])

    y_at, z_at = lax.axis_index("gy"), lax.axis_index("gz")
    y_odd, z_odd = y_at % 2 == 1, z_at % 2 == 1
    turns = [[(i, (i + step) % ka) for i in range(ka)] for step in range(1, ka)]
    ends = jnp.concatenate([loads[:, :HB], loads[:, ny - HB :]], axis=1)
    ends, sleeper_pos = lax.optimization_barrier((ends, sleeper_pos))
    got_ends = [lax.ppermute(ends, "ka", turn) for turn in turns]
    all_pos = [sleeper_pos] + [lax.ppermute(sleeper_pos, "ka", turn) for turn in turns]
    met, tied = lax.optimization_barrier((all_pos, loads))
    low = jnp.concatenate([tied[:, :HB], material[:, :HB]], axis=0)
    high = jnp.concatenate([tied[:, ny - HB :], material[:, ny - HB :]], axis=0)
    halos = (
        swap(jnp.where(y_odd, low, high), "gy", gy, 0),
        swap(jnp.where(y_odd, high, low), "gy", gy, 1),
    )
    inner, got_ends = lax.optimization_barrier((loads[:, HB : ny - HB], got_ends))
    got_inner = [lax.ppermute(inner, "ka", turn) for turn in turns]

    pieces, spots = [], []
    sides = ((HB + ny, 0), (0, HB + ny))

    def place(array, *where):
        pieces.append(array)
        spots.extend((len(pieces) - 1, *spot) for spot in where)

    def place_middle(first, outer, middle):
        place(outer, (first, own, 0, (0, HB), HB), (first, own, 0, (HB, HB), ny))
        place(middle, (first, own, 0, (0, ny - 2 * HB), 2 * HB))

    place_middle(0, ends, inner)
    place(material, (3 * sleepers, 1, 0, (0, ny), HB))
    for array, row in zip(halos, sides):
        place(array, (0, own, 0, (0, HB), row), (3 * sleepers, 1, own, (0, HB), row))
    for step, (outer, middle) in enumerate(zip(got_ends, got_inner), 1):
        place_middle(own * step, outer, middle)
        low, high = outer[:, :HB], outer[:, HB:]
        far = (
            swap(jnp.where(y_odd, low, high), "gy", gy, 0),
            swap(jnp.where(y_odd, high, low), "gy", gy, 1),
        )
        for array, row in zip(far, sides):
            place(array, (own * step, own, 0, (0, HB), row))

    met, _ = lax.optimization_barrier((met, got_ends))
    tw, tc, vectors = tables(
        jnp.concatenate(met), material_table, wave_start, count, lanes_for(sleepers)
    )
    flags = jnp.stack([y_at == 0, y_at == gy - 1, y_odd, z_odd]).astype(jnp.int32)
    sub = jnp.arange(8)[:, None]
    lane = jnp.arange(LANES)[None, :]
    edge = jnp.stack(
        [
            jnp.where((z_at == 0) & (sub == 0) & (lane < HALF), 0.0, 1.0),
            jnp.where((z_at == gz - 1) & (sub == 7) & (lane >= HALF), 0.0, 1.0),
        ]
    ).astype(jnp.float32)
    pieces[-1], flags, edge, tw, tc, vectors = lax.optimization_barrier(
        (pieces[-1], flags, edge, tw, tc, vectors)
    )

    columns = edges_of(spots, flags, pieces, sleepers, height, depth)
    high, low = columns[:, :HB], columns[:, HB:]
    inside = swap(jnp.where(z_odd, low, high), "gz", gz, 0)
    across = swap(jnp.where(z_odd, high, low), "gz", gz, 1)
    return solve_field(
        spots, pieces, flags, inside, across, tw, tc, vectors, edge, sleepers, count
    )


def solution(mesh):
    return jax.shard_map(
        local,
        mesh=mesh,
        in_specs=(P("ka", None, "gy", "gz"), P("ka"), P("gy", "gz"), P()),
        out_specs=P("ka", None, None, "gy", "gz"),
        check_vma=False,
    )
```

```python
import functools
import math

import jax
import jax.numpy as jnp
from jax import lax
from jax.experimental import pallas as pl
from jax.experimental.pallas import tpu as pltpu
from jax.sharding import PartitionSpec as P

KW = 128
NMAT = 8
DEG = 4
LANES = 128
HALF = 64
SEGS = 16
HY = 7
HB = 8


def lanes_for(sleepers):
    return -(-(3 * sleepers + 3 * NMAT) // LANES) * LANES


def two_parts(values):
    high = values.astype(jnp.bfloat16)
    low = (values - high.astype(jnp.float32)).astype(jnp.bfloat16)
    return high, low


def dot(a, b):
    return lax.dot_general(a, b, (((1,), (0,)), ((), ())), preferred_element_type=jnp.float32)


def dot_t(a, b):
    return lax.dot_general(a, b, (((1,), (1,)), ((), ())), preferred_element_type=jnp.float32)


def table_kernel(sleepers, count, start, table, cells, positions, tw, tc, vectors):
    width = tc.shape[0] // 2
    lane = lax.broadcasted_iota(jnp.int32, (8, LANES), 1)
    wave = lane % HALF
    live = wave < count
    wave = wave + start[0]
    q = (2.0 * jnp.sin(wave.astype(jnp.float32) * (math.pi / KW))) ** 2
    lowest = highest = None
    for m in range(NMAT):
        s, xx, yy, zz, xy, xz, yz = (jnp.full((8, LANES), table[m, f]) for f in range(7))
        xy, xz, yz = jnp.abs(xy), jnp.abs(xz), jnp.abs(yz)
        sums = (xy + xz, xy + yz, xz + yz)
        low = s + q * functools.reduce(jnp.minimum, [d - r for d, r in zip((xx, yy, zz), sums)])
        high = s + q * functools.reduce(jnp.maximum, [d + r for d, r in zip((xx, yy, zz), sums)])
        lowest = low if m == 0 else jnp.minimum(lowest, low)
        highest = high if m == 0 else jnp.maximum(highest, high)
    highest = 8.0 + highest
    center = 0.5 * (highest + lowest)
    half_width = 0.5 * (highest - lowest)
    ratio2 = (center / half_width) ** 2
    top = 8.0 * ratio2 * (ratio2 - 1.0) + 1.0
    h2 = half_width * half_width
    h4 = h2 * h2
    scale = 8.0 / (top * h4)
    scale = jnp.where(live, scale * scale, 0.0)
    twice = h2 * jnp.sqrt(0.5 * (top + 1.0))
    shift = 0.5 * jnp.sqrt(twice + h2)
    tilt = 0.5 * jnp.sqrt(jnp.maximum(twice - h2, 0.0))
    for n, vector in enumerate((shift, tilt, jnp.sqrt(lowest * highest), center)):
        vectors[n, :, :] = jnp.where(live, vector, 0.0)

    tc[...] = jnp.zeros(tc.shape, jnp.bfloat16)
    tw[...] = jnp.zeros(tw.shape, jnp.bfloat16)
    column = [jnp.broadcast_to(cells[:, f : f + 1], (8, LANES)) for f in range(8)]
    fields = [center - 4.0 - column[0] - q * column[c] for c in (1, 2, 3)]
    fields += [-q * column[c] for c in (4, 5, 6)] + [q * column[7]]
    rounded = lambda values: values.astype(jnp.bfloat16).astype(jnp.float32)
    for f, field in enumerate(fields):
        field = jnp.where(live, field, 0.0)
        first = rounded(field)
        second = rounded(field - first)
        third = field - first - second
        rows = jnp.concatenate([first, second, third, jnp.zeros_like(first)], axis=0)
        lanes = lax.broadcasted_iota(jnp.int32, rows.shape, 1)
        for half in range(2):
            kept = jnp.where(lanes // HALF == half, rows, 0.0).astype(jnp.bfloat16)
            at = half * width + 3 * sleepers
            tc[at : at + 32, f * LANES : (f + 1) * LANES] = kept

    turns = (positions[...] * wave[:1]) & (KW - 1)
    angles = turns.astype(jnp.float32) * (2.0 * math.pi / KW)
    lanes = lax.broadcasted_iota(jnp.int32, turns.shape, 1)
    for part, phase in enumerate((jnp.cos(angles), -jnp.sin(angles))):
        phase = phase * scale[:1]
        high = rounded(phase)
        for segment, values in enumerate((high, high, phase - high)):
            for half in range(2):
                kept = jnp.where(lanes // HALF == half, values, 0.0).astype(jnp.bfloat16)
                for c in range(3):
                    at = (2 * segment + half) * width + c * sleepers
                    to = (2 * c + part) * LANES
                    tw[at : at + sleepers, to : to + LANES] = kept


def tables(positions, material_table, start, count, width):
    sleepers = positions.shape[0]
    spots = jnp.broadcast_to(positions[:, None], (sleepers, LANES))
    return pl.pallas_call(
        functools.partial(table_kernel, sleepers, count),
        out_shape=(
            jax.ShapeDtypeStruct((6 * width, 6 * LANES), jnp.bfloat16),
            jax.ShapeDtypeStruct((2 * width, 8 * LANES), jnp.bfloat16),
            jax.ShapeDtypeStruct((4, 8, LANES), jnp.float32),
        ),
        in_specs=[pl.BlockSpec(memory_space=pltpu.SMEM)] * 2
        + [pl.BlockSpec(memory_space=pltpu.VMEM)] * 2,
        out_specs=(pl.BlockSpec(memory_space=pltpu.VMEM),) * 3,
        compiler_params=pltpu.CompilerParams(vmem_limit_bytes=32 * 1024 * 1024),
        name="tables",
    )(start.reshape(1), material_table, material_table, spots)


def row_values(planes, row, height, sleepers, width):
    depth = planes.shape[1]
    parts = [planes[pl.ds(c * height + row, sleepers, stride=3 * height), :] for c in range(3)]
    material = planes[pl.ds(3 * sleepers * height + row, 1), :]
    number = lax.broadcasted_iota(jnp.int32, (width - 3 * sleepers, depth), 0)
    kind = jnp.where(number < 3 * NMAT, number % NMAT, -1).astype(jnp.float32)
    parts.append((kind == material).astype(jnp.float32))
    return jnp.concatenate(parts, axis=0)


def gather(spots, flags, pieces, planes, sems):
    copies = []
    for n, (piece, first, count, plane, row, target) in enumerate(spots):
        src = pieces[piece]
        blocks = (0, planes.shape[1] // 8 - 1)
        if isinstance(target, tuple):
            target = pl.multiple_of(jnp.where(flags[2] == 1, target[1], target[0]), 8)
        else:
            blocks = range(target // 8, (target + row[1]) // 8)
        copy = pltpu.make_async_copy(
            src.at[plane : plane + count, row[0] : row[0] + row[1], :],
            planes.at[first : first + count, pl.ds(target, row[1]), :],
            sems.at[n],
        )
        copies.append((copy, blocks))
    for copy, _ in copies:
        copy.start()
    return copies


def edge_kernel(sleepers, spots, *refs):
    flags, *pieces, out, planes, sems = refs
    copies = gather(spots, flags, pieces, planes, sems)
    height, depth = planes.shape[1:]
    width = out.shape[2]
    strip = 2 * HB
    flat = planes.reshape(planes.shape[0] * height, depth)
    group = lax.broadcasted_iota(jnp.int32, (width, depth), 1) // strip

    last = height // 8 - 1
    for block in [*range(1, last), 0, last]:
        for copy, blocks in copies:
            if block in blocks:
                copy.wait()
        copies = [(copy, blocks) for copy, blocks in copies if block not in blocks]
        packed = None
        for line in range(8):
            values = row_values(flat, 8 * block + line, height, sleepers, width)
            moved = pltpu.roll(values, strip * line + HB, 1)
            packed = moved if line == 0 else jnp.where(group == line, moved, packed)
        for n in range(width // LANES):
            span = slice(n * LANES, (n + 1) * LANES)
            turned = jnp.transpose(packed[span])
            for line in range(8):
                out[8 * block + line, :, span] = turned[line * strip : (line + 1) * strip]


def edges_of(spots, flags, pieces, sleepers, height, depth):
    return pl.pallas_call(
        functools.partial(edge_kernel, sleepers, spots),
        out_shape=(
            jax.ShapeDtypeStruct((height, 2 * HB, lanes_for(sleepers)), jnp.float32),
            jax.ShapeDtypeStruct((3 * sleepers + 1, height, depth), jnp.float32),
        ),
        in_specs=[pl.BlockSpec(memory_space=pltpu.SMEM)]
        + [pl.BlockSpec(memory_space=pl.ANY)] * len(pieces),
        out_specs=(pl.BlockSpec(memory_space=pltpu.VMEM),) * 2,
        scratch_shapes=[pltpu.SemaphoreType.DMA((len(spots),))],
        compiler_params=pltpu.CompilerParams(vmem_limit_bytes=32 * 1024 * 1024),
        name="edge_columns",
    )(flags, *pieces)


def field_kernel(sleepers, count, seglen, scratch, *refs):
    pl.run_scoped(functools.partial(field_body, sleepers, count, seglen, refs), *scratch)


def field_body(sleepers, count, seglen, refs, *scratch):
    flags, planes, inside, across, tw, tc, vectors, edge, out = refs
    source, ghosts, coefs, made, lhs, lay, *rings = scratch[:12]
    turn, pages, page_sems = scratch[12:]
    height, depth = planes.shape[1:]
    flat = planes.reshape(planes.shape[0] * height, depth)
    ny = height - 2 * HB
    width = inside.shape[2]
    chunks = width // LANES
    cells = 8 * seglen
    page_rows = pages.reshape(2 * count * 48, depth)
    lane = lax.broadcasted_iota(jnp.int32, (8, LANES), 1)
    sub = lax.broadcasted_iota(jnp.int32, (8, LANES), 0)

    def at(zm):
        return pl.ds(8 * (zm + 1), 8)

    def around(first, last):
        before = pltpu.roll(last, 1, 0)
        after = pltpu.roll(first, 7, 0)
        return (
            jnp.where(sub == 0, pltpu.roll(before, HALF, 1), before),
            jnp.where(sub == 7, pltpu.roll(after, HALF, 1), after),
        )

    def line_at(row, zm):
        return pl.ds(pl.multiple_of((row & 15) * cells, 8) + 8 * zm, 8)

    def column(q):
        part, c = divmod(q, 3)
        return slice((2 * c + part) * LANES, (2 * c + part + 1) * LANES)

    def read_source(row, q, zm):
        if zm == -1:
            return ghosts[row & 3, q, :8, :]
        if zm == seglen:
            return ghosts[row & 3, q, 8:, :]
        rows = pl.ds(pl.multiple_of((row & 3) * cells, 8) + 8 * zm, 8)
        return source[rows, column(q)]

    def reader(ring):
        def read(row, q, zm):
            outside = ((row < HY) & (flags[0] == 1)) | ((row >= HY + ny) & (flags[1] == 1))
            return ring[jnp.where(outside, 4, row & 3), q, at(zm), :]

        return read

    def produce(pair):
        def lay_out(k):
            srow = jnp.clip(2 * pair - 2 + k + (HB - HY), 0, height - 1)
            values = row_values(flat, srow, height, sleepers, width)
            odd = flags[3] == 1
            for n in range(chunks):
                span = slice(n * LANES, (n + 1) * LANES)
                lay[k * chunks + n, HB : HB + depth, :] = jnp.transpose(values[span])
                first, second = inside[srow, :, span], across[srow, :, span]
                lay[k * chunks + n, :HB, :] = jnp.where(odd, first, second)
                lay[k * chunks + n, HB + depth :, :] = jnp.where(odd, second, first)

        def split():
            halves = [[], []]
            for k in range(2):
                for half in range(2):
                    for zm in range(seglen):
                        spot = pl.ds(half * cells + zm, 8, stride=seglen)
                        pieces_at = [lay[k * chunks + n, spot, :] for n in range(chunks)]
                        halves[half].append(jnp.concatenate(pieces_at, axis=1))
            values = jnp.concatenate(
                [jnp.concatenate(half, axis=0) for half in halves], axis=1
            )
            high, low = two_parts(values)
            lhs[:, : 2 * width] = high
            lhs[:, 2 * width : 4 * width] = low
            lhs[:, 4 * width :] = high

        first_row = 2 * pair - 2
        target = pl.ds(pl.multiple_of((first_row & 3) * cells, 8), 2 * cells)

        def spectrum(c):
            span = slice(2 * c * LANES, 2 * (c + 1) * LANES)
            source[target, span] = dot(lhs[...], tw[:, span])

        def fields(f):
            span = slice(f * LANES, (f + 2) * LANES)
            made[:, span] = dot(lhs[:, : 2 * width], tc[:, span])

        def wrap(k):
            row = first_row + k
            for q in range(6):
                ghosts[row & 3, q, :8, :], ghosts[row & 3, q, 8:, :] = around(
                    read_source(row, q, 0), read_source(row, q, seglen - 1)
                )

        return (
            [functools.partial(lay_out, 0), functools.partial(lay_out, 1), split],
            [functools.partial(spectrum, c) for c in range(3)]
            + [functools.partial(fields, f) for f in range(0, 8, 2)]
            + [functools.partial(wrap, k) for k in range(2)],
        )

    def commit(pair):
        def move(k, zm):
            rows = slice(k * cells + 8 * zm, k * cells + 8 * zm + 8)
            for n in range(7):
                span = slice(n * LANES, (n + 1) * LANES)
                coefs[line_at(2 * pair - 2 + k, zm), span] = made[rows, span]

        return [functools.partial(move, k, zm) for k in range(2) for zm in range(seglen)]

    def apply(src, row, emit, shift=None, tilt=None):
        cur = [[src(row + k, q, 0) for q in range(6)] for k in range(2)]
        behind = [
            [src(row + k, q, -1) + (cur[1][q] if k == 0 else src(row + 2, q, 0)) for q in range(6)]
            for k in range(2)
        ]
        for zm in range(seglen):
            nxt = [[src(row + k, q, zm + 1) for q in range(6)] for k in range(2)]
            ahead = [
                [src(row - 1, q, zm) + nxt[0][q] for q in range(6)],
                [cur[0][q] + nxt[1][q] for q in range(6)],
            ]
            if zm + 1 < seglen:
                below = [cur[1][q] + src(row + 2, q, zm + 1) for q in range(6)]
            for k in range(2):
                f = [
                    coefs[line_at(row + k, zm), n * LANES : (n + 1) * LANES] for n in range(7)
                ]
                diagonal, damping = f[:3], f[6]
                if shift is not None:
                    diagonal = [d + shift for d in diagonal]
                if tilt is not None:
                    damping = damping - tilt
                matrix = (
                    (diagonal[0], f[3], f[4]),
                    (f[3], diagonal[1], f[5]),
                    (f[4], f[5], diagonal[2]),
                )
                results = []
                for q in range(6):
                    part, c = divmod(q, 3)
                    mine = cur[k][3 * part : 3 * part + 3]
                    own = matrix[c][0] * mine[0] + matrix[c][1] * mine[1] + matrix[c][2] * mine[2]
                    damp = damping * cur[k][3 * (1 - part) + c]
                    total = (ahead[k][q] + behind[k][q]) + own
                    total = total + damp if part == 0 else total - damp
                    results.append(total)
                emit(k, zm, results)
            if zm + 1 < seglen:
                behind = [ahead[1], below]
            cur = nxt

    def stage(src, dst, row, shift, tilt, between=None):
        ends = {}

        def emit(k, zm, results):
            if zm == HB - 1:
                results = [value * edge[0] for value in results]
            if zm == (HB + depth) % seglen:
                results = [value * edge[1] for value in results]
            slot = (row + k) & 3
            for q in range(6):
                dst[slot, q, at(zm), :] = results[q]
            if zm in (0, seglen - 1):
                ends[k, zm] = results
            if zm == seglen - 1:
                for q in range(6):
                    dst[slot, q, at(-1), :], dst[slot, q, at(seglen), :] = around(
                        ends[k, 0][q], results[q]
                    )
            if between is not None:
                between()

        apply(src, row, emit, shift, tilt)

    def last_stage(row, between=None):
        def emit(k, zm, results):
            for c in range(3):
                real, imag = results[c], results[3 + c]
                first = jnp.where(lane < HALF, real, pltpu.roll(imag, HALF, 1))
                second = jnp.where(lane < HALF, pltpu.roll(real, HALF, 1), imag)
                turn[3 * k + c, pl.ds(zm, 8, stride=seglen), :] = first
                turn[3 * k + c, pl.ds(cells + zm, 8, stride=seglen), :] = second
            if between is not None:
                between()

        apply(reader(rings[5]), row, emit, shift=vectors[3])

    def run_stage(t, base, between=None):
        shift = (1, 1, -1, -1, 0, 0)[t - 1]
        shift = shift * vectors[0] if shift else None
        tilt = (vectors[1] if t <= 4 else vectors[2]) * (1 if t % 2 else -1)
        src = read_source if t == 1 else reader(rings[t - 2])
        stage(src, rings[t - 1], base - t, shift, tilt, between)

    def spread(tasks, slots):
        total, seen, left_over = len(tasks), [0], list(tasks)

        def between():
            seen[0] += 1
            while left_over and (total - len(left_over)) * slots < seen[0] * total:
                left_over.pop(0)()

        return between

    def mixed(first, second):
        tasks = []
        for n in range(max(len(first), len(second))):
            tasks += first[n : n + 1] + second[n : n + 1]
        return tasks

    def finish(pair):
        done = pair - HB
        block = done >> 2
        start = pl.multiple_of((block & 1) * (count * 48), 8) + 2 * (done & 3)

        def page(k, c):
            turned = jnp.transpose(turn[3 * k + c, HB : HB + depth, :])
            for part in range(2):
                rows = pl.ds(start + (part * 3 + c) * 8 + k, count, stride=48)
                page_rows[rows, :] = turned[part * HALF : part * HALF + count]

        return [functools.partial(page, k, c) for k in range(2) for c in range(3)]

    def page_copy(block):
        return pltpu.make_async_copy(
            pages.at[block & 1],
            out.at[:, :, :, pl.ds(pl.multiple_of(8 * block, 8), 8), :],
            page_sems.at[block & 1],
        )

    def ramp(pair, carry):
        base = 2 * pair - 2
        early, late = produce(pair + 1)
        for t, tasks in ((1, early), (2, late)):

            @pl.when(base >= 2 * t)
            def _():
                run_stage(t, base, spread(tasks, 2 * seglen))

            @pl.when(base < 2 * t)
            def _():
                for task in tasks:
                    task()

        for t in range(3, 7):

            @pl.when(base >= 2 * t)
            def _():
                run_stage(t, base)

        @pl.when(base >= 14)
        def _():
            last_stage(base - 7)

        for task in commit(pair + 1):
            task()
        return carry

    def steady(pair, carry):
        base = 2 * pair - 2
        done = pair - 1 - HB

        @pl.when(((done & 3) == 0) & (done >= 8))
        def _():
            page_copy((done >> 2) - 2).wait()

        early, late = produce(pair + 1)
        turning = finish(pair - 1)
        run_stage(1, base, spread(mixed(early, turning[:2]), 2 * seglen))
        between = spread(mixed(late, turning[2:]), 10 * seglen)
        for t in range(2, 7):
            run_stage(t, base, between)
        last_stage(base - 7, spread(commit(pair + 1), 2 * seglen))

        @pl.when((done & 3) == 3)
        def _():
            page_copy(done >> 2).start()

        return carry

    for ring in rings:
        for q in range(6):
            ring[4, q, :, :] = jnp.zeros(ring.shape[2:], jnp.float32)
    early, late = produce(0)
    for task in early + late + commit(0):
        task()
    final = HB + ny // 2 - 1
    lax.fori_loop(0, HB + 1, ramp, 0)
    lax.fori_loop(HB + 1, final + 1, steady, 0)
    for step in finish(final):
        step()
    blocks = ny // 8
    page_copy(blocks - 1).start()
    for block in range(max(blocks - 2, 0), blocks):
        page_copy(block).wait()


def solve_field(planes, flags, inside, across, tw, tc, vectors, edge, sleepers, count):
    height, _, width = inside.shape
    depth = planes.shape[2]
    ny = height - 2 * HB
    seglen = (depth + 2 * HB) // SEGS
    cells = 8 * seglen
    chunks = width // LANES
    ring = pltpu.VMEM((5, 6, 8 * (seglen + 2), LANES), jnp.float32)
    whole = pl.BlockSpec(memory_space=pltpu.VMEM)
    scratch = (
        pltpu.VMEM((4 * cells, 6 * LANES), jnp.float32),
        pltpu.VMEM((4, 6, 16, LANES), jnp.float32),
        pltpu.VMEM((16 * cells, 7 * LANES), jnp.float32),
        pltpu.VMEM((2 * cells, 8 * LANES), jnp.float32),
        pltpu.VMEM((2 * cells, 6 * width), jnp.bfloat16),
        pltpu.VMEM((2 * chunks, 2 * cells, LANES), jnp.float32),
        ring, ring, ring, ring, ring, ring,
        pltpu.VMEM((6, 2 * cells, LANES), jnp.float32),
        pltpu.VMEM((2, count, 2, 3, 8, depth), jnp.float32),
        pltpu.SemaphoreType.DMA((2,)),
    )
    return pl.pallas_call(
        functools.partial(field_kernel, sleepers, count, seglen, scratch),
        out_shape=jax.ShapeDtypeStruct((count, 2, 3, ny, depth), jnp.float32),
        in_specs=[pl.BlockSpec(memory_space=pltpu.SMEM)]
        + [whole] * 7,
        out_specs=pl.BlockSpec(memory_space=pl.ANY),
        compiler_params=pltpu.CompilerParams(vmem_limit_bytes=40 * 1024 * 1024),
        name="adjoint_field",
    )(flags, planes, inside, across, tw, tc, vectors, edge)


def local(loads, sleeper_pos, material, material_table):
    ka = lax.axis_size("ka")
    gy, gz = lax.axis_size("gy"), lax.axis_size("gz")
    count = KW // ka
    wave_start = lax.axis_index("ka") * count
    sleepers = ka * loads.shape[0]
    own = 3 * loads.shape[0]
    ny, depth = material.shape
    height = ny + 2 * HB
    loads = loads.reshape(own, ny, depth)
    material = material.astype(jnp.float32)[None]

    def swap(array, axis, size, first):
        pairs = [(i, i + 1) for i in range(first, size - 1, 2)]
        return lax.ppermute(array, axis, pairs + [(high, low) for low, high in pairs])

    y_at, z_at = lax.axis_index("gy"), lax.axis_index("gz")
    y_odd, z_odd = y_at % 2 == 1, z_at % 2 == 1
    turns = [[(i, (i + step) % ka) for i in range(ka)] for step in range(1, ka)]
    ends = jnp.concatenate([loads[:, :HB], loads[:, ny - HB :]], axis=1)
    ends, sleeper_pos = lax.optimization_barrier((ends, sleeper_pos))
    got_ends = [lax.ppermute(ends, "ka", turn) for turn in turns]
    all_pos = [sleeper_pos] + [lax.ppermute(sleeper_pos, "ka", turn) for turn in turns]
    met, tied = lax.optimization_barrier((all_pos, loads))
    low = jnp.concatenate([tied[:, :HB], material[:, :HB]], axis=0)
    high = jnp.concatenate([tied[:, ny - HB :], material[:, ny - HB :]], axis=0)
    halos = (
        swap(jnp.where(y_odd, low, high), "gy", gy, 0),
        swap(jnp.where(y_odd, high, low), "gy", gy, 1),
    )
    inner, got_ends = lax.optimization_barrier((loads[:, HB : ny - HB], got_ends))
    got_inner = [lax.ppermute(inner, "ka", turn) for turn in turns]

    pieces, spots = [], []
    sides = ((HB + ny, 0), (0, HB + ny))

    def place(array, *where):
        pieces.append(array)
        spots.extend((len(pieces) - 1, *spot) for spot in where)

    def place_middle(first, outer, middle):
        place(outer, (first, own, 0, (0, HB), HB), (first, own, 0, (HB, HB), ny))
        place(middle, (first, own, 0, (0, ny - 2 * HB), 2 * HB))

    place_middle(0, ends, inner)
    place(material, (3 * sleepers, 1, 0, (0, ny), HB))
    for array, row in zip(halos, sides):
        place(array, (0, own, 0, (0, HB), row), (3 * sleepers, 1, own, (0, HB), row))
    for step, (outer, middle) in enumerate(zip(got_ends, got_inner), 1):
        place_middle(own * step, outer, middle)
        low, high = outer[:, :HB], outer[:, HB:]
        far = (
            swap(jnp.where(y_odd, low, high), "gy", gy, 0),
            swap(jnp.where(y_odd, high, low), "gy", gy, 1),
        )
        for array, row in zip(far, sides):
            place(array, (own * step, own, 0, (0, HB), row))

    met, _ = lax.optimization_barrier((met, got_ends))
    tw, tc, vectors = tables(
        jnp.concatenate(met), material_table, wave_start, count, lanes_for(sleepers)
    )
    flags = jnp.stack([y_at == 0, y_at == gy - 1, y_odd, z_odd]).astype(jnp.int32)
    sub = jnp.arange(8)[:, None]
    lane = jnp.arange(LANES)[None, :]
    edge = jnp.stack(
        [
            jnp.where((z_at == 0) & (sub == 0) & (lane < HALF), 0.0, 1.0),
            jnp.where((z_at == gz - 1) & (sub == 7) & (lane >= HALF), 0.0, 1.0),
        ]
    ).astype(jnp.float32)
    pieces[-1], flags, edge, tw, tc, vectors = lax.optimization_barrier(
        (pieces[-1], flags, edge, tw, tc, vectors)
    )

    columns, planes = edges_of(spots, flags, pieces, sleepers, height, depth)
    high, low = columns[:, :HB], columns[:, HB:]
    inside = swap(jnp.where(z_odd, low, high), "gz", gz, 0)
    across = swap(jnp.where(z_odd, high, low), "gz", gz, 1)
    return solve_field(
        planes, flags, inside, across, tw, tc, vectors, edge, sleepers, count
    )


def solution(mesh):
    return jax.shard_map(
        local,
        mesh=mesh,
        in_specs=(P("ka", None, "gy", "gz"), P("ka"), P("gy", "gz"), P()),
        out_specs=P("ka", None, None, "gy", "gz"),
        check_vma=False,
    )
```

```python
import functools
import math

import jax
import jax.numpy as jnp
from jax import lax
from jax.experimental import pallas as pl
from jax.experimental.pallas import tpu as pltpu
from jax.sharding import PartitionSpec as P

KW = 128
NMAT = 8
DEG = 4
LANES = 128
HALF = 64
SEGS = 16
HY = 7
HB = 8


def lanes_for(sleepers):
    return -(-(3 * sleepers + 3 * NMAT) // LANES) * LANES


def two_parts(values):
    high = values.astype(jnp.bfloat16)
    low = (values - high.astype(jnp.float32)).astype(jnp.bfloat16)
    return high, low


def dot(a, b):
    return lax.dot_general(a, b, (((1,), (0,)), ((), ())), preferred_element_type=jnp.float32)


def table_kernel(sleepers, count, start, table, cells, positions, tw, tc, vectors):
    width = tc.shape[0] // 2
    lane = lax.broadcasted_iota(jnp.int32, (8, LANES), 1)
    wave = lane % HALF
    live = wave < count
    wave = wave + start[0]
    q = (2.0 * jnp.sin(wave.astype(jnp.float32) * (math.pi / KW))) ** 2
    lowest = highest = None
    for m in range(NMAT):
        s, xx, yy, zz, xy, xz, yz = (jnp.full((8, LANES), table[m, f]) for f in range(7))
        xy, xz, yz = jnp.abs(xy), jnp.abs(xz), jnp.abs(yz)
        sums = (xy + xz, xy + yz, xz + yz)
        low = s + q * functools.reduce(jnp.minimum, [d - r for d, r in zip((xx, yy, zz), sums)])
        high = s + q * functools.reduce(jnp.maximum, [d + r for d, r in zip((xx, yy, zz), sums)])
        lowest = low if m == 0 else jnp.minimum(lowest, low)
        highest = high if m == 0 else jnp.maximum(highest, high)
    highest = 8.0 + highest
    center = 0.5 * (highest + lowest)
    half_width = 0.5 * (highest - lowest)
    ratio2 = (center / half_width) ** 2
    top = 8.0 * ratio2 * (ratio2 - 1.0) + 1.0
    h2 = half_width * half_width
    h4 = h2 * h2
    scale = 8.0 / (top * h4)
    scale = jnp.where(live, scale * scale, 0.0)
    twice = h2 * jnp.sqrt(0.5 * (top + 1.0))
    shift = 0.5 * jnp.sqrt(twice + h2)
    tilt = 0.5 * jnp.sqrt(jnp.maximum(twice - h2, 0.0))
    for n, vector in enumerate((shift, tilt, jnp.sqrt(lowest * highest), center)):
        vectors[n, :, :] = jnp.where(live, vector, 0.0)

    tc[...] = jnp.zeros(tc.shape, jnp.bfloat16)
    tw[...] = jnp.zeros(tw.shape, jnp.bfloat16)
    column = [jnp.broadcast_to(cells[:, f : f + 1], (8, LANES)) for f in range(8)]
    fields = [center - 4.0 - column[0] - q * column[c] for c in (1, 2, 3)]
    fields += [-q * column[c] for c in (4, 5, 6)] + [q * column[7]]
    rounded = lambda values: values.astype(jnp.bfloat16).astype(jnp.float32)
    for f, field in enumerate(fields):
        field = jnp.where(live, field, 0.0)
        first = rounded(field)
        second = rounded(field - first)
        third = field - first - second
        rows = jnp.concatenate([first, second, third, jnp.zeros_like(first)], axis=0)
        lanes = lax.broadcasted_iota(jnp.int32, rows.shape, 1)
        for half in range(2):
            kept = jnp.where(lanes // HALF == half, rows, 0.0).astype(jnp.bfloat16)
            at = half * width + 3 * sleepers
            tc[at : at + 32, f * LANES : (f + 1) * LANES] = kept

    turns = (positions[...] * wave[:1]) & (KW - 1)
    angles = turns.astype(jnp.float32) * (2.0 * math.pi / KW)
    lanes = lax.broadcasted_iota(jnp.int32, turns.shape, 1)
    for part, phase in enumerate((jnp.cos(angles), -jnp.sin(angles))):
        phase = phase * scale[:1]
        high = rounded(phase)
        for segment, values in enumerate((high, high, phase - high)):
            for half in range(2):
                kept = jnp.where(lanes // HALF == half, values, 0.0).astype(jnp.bfloat16)
                for c in range(3):
                    at = (2 * segment + half) * width + c * sleepers
                    to = (2 * c + part) * LANES
                    tw[at : at + sleepers, to : to + LANES] = kept


def tables(positions, material_table, start, count, width):
    sleepers = positions.shape[0]
    spots = jnp.broadcast_to(positions[:, None], (sleepers, LANES))
    return pl.pallas_call(
        functools.partial(table_kernel, sleepers, count),
        out_shape=(
            jax.ShapeDtypeStruct((6 * width, 6 * LANES), jnp.bfloat16),
            jax.ShapeDtypeStruct((2 * width, 8 * LANES), jnp.bfloat16),
            jax.ShapeDtypeStruct((4, 8, LANES), jnp.float32),
        ),
        in_specs=[pl.BlockSpec(memory_space=pltpu.SMEM)] * 2
        + [pl.BlockSpec(memory_space=pltpu.VMEM)] * 2,
        out_specs=(pl.BlockSpec(memory_space=pltpu.VMEM),) * 3,
        compiler_params=pltpu.CompilerParams(vmem_limit_bytes=32 * 1024 * 1024),
        name="tables",
    )(start.reshape(1), material_table, material_table, spots)


def row_values(planes, row, height, sleepers, width):
    depth = planes.shape[1]
    parts = [planes[pl.ds(c * height + row, sleepers, stride=3 * height), :] for c in range(3)]
    material = planes[pl.ds(3 * sleepers * height + row, 1), :]
    number = lax.broadcasted_iota(jnp.int32, (width - 3 * sleepers, depth), 0)
    kind = jnp.where(number < 3 * NMAT, number % NMAT, -1).astype(jnp.float32)
    parts.append((kind == material).astype(jnp.float32))
    return jnp.concatenate(parts, axis=0)


def gather(spots, flags, pieces, planes, sems):
    copies = []
    for n, (piece, first, count, plane, row, target) in enumerate(spots):
        src = pieces[piece]
        blocks = (0, planes.shape[1] // 8 - 1)
        if isinstance(target, tuple):
            target = pl.multiple_of(jnp.where(flags[2] == 1, target[1], target[0]), 8)
        else:
            blocks = range(target // 8, (target + row[1]) // 8)
        copy = pltpu.make_async_copy(
            src.at[plane : plane + count, row[0] : row[0] + row[1], :],
            planes.at[first : first + count, pl.ds(target, row[1]), :],
            sems.at[n],
        )
        copies.append((copy, blocks))
    for copy, _ in copies:
        copy.start()
    return copies


def edge_kernel(sleepers, spots, *refs):
    flags, *pieces, out, planes, sems = refs
    copies = gather(spots, flags, pieces, planes, sems)
    height, depth = planes.shape[1:]
    width = out.shape[2]
    strip = 2 * HB
    flat = planes.reshape(planes.shape[0] * height, depth)
    group = lax.broadcasted_iota(jnp.int32, (width, depth), 1) // strip

    last = height // 8 - 1
    for block in [*range(1, last), 0, last]:
        for copy, blocks in copies:
            if block in blocks:
                copy.wait()
        copies = [(copy, blocks) for copy, blocks in copies if block not in blocks]
        packed = None
        for line in range(8):
            values = row_values(flat, 8 * block + line, height, sleepers, width)
            moved = pltpu.roll(values, strip * line + HB, 1)
            packed = moved if line == 0 else jnp.where(group == line, moved, packed)
        for n in range(width // LANES):
            span = slice(n * LANES, (n + 1) * LANES)
            turned = jnp.transpose(packed[span])
            for line in range(8):
                out[8 * block + line, :, span] = turned[line * strip : (line + 1) * strip]


def edges_of(spots, flags, pieces, sleepers, height, depth):
    return pl.pallas_call(
        functools.partial(edge_kernel, sleepers, spots),
        out_shape=(
            jax.ShapeDtypeStruct((height, 2 * HB, lanes_for(sleepers)), jnp.float32),
            jax.ShapeDtypeStruct((3 * sleepers + 1, height, depth), jnp.float32),
        ),
        in_specs=[pl.BlockSpec(memory_space=pltpu.SMEM)]
        + [pl.BlockSpec(memory_space=pl.ANY)] * len(pieces),
        out_specs=(pl.BlockSpec(memory_space=pltpu.VMEM),) * 2,
        scratch_shapes=[pltpu.SemaphoreType.DMA((len(spots),))],
        compiler_params=pltpu.CompilerParams(vmem_limit_bytes=32 * 1024 * 1024),
        name="edge_columns",
    )(flags, *pieces)


def field_kernel(sleepers, count, seglen, scratch, *refs):
    pl.run_scoped(functools.partial(field_body, sleepers, count, seglen, refs), *scratch)


def field_body(sleepers, count, seglen, refs, *scratch):
    flags, planes, inside, across, tw, tc, vectors, edge, out = refs
    source, ghosts, coefs, made, lhs, lay, *rings = scratch[:12]
    turn, pages, page_sems = scratch[12:]
    height, depth = planes.shape[1:]
    flat = planes.reshape(planes.shape[0] * height, depth)
    ny = height - 2 * HB
    width = inside.shape[2]
    chunks = width // LANES
    cells = 8 * seglen
    page_rows = pages.reshape(2 * count * 48, depth)
    lane = lax.broadcasted_iota(jnp.int32, (8, LANES), 1)
    sub = lax.broadcasted_iota(jnp.int32, (8, LANES), 0)

    def at(zm):
        return pl.ds(8 * (zm + 1), 8)

    def around(first, last):
        before = pltpu.roll(last, 1, 0)
        after = pltpu.roll(first, 7, 0)
        return (
            jnp.where(sub == 0, pltpu.roll(before, HALF, 1), before),
            jnp.where(sub == 7, pltpu.roll(after, HALF, 1), after),
        )

    def line_at(row, zm):
        return pl.ds(pl.multiple_of((row & 15) * cells, 8) + 8 * zm, 8)

    def column(q):
        part, c = divmod(q, 3)
        return slice((2 * c + part) * LANES, (2 * c + part + 1) * LANES)

    def read_source(row, q, zm):
        if zm == -1:
            return ghosts[row & 3, q, :8, :]
        if zm == seglen:
            return ghosts[row & 3, q, 8:, :]
        rows = pl.ds(pl.multiple_of((row & 3) * cells, 8) + 8 * zm, 8)
        return source[rows, column(q)]

    def reader(ring):
        def read(row, q, zm):
            outside = ((row < HY) & (flags[0] == 1)) | ((row >= HY + ny) & (flags[1] == 1))
            return ring[jnp.where(outside, 4, row & 3), q, at(zm), :]

        return read

    def produce(pair):
        def lay_out(k):
            srow = jnp.clip(2 * pair - 2 + k + (HB - HY), 0, height - 1)
            values = row_values(flat, srow, height, sleepers, width)
            odd = flags[3] == 1
            for n in range(chunks):
                span = slice(n * LANES, (n + 1) * LANES)
                lay[k * chunks + n, HB : HB + depth, :] = jnp.transpose(values[span])
                first, second = inside[srow, :, span], across[srow, :, span]
                lay[k * chunks + n, :HB, :] = jnp.where(odd, first, second)
                lay[k * chunks + n, HB + depth :, :] = jnp.where(odd, second, first)

        def split():
            halves = [[], []]
            for k in range(2):
                for half in range(2):
                    for zm in range(seglen):
                        spot = pl.ds(half * cells + zm, 8, stride=seglen)
                        pieces_at = [lay[k * chunks + n, spot, :] for n in range(chunks)]
                        halves[half].append(jnp.concatenate(pieces_at, axis=1))
            values = jnp.concatenate(
                [jnp.concatenate(half, axis=0) for half in halves], axis=1
            )
            high, low = two_parts(values)
            lhs[:, : 2 * width] = high
            lhs[:, 2 * width : 4 * width] = low
            lhs[:, 4 * width :] = high

        first_row = 2 * pair - 2
        target = pl.ds(pl.multiple_of((first_row & 3) * cells, 8), 2 * cells)

        def spectrum(c):
            span = slice(2 * c * LANES, 2 * (c + 1) * LANES)
            source[target, span] = dot(lhs[...], tw[:, span])

        def fields(f):
            span = slice(f * LANES, (f + 2) * LANES)
            made[:, span] = dot(lhs[:, : 2 * width], tc[:, span])

        def wrap(k):
            row = first_row + k
            for q in range(6):
                ghosts[row & 3, q, :8, :], ghosts[row & 3, q, 8:, :] = around(
                    read_source(row, q, 0), read_source(row, q, seglen - 1)
                )

        return (
            [functools.partial(lay_out, 0), functools.partial(lay_out, 1), split],
            [functools.partial(spectrum, c) for c in range(3)]
            + [functools.partial(wrap, k) for k in range(2)],
            [functools.partial(fields, f) for f in range(0, 8, 2)],
        )

    def commit(pair):
        def move(k, zm):
            rows = slice(k * cells + 8 * zm, k * cells + 8 * zm + 8)
            for n in range(7):
                span = slice(n * LANES, (n + 1) * LANES)
                coefs[line_at(2 * pair - 2 + k, zm), span] = made[rows, span]

        return [functools.partial(move, k, zm) for k in range(2) for zm in range(seglen)]

    def apply(src, row, emit, shift=None, tilt=None):
        cur = [[src(row + k, q, 0) for q in range(6)] for k in range(2)]
        behind = [
            [src(row + k, q, -1) + (cur[1][q] if k == 0 else src(row + 2, q, 0)) for q in range(6)]
            for k in range(2)
        ]
        for zm in range(seglen):
            nxt = [[src(row + k, q, zm + 1) for q in range(6)] for k in range(2)]
            ahead = [
                [src(row - 1, q, zm) + nxt[0][q] for q in range(6)],
                [cur[0][q] + nxt[1][q] for q in range(6)],
            ]
            if zm + 1 < seglen:
                below = [cur[1][q] + src(row + 2, q, zm + 1) for q in range(6)]
            for k in range(2):
                f = [
                    coefs[line_at(row + k, zm), n * LANES : (n + 1) * LANES] for n in range(7)
                ]
                diagonal, damping = f[:3], f[6]
                if shift is not None:
                    diagonal = [d + shift for d in diagonal]
                if tilt is not None:
                    damping = damping - tilt
                matrix = (
                    (diagonal[0], f[3], f[4]),
                    (f[3], diagonal[1], f[5]),
                    (f[4], f[5], diagonal[2]),
                )
                results = []
                for q in range(6):
                    part, c = divmod(q, 3)
                    mine = cur[k][3 * part : 3 * part + 3]
                    own = matrix[c][0] * mine[0] + matrix[c][1] * mine[1] + matrix[c][2] * mine[2]
                    damp = damping * cur[k][3 * (1 - part) + c]
                    total = (ahead[k][q] + behind[k][q]) + own
                    total = total + damp if part == 0 else total - damp
                    results.append(total)
                emit(k, zm, results)
            if zm + 1 < seglen:
                behind = [ahead[1], below]
            cur = nxt

    def stage(src, dst, row, shift, tilt, between=None):
        ends = {}

        def emit(k, zm, results):
            if zm == HB - 1:
                results = [value * edge[0] for value in results]
            if zm == (HB + depth) % seglen:
                results = [value * edge[1] for value in results]
            slot = (row + k) & 3
            for q in range(6):
                dst[slot, q, at(zm), :] = results[q]
            if zm in (0, seglen - 1):
                ends[k, zm] = results
            if zm == seglen - 1:
                for q in range(6):
                    dst[slot, q, at(-1), :], dst[slot, q, at(seglen), :] = around(
                        ends[k, 0][q], results[q]
                    )
            if between is not None:
                between()

        apply(src, row, emit, shift, tilt)

    def last_stage(row, between=None):
        def emit(k, zm, results):
            for c in range(3):
                real, imag = results[c], results[3 + c]
                first = jnp.where(lane < HALF, real, pltpu.roll(imag, HALF, 1))
                second = jnp.where(lane < HALF, pltpu.roll(real, HALF, 1), imag)
                turn[3 * k + c, pl.ds(zm, 8, stride=seglen), :] = first
                turn[3 * k + c, pl.ds(cells + zm, 8, stride=seglen), :] = second
            if between is not None:
                between()

        apply(reader(rings[5]), row, emit, shift=vectors[3])

    def run_stage(t, base, between=None):
        shift = (1, 1, -1, -1, 0, 0)[t - 1]
        shift = shift * vectors[0] if shift else None
        tilt = (vectors[1] if t <= 4 else vectors[2]) * (1 if t % 2 else -1)
        src = read_source if t == 1 else reader(rings[t - 2])
        stage(src, rings[t - 1], base - t, shift, tilt, between)

    def spread(tasks, slots):
        total, seen, left_over = len(tasks), [0], list(tasks)

        def between():
            seen[0] += 1
            while left_over and (total - len(left_over)) * slots < seen[0] * total:
                left_over.pop(0)()

        return between

    def mixed(first, second):
        tasks = []
        for n in range(max(len(first), len(second))):
            tasks += first[n : n + 1] + second[n : n + 1]
        return tasks

    def finish(pair):
        done = pair - HB
        block = done >> 2
        start = pl.multiple_of((block & 1) * (count * 48), 8) + 2 * (done & 3)

        def page(k, c):
            turned = jnp.transpose(turn[3 * k + c, HB : HB + depth, :])
            for part in range(2):
                rows = pl.ds(start + (part * 3 + c) * 8 + k, count, stride=48)
                page_rows[rows, :] = turned[part * HALF : part * HALF + count]

        return [functools.partial(page, k, c) for k in range(2) for c in range(3)]

    def page_copy(block):
        return pltpu.make_async_copy(
            pages.at[block & 1],
            out.at[:, :, :, pl.ds(pl.multiple_of(8 * block, 8), 8), :],
            page_sems.at[block & 1],
        )

    def ramp(pair, carry):
        base = 2 * pair - 2
        for t, tasks in enumerate(produce(pair + 1), 1):

            @pl.when(base >= 2 * t)
            def _():
                run_stage(t, base, spread(tasks, 2 * seglen))

            @pl.when(base < 2 * t)
            def _():
                for task in tasks:
                    task()

        for t in range(4, 7):

            @pl.when(base >= 2 * t)
            def _():
                run_stage(t, base)

        @pl.when(base >= 14)
        def _():
            last_stage(base - 7)

        for task in commit(pair + 1):
            task()
        return carry

    def steady(pair, carry):
        base = 2 * pair - 2
        done = pair - 1 - HB

        @pl.when(((done & 3) == 0) & (done >= 8))
        def _():
            page_copy((done >> 2) - 2).wait()

        early, middle, late = produce(pair + 1)
        turning = finish(pair - 1)
        run_stage(1, base, spread(mixed(early, turning[:2]), 2 * seglen))
        between = spread(mixed(middle + late, turning[2:]), 10 * seglen)
        for t in range(2, 7):
            run_stage(t, base, between)
        last_stage(base - 7, spread(commit(pair + 1), 2 * seglen))

        @pl.when((done & 3) == 3)
        def _():
            page_copy(done >> 2).start()

        return carry

    for ring in rings:
        for q in range(6):
            ring[4, q, :, :] = jnp.zeros(ring.shape[2:], jnp.float32)
    for tasks in (*produce(1), commit(1)):
        for task in tasks:
            task()
    final = HB + ny // 2 - 1
    lax.fori_loop(1, HB + 1, ramp, 0)
    lax.fori_loop(HB + 1, final + 1, steady, 0)
    blocks = ny // 8
    pieces = []
    for c in range(3):
        for page in finish(final)[c::3]:
            page()
        piece = pltpu.make_async_copy(
            pages.at[(blocks - 1) & 1, :, :, c],
            out.at[:, :, c, pl.ds(8 * (blocks - 1), 8), :],
            page_sems.at[2 + c],
        )
        piece.start()
        pieces.append(piece)
    if blocks > 1:
        page_copy(blocks - 2).wait()
    for piece in pieces:
        piece.wait()


def solve_field(planes, flags, inside, across, tw, tc, vectors, edge, sleepers, count):
    height, _, width = inside.shape
    depth = planes.shape[2]
    ny = height - 2 * HB
    seglen = (depth + 2 * HB) // SEGS
    cells = 8 * seglen
    chunks = width // LANES
    ring = pltpu.VMEM((5, 6, 8 * (seglen + 2), LANES), jnp.float32)
    whole = pl.BlockSpec(memory_space=pltpu.VMEM)
    scratch = (
        pltpu.VMEM((4 * cells, 6 * LANES), jnp.float32),
        pltpu.VMEM((4, 6, 16, LANES), jnp.float32),
        pltpu.VMEM((16 * cells, 7 * LANES), jnp.float32),
        pltpu.VMEM((2 * cells, 8 * LANES), jnp.float32),
        pltpu.VMEM((2 * cells, 6 * width), jnp.bfloat16),
        pltpu.VMEM((2 * chunks, 2 * cells, LANES), jnp.float32),
        ring, ring, ring, ring, ring, ring,
        pltpu.VMEM((6, 2 * cells, LANES), jnp.float32),
        pltpu.VMEM((2, count, 2, 3, 8, depth), jnp.float32),
        pltpu.SemaphoreType.DMA((5,)),
    )
    return pl.pallas_call(
        functools.partial(field_kernel, sleepers, count, seglen, scratch),
        out_shape=jax.ShapeDtypeStruct((count, 2, 3, ny, depth), jnp.float32),
        in_specs=[pl.BlockSpec(memory_space=pltpu.SMEM)]
        + [whole] * 7,
        out_specs=pl.BlockSpec(memory_space=pl.ANY),
        compiler_params=pltpu.CompilerParams(vmem_limit_bytes=40 * 1024 * 1024),
        name="adjoint_field",
    )(flags, planes, inside, across, tw, tc, vectors, edge)


def local(loads, sleeper_pos, material, material_table):
    ka = lax.axis_size("ka")
    gy, gz = lax.axis_size("gy"), lax.axis_size("gz")
    count = KW // ka
    wave_start = lax.axis_index("ka") * count
    sleepers = ka * loads.shape[0]
    own = 3 * loads.shape[0]
    ny, depth = material.shape
    height = ny + 2 * HB
    loads = loads.reshape(own, ny, depth)
    material = material.astype(jnp.float32)[None]

    def swap(array, axis, size, first):
        pairs = [(i, i + 1) for i in range(first, size - 1, 2)]
        return lax.ppermute(array, axis, pairs + [(high, low) for low, high in pairs])

    y_at, z_at = lax.axis_index("gy"), lax.axis_index("gz")
    y_odd, z_odd = y_at % 2 == 1, z_at % 2 == 1
    turns = [[(i, (i + step) % ka) for i in range(ka)] for step in range(1, ka)]
    ends = jnp.concatenate([loads[:, :HB], loads[:, ny - HB :]], axis=1)
    ends, sleeper_pos = lax.optimization_barrier((ends, sleeper_pos))
    got_ends = [lax.ppermute(ends, "ka", turn) for turn in turns]
    all_pos = [sleeper_pos] + [lax.ppermute(sleeper_pos, "ka", turn) for turn in turns]
    met, tied = lax.optimization_barrier((all_pos, loads))
    low = jnp.concatenate([tied[:, :HB], material[:, :HB]], axis=0)
    high = jnp.concatenate([tied[:, ny - HB :], material[:, ny - HB :]], axis=0)
    halos = (
        swap(jnp.where(y_odd, low, high), "gy", gy, 0),
        swap(jnp.where(y_odd, high, low), "gy", gy, 1),
    )
    inner, got_ends = lax.optimization_barrier((loads[:, HB : ny - HB], got_ends))
    got_inner = [lax.ppermute(inner, "ka", turn) for turn in turns]

    pieces, spots = [], []
    sides = ((HB + ny, 0), (0, HB + ny))

    def place(array, *where):
        pieces.append(array)
        spots.extend((len(pieces) - 1, *spot) for spot in where)

    def place_middle(first, outer, middle):
        place(outer, (first, own, 0, (0, HB), HB), (first, own, 0, (HB, HB), ny))
        place(middle, (first, own, 0, (0, ny - 2 * HB), 2 * HB))

    place_middle(0, ends, inner)
    place(material, (3 * sleepers, 1, 0, (0, ny), HB))
    for array, row in zip(halos, sides):
        place(array, (0, own, 0, (0, HB), row), (3 * sleepers, 1, own, (0, HB), row))
    for step, (outer, middle) in enumerate(zip(got_ends, got_inner), 1):
        place_middle(own * step, outer, middle)
        low, high = outer[:, :HB], outer[:, HB:]
        far = (
            swap(jnp.where(y_odd, low, high), "gy", gy, 0),
            swap(jnp.where(y_odd, high, low), "gy", gy, 1),
        )
        for array, row in zip(far, sides):
            place(array, (own * step, own, 0, (0, HB), row))

    met, _ = lax.optimization_barrier((met, got_ends))
    tw, tc, vectors = tables(
        jnp.concatenate(met), material_table, wave_start, count, lanes_for(sleepers)
    )
    flags = jnp.stack([y_at == 0, y_at == gy - 1, y_odd, z_odd]).astype(jnp.int32)
    sub = jnp.arange(8)[:, None]
    lane = jnp.arange(LANES)[None, :]
    edge = jnp.stack(
        [
            jnp.where((z_at == 0) & (sub == 0) & (lane < HALF), 0.0, 1.0),
            jnp.where((z_at == gz - 1) & (sub == 7) & (lane >= HALF), 0.0, 1.0),
        ]
    ).astype(jnp.float32)
    pieces[-1], flags, edge, tw, tc, vectors = lax.optimization_barrier(
        (pieces[-1], flags, edge, tw, tc, vectors)
    )

    columns, planes = edges_of(spots, flags, pieces, sleepers, height, depth)
    high, low = columns[:, :HB], columns[:, HB:]
    inside = swap(jnp.where(z_odd, low, high), "gz", gz, 0)
    across = swap(jnp.where(z_odd, high, low), "gz", gz, 1)
    return solve_field(
        planes, flags, inside, across, tw, tc, vectors, edge, sleepers, count
    )


def solution(mesh):
    return jax.shard_map(
        local,
        mesh=mesh,
        in_specs=(P("ka", None, "gy", "gz"), P("ka"), P("gy", "gz"), P()),
        out_specs=P("ka", None, None, "gy", "gz"),
        check_vma=False,
    )
```

```python
import functools
import math

import jax
import jax.numpy as jnp
from jax import lax
from jax.experimental import pallas as pl
from jax.experimental.pallas import tpu as pltpu
from jax.sharding import PartitionSpec as P

KW = 128
NMAT = 8
DEG = 4
LANES = 128
HALF = 64
SEGS = 16
HY = 7
HB = 8
FIELDS = 20


def lanes_for(sleepers):
    return -(-(3 * sleepers + 3 * NMAT) // LANES) * LANES


def two_parts(values):
    high = values.astype(jnp.bfloat16)
    low = (values - high.astype(jnp.float32)).astype(jnp.bfloat16)
    return high, low


def dot(a, b):
    return lax.dot_general(a, b, (((1,), (0,)), ((), ())), preferred_element_type=jnp.float32)


def table_kernel(sleepers, count, start, table, cells, positions, tw, tc):
    width = tc.shape[0] // 2
    lane = lax.broadcasted_iota(jnp.int32, (8, LANES), 1)
    wave = lane % HALF
    live = wave < count
    wave = wave + start[0]
    q = (2.0 * jnp.sin(wave.astype(jnp.float32) * (math.pi / KW))) ** 2
    lowest = highest = None
    for m in range(NMAT):
        s, xx, yy, zz, xy, xz, yz = (jnp.full((8, LANES), table[m, f]) for f in range(7))
        xy, xz, yz = jnp.abs(xy), jnp.abs(xz), jnp.abs(yz)
        sums = (xy + xz, xy + yz, xz + yz)
        low = s + q * functools.reduce(jnp.minimum, [d - r for d, r in zip((xx, yy, zz), sums)])
        high = s + q * functools.reduce(jnp.maximum, [d + r for d, r in zip((xx, yy, zz), sums)])
        lowest = low if m == 0 else jnp.minimum(lowest, low)
        highest = high if m == 0 else jnp.maximum(highest, high)
    highest = 8.0 + highest
    center = 0.5 * (highest + lowest)
    half_width = 0.5 * (highest - lowest)
    ratio2 = (center / half_width) ** 2
    top = 8.0 * ratio2 * (ratio2 - 1.0) + 1.0
    h2 = half_width * half_width
    h4 = h2 * h2
    scale = 8.0 / (top * h4)
    scale = jnp.where(live, scale * scale, 0.0)
    twice = h2 * jnp.sqrt(0.5 * (top + 1.0))
    shift = 0.5 * jnp.sqrt(twice + h2)
    tilt = 0.5 * jnp.sqrt(jnp.maximum(twice - h2, 0.0))
    beta = jnp.sqrt(lowest * highest)

    tc[...] = jnp.zeros(tc.shape, jnp.bfloat16)
    tw[...] = jnp.zeros(tw.shape, jnp.bfloat16)
    column = [jnp.broadcast_to(cells[:, f : f + 1], (8, LANES)) for f in range(8)]
    diagonal = [center - 4.0 - column[0] - q * column[c] for c in (1, 2, 3)]
    fields = [d + by for by in (shift, -shift, jnp.zeros_like(shift), center) for d in diagonal]
    fields += [-q * column[c] for c in (4, 5, 6)]
    damping = q * column[7]
    fields += [damping - by for by in (tilt, -tilt, beta, -beta)] + [damping]
    rounded = lambda values: values.astype(jnp.bfloat16).astype(jnp.float32)
    for f, field in enumerate(fields):
        field = jnp.where(live, field, 0.0)
        first = rounded(field)
        second = rounded(field - first)
        third = field - first - second
        rows = jnp.concatenate([first, second, third, jnp.zeros_like(first)], axis=0)
        lanes = lax.broadcasted_iota(jnp.int32, rows.shape, 1)
        for half in range(2):
            kept = jnp.where(lanes // HALF == half, rows, 0.0).astype(jnp.bfloat16)
            at = half * width + 3 * sleepers
            tc[at : at + 32, f * LANES : (f + 1) * LANES] = kept

    turns = (positions[...] * wave[:1]) & (KW - 1)
    angles = turns.astype(jnp.float32) * (2.0 * math.pi / KW)
    lanes = lax.broadcasted_iota(jnp.int32, turns.shape, 1)
    for part, phase in enumerate((jnp.cos(angles), -jnp.sin(angles))):
        phase = phase * scale[:1]
        high = rounded(phase)
        for segment, values in enumerate((high, high, phase - high)):
            for half in range(2):
                kept = jnp.where(lanes // HALF == half, values, 0.0).astype(jnp.bfloat16)
                for c in range(3):
                    at = (2 * segment + half) * width + c * sleepers
                    to = (2 * c + part) * LANES
                    tw[at : at + sleepers, to : to + LANES] = kept


def tables(positions, material_table, start, count, width):
    sleepers = positions.shape[0]
    spots = jnp.broadcast_to(positions[:, None], (sleepers, LANES))
    return pl.pallas_call(
        functools.partial(table_kernel, sleepers, count),
        out_shape=(
            jax.ShapeDtypeStruct((6 * width, 6 * LANES), jnp.bfloat16),
            jax.ShapeDtypeStruct((2 * width, FIELDS * LANES), jnp.bfloat16),
        ),
        in_specs=[pl.BlockSpec(memory_space=pltpu.SMEM)] * 2
        + [pl.BlockSpec(memory_space=pltpu.VMEM)] * 2,
        out_specs=(pl.BlockSpec(memory_space=pltpu.VMEM),) * 2,
        compiler_params=pltpu.CompilerParams(vmem_limit_bytes=32 * 1024 * 1024),
        name="tables",
    )(start.reshape(1), material_table, material_table, spots)


def row_values(planes, row, height, sleepers, width):
    depth = planes.shape[1]
    parts = [planes[pl.ds(c * height + row, sleepers, stride=3 * height), :] for c in range(3)]
    material = planes[pl.ds(3 * sleepers * height + row, 1), :]
    number = lax.broadcasted_iota(jnp.int32, (width - 3 * sleepers, depth), 0)
    kind = jnp.where(number < 3 * NMAT, number % NMAT, -1).astype(jnp.float32)
    parts.append((kind == material).astype(jnp.float32))
    return jnp.concatenate(parts, axis=0)


def gather(spots, flags, pieces, planes, sems):
    copies = []
    for n, (piece, first, count, plane, row, target) in enumerate(spots):
        src = pieces[piece]
        blocks = (0, planes.shape[1] // 8 - 1)
        if isinstance(target, tuple):
            target = pl.multiple_of(jnp.where(flags[2] == 1, target[1], target[0]), 8)
        else:
            blocks = range(target // 8, (target + row[1]) // 8)
        copy = pltpu.make_async_copy(
            src.at[plane : plane + count, row[0] : row[0] + row[1], :],
            planes.at[first : first + count, pl.ds(target, row[1]), :],
            sems.at[n],
        )
        copies.append((copy, blocks))
    for copy, _ in copies:
        copy.start()
    return copies


def edge_kernel(sleepers, spots, *refs):
    flags, *pieces, out, planes, sems = refs
    copies = gather(spots, flags, pieces, planes, sems)
    height, depth = planes.shape[1:]
    width = out.shape[2]
    strip = 2 * HB
    flat = planes.reshape(planes.shape[0] * height, depth)
    group = lax.broadcasted_iota(jnp.int32, (width, depth), 1) // strip

    last = height // 8 - 1
    for block in [*range(1, last), 0, last]:
        for copy, blocks in copies:
            if block in blocks:
                copy.wait()
        copies = [(copy, blocks) for copy, blocks in copies if block not in blocks]
        packed = None
        for line in range(8):
            values = row_values(flat, 8 * block + line, height, sleepers, width)
            moved = pltpu.roll(values, strip * line + HB, 1)
            packed = moved if line == 0 else jnp.where(group == line, moved, packed)
        for n in range(width // LANES):
            span = slice(n * LANES, (n + 1) * LANES)
            turned = jnp.transpose(packed[span])
            for line in range(8):
                out[8 * block + line, :, span] = turned[line * strip : (line + 1) * strip]


def edges_of(spots, flags, pieces, sleepers, height, depth):
    return pl.pallas_call(
        functools.partial(edge_kernel, sleepers, spots),
        out_shape=(
            jax.ShapeDtypeStruct((height, 2 * HB, lanes_for(sleepers)), jnp.float32),
            jax.ShapeDtypeStruct((3 * sleepers + 1, height, depth), jnp.float32),
        ),
        in_specs=[pl.BlockSpec(memory_space=pltpu.SMEM)]
        + [pl.BlockSpec(memory_space=pl.ANY)] * len(pieces),
        out_specs=(pl.BlockSpec(memory_space=pltpu.VMEM),) * 2,
        scratch_shapes=[pltpu.SemaphoreType.DMA((len(spots),))],
        compiler_params=pltpu.CompilerParams(vmem_limit_bytes=32 * 1024 * 1024),
        name="edge_columns",
    )(flags, *pieces)


def field_kernel(sleepers, count, seglen, scratch, *refs):
    pl.run_scoped(functools.partial(field_body, sleepers, count, seglen, refs), *scratch)


def field_body(sleepers, count, seglen, refs, *scratch):
    flags, planes, inside, across, tw, tc, edge, out = refs
    source, ghosts, coefs, made, lhs, lay, *rings = scratch[:12]
    turn, pages, page_sems = scratch[12:]
    height, depth = planes.shape[1:]
    flat = planes.reshape(planes.shape[0] * height, depth)
    ny = height - 2 * HB
    width = inside.shape[2]
    chunks = width // LANES
    cells = 8 * seglen
    page_rows = pages.reshape(2 * count * 48, depth)
    lane = lax.broadcasted_iota(jnp.int32, (8, LANES), 1)
    sub = lax.broadcasted_iota(jnp.int32, (8, LANES), 0)

    def at(zm):
        return pl.ds(8 * (zm + 1), 8)

    def around(first, last):
        before = pltpu.roll(last, 1, 0)
        after = pltpu.roll(first, 7, 0)
        return (
            jnp.where(sub == 0, pltpu.roll(before, HALF, 1), before),
            jnp.where(sub == 7, pltpu.roll(after, HALF, 1), after),
        )

    def line_at(row, zm):
        return pl.ds(pl.multiple_of((row & 15) * cells, 8) + 8 * zm, 8)

    def column(q):
        part, c = divmod(q, 3)
        return slice((2 * c + part) * LANES, (2 * c + part + 1) * LANES)

    def read_source(row, q, zm):
        if zm == -1:
            return ghosts[row & 3, q, :8, :]
        if zm == seglen:
            return ghosts[row & 3, q, 8:, :]
        rows = pl.ds(pl.multiple_of((row & 3) * cells, 8) + 8 * zm, 8)
        return source[rows, column(q)]

    def reader(ring):
        def read(row, q, zm):
            outside = ((row < HY) & (flags[0] == 1)) | ((row >= HY + ny) & (flags[1] == 1))
            return ring[jnp.where(outside, 4, row & 3), q, at(zm), :]

        return read

    def produce(pair):
        def lay_out(k):
            srow = jnp.clip(2 * pair - 2 + k + (HB - HY), 0, height - 1)
            values = row_values(flat, srow, height, sleepers, width)
            odd = flags[3] == 1
            for n in range(chunks):
                span = slice(n * LANES, (n + 1) * LANES)
                lay[k * chunks + n, HB : HB + depth, :] = jnp.transpose(values[span])
                first, second = inside[srow, :, span], across[srow, :, span]
                lay[k * chunks + n, :HB, :] = jnp.where(odd, first, second)
                lay[k * chunks + n, HB + depth :, :] = jnp.where(odd, second, first)

        def split():
            halves = [[], []]
            for k in range(2):
                for half in range(2):
                    for zm in range(seglen):
                        spot = pl.ds(half * cells + zm, 8, stride=seglen)
                        pieces_at = [lay[k * chunks + n, spot, :] for n in range(chunks)]
                        halves[half].append(jnp.concatenate(pieces_at, axis=1))
            values = jnp.concatenate(
                [jnp.concatenate(half, axis=0) for half in halves], axis=1
            )
            high, low = two_parts(values)
            lhs[:, : 2 * width] = high
            lhs[:, 2 * width : 4 * width] = low
            lhs[:, 4 * width :] = high

        first_row = 2 * pair - 2
        target = pl.ds(pl.multiple_of((first_row & 3) * cells, 8), 2 * cells)

        def spectrum(c):
            span = slice(2 * c * LANES, 2 * (c + 1) * LANES)
            source[target, span] = dot(lhs[...], tw[:, span])

        def fields(f):
            span = slice(f * LANES, (f + 2) * LANES)
            made[:, span] = dot(lhs[:, : 2 * width], tc[:, span])

        def wrap(k):
            row = first_row + k
            for q in range(6):
                ghosts[row & 3, q, :8, :], ghosts[row & 3, q, 8:, :] = around(
                    read_source(row, q, 0), read_source(row, q, seglen - 1)
                )

        return (
            [functools.partial(lay_out, 0), functools.partial(lay_out, 1), split],
            [functools.partial(spectrum, c) for c in range(3)]
            + [functools.partial(wrap, k) for k in range(2)],
            [functools.partial(fields, f) for f in range(0, FIELDS, 2)],
        )

    def commit(pair):
        def move(k, zm):
            rows = slice(k * cells + 8 * zm, k * cells + 8 * zm + 8)
            for n in range(FIELDS):
                span = slice(n * LANES, (n + 1) * LANES)
                coefs[line_at(2 * pair - 2 + k, zm), span] = made[rows, span]

        return [functools.partial(move, k, zm) for k in range(2) for zm in range(seglen)]

    def apply(src, row, emit, shift, tilt):
        cur = [[src(row + k, q, 0) for q in range(6)] for k in range(2)]
        behind = [
            [src(row + k, q, -1) + (cur[1][q] if k == 0 else src(row + 2, q, 0)) for q in range(6)]
            for k in range(2)
        ]
        for zm in range(seglen):
            nxt = [[src(row + k, q, zm + 1) for q in range(6)] for k in range(2)]
            ahead = [
                [src(row - 1, q, zm) + nxt[0][q] for q in range(6)],
                [cur[0][q] + nxt[1][q] for q in range(6)],
            ]
            if zm + 1 < seglen:
                below = [cur[1][q] + src(row + 2, q, zm + 1) for q in range(6)]
            for k in range(2):
                xx, yy, zz, xy, xz, yz, damping = (
                    coefs[line_at(row + k, zm), n * LANES : (n + 1) * LANES]
                    for n in (3 * shift, 3 * shift + 1, 3 * shift + 2, 12, 13, 14, 15 + tilt)
                )
                matrix = ((xx, xy, xz), (xy, yy, yz), (xz, yz, zz))
                results = []
                for q in range(6):
                    part, c = divmod(q, 3)
                    mine = cur[k][3 * part : 3 * part + 3]
                    own = matrix[c][0] * mine[0] + matrix[c][1] * mine[1] + matrix[c][2] * mine[2]
                    damp = damping * cur[k][3 * (1 - part) + c]
                    total = (ahead[k][q] + behind[k][q]) + own
                    total = total + damp if part == 0 else total - damp
                    results.append(total)
                emit(k, zm, results)
            if zm + 1 < seglen:
                behind = [ahead[1], below]
            cur = nxt

    def stage(src, dst, row, shift, tilt, between=None):
        ends = {}

        def emit(k, zm, results):
            if zm == HB - 1:
                results = [value * edge[0] for value in results]
            if zm == (HB + depth) % seglen:
                results = [value * edge[1] for value in results]
            slot = (row + k) & 3
            for q in range(6):
                dst[slot, q, at(zm), :] = results[q]
            if zm in (0, seglen - 1):
                ends[k, zm] = results
            if zm == seglen - 1:
                for q in range(6):
                    dst[slot, q, at(-1), :], dst[slot, q, at(seglen), :] = around(
                        ends[k, 0][q], results[q]
                    )
            if between is not None:
                between()

        apply(src, row, emit, shift, tilt)

    def last_stage(row, between=None):
        def emit(k, zm, results):
            for c in range(3):
                real, imag = results[c], results[3 + c]
                first = jnp.where(lane < HALF, real, pltpu.roll(imag, HALF, 1))
                second = jnp.where(lane < HALF, pltpu.roll(real, HALF, 1), imag)
                turn[3 * k + c, pl.ds(zm, 8, stride=seglen), :] = first
                turn[3 * k + c, pl.ds(cells + zm, 8, stride=seglen), :] = second
            if between is not None:
                between()

        apply(reader(rings[5]), row, emit, 3, 4)

    def run_stage(t, base, between=None):
        shift = (t - 1) // 2
        tilt = (0, 1, 0, 1, 2, 3)[t - 1]
        src = read_source if t == 1 else reader(rings[t - 2])
        stage(src, rings[t - 1], base - t, shift, tilt, between)

    def spread(tasks, slots):
        total, seen, left_over = len(tasks), [0], list(tasks)

        def between():
            seen[0] += 1
            while left_over and (total - len(left_over)) * slots < seen[0] * total:
                left_over.pop(0)()

        return between

    def mixed(first, second):
        tasks = []
        for n in range(max(len(first), len(second))):
            tasks += first[n : n + 1] + second[n : n + 1]
        return tasks

    def finish(pair):
        done = pair - HB
        block = done >> 2
        start = pl.multiple_of((block & 1) * (count * 48), 8) + 2 * (done & 3)

        def page(k, c):
            turned = jnp.transpose(turn[3 * k + c, HB : HB + depth, :])
            for part in range(2):
                rows = pl.ds(start + (part * 3 + c) * 8 + k, count, stride=48)
                page_rows[rows, :] = turned[part * HALF : part * HALF + count]

        return [functools.partial(page, k, c) for k in range(2) for c in range(3)]

    def page_copy(block):
        return pltpu.make_async_copy(
            pages.at[block & 1],
            out.at[:, :, :, pl.ds(pl.multiple_of(8 * block, 8), 8), :],
            page_sems.at[block & 1],
        )

    def ramp(pair, carry):
        base = 2 * pair - 2
        for t, tasks in enumerate(produce(pair + 1), 1):

            @pl.when(base >= 2 * t)
            def _():
                run_stage(t, base, spread(tasks, 2 * seglen))

            @pl.when(base < 2 * t)
            def _():
                for task in tasks:
                    task()

        for t in range(4, 7):

            @pl.when(base >= 2 * t)
            def _():
                run_stage(t, base)

        @pl.when(base >= 14)
        def _():
            last_stage(base - 7)

        for task in commit(pair + 1):
            task()
        return carry

    def steady(pair, carry):
        base = 2 * pair - 2
        done = pair - 1 - HB

        @pl.when(((done & 3) == 0) & (done >= 8))
        def _():
            page_copy((done >> 2) - 2).wait()

        early, middle, late = produce(pair + 1)
        turning = finish(pair - 1)
        run_stage(1, base, spread(mixed(early, turning[:2]), 2 * seglen))
        between = spread(mixed(middle + late, turning[2:]), 10 * seglen)
        for t in range(2, 7):
            run_stage(t, base, between)
        last_stage(base - 7, spread(commit(pair + 1), 2 * seglen))

        @pl.when((done & 3) == 3)
        def _():
            page_copy(done >> 2).start()

        return carry

    for ring in rings:
        for q in range(6):
            ring[4, q, :, :] = jnp.zeros(ring.shape[2:], jnp.float32)
    for tasks in (*produce(1), commit(1)):
        for task in tasks:
            task()
    final = HB + ny // 2 - 1
    lax.fori_loop(1, HB + 1, ramp, 0)
    lax.fori_loop(HB + 1, final + 1, steady, 0)
    blocks = ny // 8
    pieces = []
    for c in range(3):
        for page in finish(final)[c::3]:
            page()
        piece = pltpu.make_async_copy(
            pages.at[(blocks - 1) & 1, :, :, c],
            out.at[:, :, c, pl.ds(8 * (blocks - 1), 8), :],
            page_sems.at[2 + c],
        )
        piece.start()
        pieces.append(piece)
    if blocks > 1:
        page_copy(blocks - 2).wait()
    for piece in pieces:
        piece.wait()


def solve_field(planes, flags, inside, across, tw, tc, edge, sleepers, count):
    height, _, width = inside.shape
    depth = planes.shape[2]
    ny = height - 2 * HB
    seglen = (depth + 2 * HB) // SEGS
    cells = 8 * seglen
    chunks = width // LANES
    ring = pltpu.VMEM((5, 6, 8 * (seglen + 2), LANES), jnp.float32)
    whole = pl.BlockSpec(memory_space=pltpu.VMEM)
    scratch = (
        pltpu.VMEM((4 * cells, 6 * LANES), jnp.float32),
        pltpu.VMEM((4, 6, 16, LANES), jnp.float32),
        pltpu.VMEM((16 * cells, FIELDS * LANES), jnp.float32),
        pltpu.VMEM((2 * cells, FIELDS * LANES), jnp.float32),
        pltpu.VMEM((2 * cells, 6 * width), jnp.bfloat16),
        pltpu.VMEM((2 * chunks, 2 * cells, LANES), jnp.float32),
        ring, ring, ring, ring, ring, ring,
        pltpu.VMEM((6, 2 * cells, LANES), jnp.float32),
        pltpu.VMEM((2, count, 2, 3, 8, depth), jnp.float32),
        pltpu.SemaphoreType.DMA((5,)),
    )
    return pl.pallas_call(
        functools.partial(field_kernel, sleepers, count, seglen, scratch),
        out_shape=jax.ShapeDtypeStruct((count, 2, 3, ny, depth), jnp.float32),
        in_specs=[pl.BlockSpec(memory_space=pltpu.SMEM)]
        + [whole] * 6,
        out_specs=pl.BlockSpec(memory_space=pl.ANY),
        compiler_params=pltpu.CompilerParams(vmem_limit_bytes=40 * 1024 * 1024),
        name="adjoint_field",
    )(flags, planes, inside, across, tw, tc, edge)


def local(loads, sleeper_pos, material, material_table):
    ka = lax.axis_size("ka")
    gy, gz = lax.axis_size("gy"), lax.axis_size("gz")
    count = KW // ka
    wave_start = lax.axis_index("ka") * count
    sleepers = ka * loads.shape[0]
    own = 3 * loads.shape[0]
    ny, depth = material.shape
    height = ny + 2 * HB
    loads = loads.reshape(own, ny, depth)
    material = material.astype(jnp.float32)[None]

    def swap(array, axis, size, first):
        pairs = [(i, i + 1) for i in range(first, size - 1, 2)]
        return lax.ppermute(array, axis, pairs + [(high, low) for low, high in pairs])

    y_at, z_at = lax.axis_index("gy"), lax.axis_index("gz")
    y_odd, z_odd = y_at % 2 == 1, z_at % 2 == 1
    turns = [[(i, (i + step) % ka) for i in range(ka)] for step in range(1, ka)]
    ends = jnp.concatenate([loads[:, :HB], loads[:, ny - HB :]], axis=1)
    ends, sleeper_pos = lax.optimization_barrier((ends, sleeper_pos))
    got_ends = [lax.ppermute(ends, "ka", turn) for turn in turns]
    all_pos = [sleeper_pos] + [lax.ppermute(sleeper_pos, "ka", turn) for turn in turns]
    met, tied = lax.optimization_barrier((all_pos, loads))
    low = jnp.concatenate([tied[:, :HB], material[:, :HB]], axis=0)
    high = jnp.concatenate([tied[:, ny - HB :], material[:, ny - HB :]], axis=0)
    halos = (
        swap(jnp.where(y_odd, low, high), "gy", gy, 0),
        swap(jnp.where(y_odd, high, low), "gy", gy, 1),
    )
    inner, got_ends = lax.optimization_barrier((loads[:, HB : ny - HB], got_ends))
    got_inner = [lax.ppermute(inner, "ka", turn) for turn in turns]

    pieces, spots = [], []
    sides = ((HB + ny, 0), (0, HB + ny))

    def place(array, *where):
        pieces.append(array)
        spots.extend((len(pieces) - 1, *spot) for spot in where)

    def place_middle(first, outer, middle):
        place(outer, (first, own, 0, (0, HB), HB), (first, own, 0, (HB, HB), ny))
        place(middle, (first, own, 0, (0, ny - 2 * HB), 2 * HB))

    place_middle(0, ends, inner)
    place(material, (3 * sleepers, 1, 0, (0, ny), HB))
    for array, row in zip(halos, sides):
        place(array, (0, own, 0, (0, HB), row), (3 * sleepers, 1, own, (0, HB), row))
    for step, (outer, middle) in enumerate(zip(got_ends, got_inner), 1):
        place_middle(own * step, outer, middle)
        low, high = outer[:, :HB], outer[:, HB:]
        far = (
            swap(jnp.where(y_odd, low, high), "gy", gy, 0),
            swap(jnp.where(y_odd, high, low), "gy", gy, 1),
        )
        for array, row in zip(far, sides):
            place(array, (own * step, own, 0, (0, HB), row))

    met, _ = lax.optimization_barrier((met, got_ends))
    tw, tc = tables(
        jnp.concatenate(met), material_table, wave_start, count, lanes_for(sleepers)
    )
    flags = jnp.stack([y_at == 0, y_at == gy - 1, y_odd, z_odd]).astype(jnp.int32)
    sub = jnp.arange(8)[:, None]
    lane = jnp.arange(LANES)[None, :]
    edge = jnp.stack(
        [
            jnp.where((z_at == 0) & (sub == 0) & (lane < HALF), 0.0, 1.0),
            jnp.where((z_at == gz - 1) & (sub == 7) & (lane >= HALF), 0.0, 1.0),
        ]
    ).astype(jnp.float32)
    pieces[-1], flags, edge, tw, tc = lax.optimization_barrier(
        (pieces[-1], flags, edge, tw, tc)
    )

    columns, planes = edges_of(spots, flags, pieces, sleepers, height, depth)
    high, low = columns[:, :HB], columns[:, HB:]
    inside = swap(jnp.where(z_odd, low, high), "gz", gz, 0)
    across = swap(jnp.where(z_odd, high, low), "gz", gz, 1)
    return solve_field(
        planes, flags, inside, across, tw, tc, edge, sleepers, count
    )


def solution(mesh):
    return jax.shard_map(
        local,
        mesh=mesh,
        in_specs=(P("ka", None, "gy", "gz"), P("ka"), P("gy", "gz"), P()),
        out_specs=P("ka", None, None, "gy", "gz"),
        check_vma=False,
    )
```

```python
import functools
import math

import jax
import jax.numpy as jnp
from jax import lax
from jax.experimental import pallas as pl
from jax.experimental.pallas import tpu as pltpu
from jax.sharding import PartitionSpec as P

KW = 128
NMAT = 8
DEG = 4
LANES = 128
HALF = 64
SEGS = 16
HY = 7
HB = 8


def lanes_for(sleepers):
    return -(-(3 * sleepers + 3 * NMAT) // LANES) * LANES


def two_parts(values):
    high = values.astype(jnp.bfloat16)
    low = (values - high.astype(jnp.float32)).astype(jnp.bfloat16)
    return high, low


def dot(a, b):
    return lax.dot_general(a, b, (((1,), (0,)), ((), ())), preferred_element_type=jnp.float32)


def table_kernel(sleepers, count, start, table, cells, positions, tw, tc, vectors):
    width = tc.shape[0] // 2
    lane = lax.broadcasted_iota(jnp.int32, (8, LANES), 1)
    wave = lane % HALF
    live = wave < count
    wave = wave + start[0]
    q = (2.0 * jnp.sin(wave.astype(jnp.float32) * (math.pi / KW))) ** 2
    lowest = highest = None
    for m in range(NMAT):
        s, xx, yy, zz, xy, xz, yz = (jnp.full((8, LANES), table[m, f]) for f in range(7))
        xy, xz, yz = jnp.abs(xy), jnp.abs(xz), jnp.abs(yz)
        sums = (xy + xz, xy + yz, xz + yz)
        low = s + q * functools.reduce(jnp.minimum, [d - r for d, r in zip((xx, yy, zz), sums)])
        high = s + q * functools.reduce(jnp.maximum, [d + r for d, r in zip((xx, yy, zz), sums)])
        lowest = low if m == 0 else jnp.minimum(lowest, low)
        highest = high if m == 0 else jnp.maximum(highest, high)
    highest = 8.0 + highest
    center = 0.5 * (highest + lowest)
    half_width = 0.5 * (highest - lowest)
    ratio2 = (center / half_width) ** 2
    top = 8.0 * ratio2 * (ratio2 - 1.0) + 1.0
    h2 = half_width * half_width
    h4 = h2 * h2
    scale = 8.0 / (top * h4)
    scale = jnp.where(live, scale * scale, 0.0)
    twice = h2 * jnp.sqrt(0.5 * (top + 1.0))
    shift = 0.5 * jnp.sqrt(twice + h2)
    tilt = 0.5 * jnp.sqrt(jnp.maximum(twice - h2, 0.0))
    for n, vector in enumerate((shift, tilt, jnp.sqrt(lowest * highest), center)):
        vectors[n, :, :] = jnp.where(live, vector, 0.0)

    tc[...] = jnp.zeros(tc.shape, jnp.bfloat16)
    tw[...] = jnp.zeros(tw.shape, jnp.bfloat16)
    column = [jnp.broadcast_to(cells[:, f : f + 1], (8, LANES)) for f in range(8)]
    fields = [center - 4.0 - column[0] - q * column[c] for c in (1, 2, 3)]
    fields += [-q * column[c] for c in (4, 5, 6)] + [q * column[7]]
    rounded = lambda values: values.astype(jnp.bfloat16).astype(jnp.float32)
    for f, field in enumerate(fields):
        field = jnp.where(live, field, 0.0)
        first = rounded(field)
        second = rounded(field - first)
        third = field - first - second
        rows = jnp.concatenate([first, second, third, jnp.zeros_like(first)], axis=0)
        lanes = lax.broadcasted_iota(jnp.int32, rows.shape, 1)
        for half in range(2):
            kept = jnp.where(lanes // HALF == half, rows, 0.0).astype(jnp.bfloat16)
            at = half * width + 3 * sleepers
            tc[at : at + 32, f * LANES : (f + 1) * LANES] = kept

    turns = (positions[...] * wave[:1]) & (KW - 1)
    angles = turns.astype(jnp.float32) * (2.0 * math.pi / KW)
    lanes = lax.broadcasted_iota(jnp.int32, turns.shape, 1)
    for part, phase in enumerate((jnp.cos(angles), -jnp.sin(angles))):
        phase = phase * scale[:1]
        high = rounded(phase)
        for segment, values in enumerate((high, high, phase - high)):
            for half in range(2):
                kept = jnp.where(lanes // HALF == half, values, 0.0).astype(jnp.bfloat16)
                for c in range(3):
                    at = (2 * segment + half) * width + c * sleepers
                    to = (2 * c + part) * LANES
                    tw[at : at + sleepers, to : to + LANES] = kept


def tables(positions, material_table, start, count, width):
    sleepers = positions.shape[0]
    spots = jnp.broadcast_to(positions[:, None], (sleepers, LANES))
    return pl.pallas_call(
        functools.partial(table_kernel, sleepers, count),
        out_shape=(
            jax.ShapeDtypeStruct((6 * width, 6 * LANES), jnp.bfloat16),
            jax.ShapeDtypeStruct((2 * width, 8 * LANES), jnp.bfloat16),
            jax.ShapeDtypeStruct((4, 8, LANES), jnp.float32),
        ),
        in_specs=[pl.BlockSpec(memory_space=pltpu.SMEM)] * 2
        + [pl.BlockSpec(memory_space=pltpu.VMEM)] * 2,
        out_specs=(pl.BlockSpec(memory_space=pltpu.VMEM),) * 3,
        compiler_params=pltpu.CompilerParams(vmem_limit_bytes=32 * 1024 * 1024),
        name="tables",
    )(start.reshape(1), material_table, material_table, spots)


def row_values(planes, row, height, sleepers, width):
    depth = planes.shape[1]
    parts = [planes[pl.ds(c * height + row, sleepers, stride=3 * height), :] for c in range(3)]
    material = planes[pl.ds(3 * sleepers * height + row, 1), :]
    number = lax.broadcasted_iota(jnp.int32, (width - 3 * sleepers, depth), 0)
    kind = jnp.where(number < 3 * NMAT, number % NMAT, -1).astype(jnp.float32)
    parts.append((kind == material).astype(jnp.float32))
    return jnp.concatenate(parts, axis=0)


def gather(spots, flags, pieces, planes, sems):
    copies = []
    for n, (piece, first, count, plane, row, target) in enumerate(spots):
        src = pieces[piece]
        blocks = (0, planes.shape[1] // 8 - 1)
        if isinstance(target, tuple):
            target = pl.multiple_of(jnp.where(flags[2] == 1, target[1], target[0]), 8)
        else:
            blocks = range(target // 8, (target + row[1]) // 8)
        copy = pltpu.make_async_copy(
            src.at[plane : plane + count, row[0] : row[0] + row[1], :],
            planes.at[first : first + count, pl.ds(target, row[1]), :],
            sems.at[n],
        )
        copies.append((copy, blocks))
    for copy, _ in copies:
        copy.start()
    return copies


def edge_kernel(sleepers, spots, *refs):
    flags, *pieces, out, planes, sems = refs
    copies = gather(spots, flags, pieces, planes, sems)
    height, depth = planes.shape[1:]
    width = out.shape[2]
    strip = 2 * HB
    flat = planes.reshape(planes.shape[0] * height, depth)
    group = lax.broadcasted_iota(jnp.int32, (width, depth), 1) // strip

    last = height // 8 - 1
    for block in [*range(1, last), 0, last]:
        for copy, blocks in copies:
            if block in blocks:
                copy.wait()
        copies = [(copy, blocks) for copy, blocks in copies if block not in blocks]
        packed = None
        for line in range(8):
            values = row_values(flat, 8 * block + line, height, sleepers, width)
            moved = pltpu.roll(values, strip * line + HB, 1)
            packed = moved if line == 0 else jnp.where(group == line, moved, packed)
        for n in range(width // LANES):
            span = slice(n * LANES, (n + 1) * LANES)
            turned = jnp.transpose(packed[span])
            for line in range(8):
                out[8 * block + line, :, span] = turned[line * strip : (line + 1) * strip]


def edges_of(spots, flags, pieces, sleepers, height, depth):
    return pl.pallas_call(
        functools.partial(edge_kernel, sleepers, spots),
        out_shape=(
            jax.ShapeDtypeStruct((height, 2 * HB, lanes_for(sleepers)), jnp.float32),
            jax.ShapeDtypeStruct((3 * sleepers + 1, height, depth), jnp.float32),
        ),
        in_specs=[pl.BlockSpec(memory_space=pltpu.SMEM)]
        + [pl.BlockSpec(memory_space=pl.ANY)] * len(pieces),
        out_specs=(pl.BlockSpec(memory_space=pltpu.VMEM),) * 2,
        scratch_shapes=[pltpu.SemaphoreType.DMA((len(spots),))],
        compiler_params=pltpu.CompilerParams(vmem_limit_bytes=32 * 1024 * 1024),
        name="edge_columns",
    )(flags, *pieces)


def field_kernel(sleepers, count, seglen, scratch, *refs):
    pl.run_scoped(functools.partial(field_body, sleepers, count, seglen, refs), *scratch)


def field_body(sleepers, count, seglen, refs, *scratch):
    flags, planes, inside, across, tw, tc, vectors, edge, out = refs
    source, ghosts, coefs, made, lhs, lay, *rings = scratch[:12]
    turn, pages, page_sems = scratch[12:]
    height, depth = planes.shape[1:]
    flat = planes.reshape(planes.shape[0] * height, depth)
    ny = height - 2 * HB
    width = inside.shape[2]
    chunks = width // LANES
    cells = 8 * seglen
    page_rows = pages.reshape(2 * count * 48, depth)
    lane = lax.broadcasted_iota(jnp.int32, (8, LANES), 1)
    sub = lax.broadcasted_iota(jnp.int32, (8, LANES), 0)

    borders = (HB - 1, (HB + depth) % seglen)

    def at(zm):
        return pl.ds(8 * (zm + 1), 8)

    def around(first, last):
        before = pltpu.roll(last, 1, 0)
        after = pltpu.roll(first, 7, 0)
        return (
            jnp.where(sub == 0, pltpu.roll(before, HALF, 1), before),
            jnp.where(sub == 7, pltpu.roll(after, HALF, 1), after),
        )

    def line_at(row, zm):
        return pl.ds(pl.multiple_of((row & 15) * cells, 8) + 8 * zm, 8)

    def column(q):
        part, c = divmod(q, 3)
        return slice((2 * c + part) * LANES, (2 * c + part + 1) * LANES)

    def read_source(row, q, zm):
        if zm == -1:
            return ghosts[row & 3, q, :8, :]
        if zm == seglen:
            return ghosts[row & 3, q, 8:, :]
        rows = pl.ds(pl.multiple_of((row & 3) * cells, 8) + 8 * zm, 8)
        return source[rows, column(q)]

    def reader(ring):
        def read(row, q, zm):
            outside = ((row < HY) & (flags[0] == 1)) | ((row >= HY + ny) & (flags[1] == 1))
            return ring[jnp.where(outside, 4, row & 3), q, at(zm), :]

        return read

    def produce(pair):
        def lay_out(k):
            srow = jnp.clip(2 * pair - 2 + k + (HB - HY), 0, height - 1)
            values = row_values(flat, srow, height, sleepers, width)
            odd = flags[3] == 1
            for n in range(chunks):
                span = slice(n * LANES, (n + 1) * LANES)
                lay[k * chunks + n, HB : HB + depth, :] = jnp.transpose(values[span])
                first, second = inside[srow, :, span], across[srow, :, span]
                lay[k * chunks + n, :HB, :] = jnp.where(odd, first, second)
                lay[k * chunks + n, HB + depth :, :] = jnp.where(odd, second, first)

        def split():
            halves = [[], []]
            for k in range(2):
                for half in range(2):
                    for zm in range(seglen):
                        spot = pl.ds(half * cells + zm, 8, stride=seglen)
                        pieces_at = [lay[k * chunks + n, spot, :] for n in range(chunks)]
                        halves[half].append(jnp.concatenate(pieces_at, axis=1))
            values = jnp.concatenate(
                [jnp.concatenate(half, axis=0) for half in halves], axis=1
            )
            high, low = two_parts(values)
            lhs[:, : 2 * width] = high
            lhs[:, 2 * width : 4 * width] = low
            lhs[:, 4 * width :] = high

        first_row = 2 * pair - 2
        target = pl.ds(pl.multiple_of((first_row & 3) * cells, 8), 2 * cells)

        def spectrum(c):
            span = slice(2 * c * LANES, 2 * (c + 1) * LANES)
            source[target, span] = dot(lhs[...], tw[:, span])

        def fields(f):
            span = slice(f * LANES, min(f + 2, 7) * LANES)
            made[:, span] = dot(lhs[:, : 2 * width], tc[:, span])

        def wrap(k):
            row = first_row + k
            for q in range(6):
                ghosts[row & 3, q, :8, :], ghosts[row & 3, q, 8:, :] = around(
                    read_source(row, q, 0), read_source(row, q, seglen - 1)
                )

        return (
            [functools.partial(lay_out, 0), functools.partial(lay_out, 1), split],
            [functools.partial(spectrum, c) for c in range(3)]
            + [functools.partial(wrap, k) for k in range(2)],
            [functools.partial(fields, f) for f in range(0, 8, 2)],
        )

    def commit(pair):
        def move(k, zm):
            rows = slice(k * cells + 8 * zm, k * cells + 8 * zm + 8)
            for n in range(7):
                span = slice(n * LANES, (n + 1) * LANES)
                coefs[line_at(2 * pair - 2 + k, zm), span] = made[rows, span]

        return [functools.partial(move, k, zm) for k in range(2) for zm in range(seglen)]

    def apply(src, row, emit, shift=None, tilt=None):
        cur = [[src(row + k, q, 0) for q in range(6)] for k in range(2)]
        behind = [
            [src(row + k, q, -1) + (cur[1][q] if k == 0 else src(row + 2, q, 0)) for q in range(6)]
            for k in range(2)
        ]
        for zm in range(seglen):
            nxt = [[src(row + k, q, zm + 1) for q in range(6)] for k in range(2)]
            ahead = [
                [src(row - 1, q, zm) + nxt[0][q] for q in range(6)],
                [cur[0][q] + nxt[1][q] for q in range(6)],
            ]
            if zm + 1 < seglen:
                below = [cur[1][q] + src(row + 2, q, zm + 1) for q in range(6)]
            for k in range(2):
                f = [
                    coefs[line_at(row + k, zm), n * LANES : (n + 1) * LANES] for n in range(7)
                ]
                diagonal, damping = f[:3], f[6]
                if shift is not None:
                    diagonal = [d + shift for d in diagonal]
                if tilt is not None:
                    damping = damping - tilt
                matrix = (
                    (diagonal[0], f[3], f[4]),
                    (f[3], diagonal[1], f[5]),
                    (f[4], f[5], diagonal[2]),
                )
                results = []
                for q in range(6):
                    part, c = divmod(q, 3)
                    mine = cur[k][3 * part : 3 * part + 3]
                    own = matrix[c][0] * mine[0] + matrix[c][1] * mine[1] + matrix[c][2] * mine[2]
                    damp = damping * cur[k][3 * (1 - part) + c]
                    total = (ahead[k][q] + behind[k][q]) + own
                    total = total + damp if part == 0 else total - damp
                    results.append(total)
                emit(k, zm, results)
            if zm + 1 < seglen:
                behind = [ahead[1], below]
            cur = nxt

    def stage(src, dst, row, shift, tilt, between=None):
        ends = {}

        def emit(k, zm, results):
            slot = (row + k) & 3
            for q in range(6):
                if zm in borders:
                    kept = edge[borders.index(zm)] != 0.0
                    pltpu.store(dst.at[slot, q, at(zm), :], results[q], mask=kept)
                else:
                    dst[slot, q, at(zm), :] = results[q]
            if zm in (0, seglen - 1):
                ends[k, zm] = results
            if zm == seglen - 1:
                for q in range(6):
                    dst[slot, q, at(-1), :], dst[slot, q, at(seglen), :] = around(
                        ends[k, 0][q], results[q]
                    )
            if between is not None:
                between()

        apply(src, row, emit, shift, tilt)

    def last_stage(row, between=None):
        def emit(k, zm, results):
            for c in range(3):
                real, imag = results[c], results[3 + c]
                first = jnp.where(lane < HALF, real, pltpu.roll(imag, HALF, 1))
                second = jnp.where(lane < HALF, pltpu.roll(real, HALF, 1), imag)
                turn[3 * k + c, pl.ds(zm, 8, stride=seglen), :] = first
                turn[3 * k + c, pl.ds(cells + zm, 8, stride=seglen), :] = second
            if between is not None:
                between()

        apply(reader(rings[5]), row, emit, shift=vectors[3])

    def run_stage(t, base, between=None):
        shift = (1, 1, -1, -1, 0, 0)[t - 1]
        shift = shift * vectors[0] if shift else None
        tilt = (vectors[1] if t <= 4 else vectors[2]) * (1 if t % 2 else -1)
        src = read_source if t == 1 else reader(rings[t - 2])
        stage(src, rings[t - 1], base - t, shift, tilt, between)

    def spread(tasks, slots):
        total, seen, left_over = len(tasks), [0], list(tasks)

        def between():
            seen[0] += 1
            while left_over and (total - len(left_over)) * slots < seen[0] * total:
                left_over.pop(0)()

        return between

    def mixed(first, second):
        tasks = []
        for n in range(max(len(first), len(second))):
            tasks += first[n : n + 1] + second[n : n + 1]
        return tasks

    def finish(pair):
        done = pair - HB
        block = done >> 2
        start = pl.multiple_of((block & 1) * (count * 48), 8) + 2 * (done & 3)

        def page(k, c):
            turned = jnp.transpose(turn[3 * k + c, HB : HB + depth, :])
            for part in range(2):
                rows = pl.ds(start + (part * 3 + c) * 8 + k, count, stride=48)
                page_rows[rows, :] = turned[part * HALF : part * HALF + count]

        return [functools.partial(page, k, c) for k in range(2) for c in range(3)]

    def page_copy(block):
        return pltpu.make_async_copy(
            pages.at[block & 1],
            out.at[:, :, :, pl.ds(pl.multiple_of(8 * block, 8), 8), :],
            page_sems.at[block & 1],
        )

    def ramp(pair, carry):
        base = 2 * pair - 2
        for t, tasks in enumerate(produce(pair + 1), 1):

            @pl.when(base >= 2 * t)
            def _():
                run_stage(t, base, spread(tasks, 2 * seglen))

            @pl.when(base < 2 * t)
            def _():
                for task in tasks:
                    task()

        for t in range(4, 7):

            @pl.when(base >= 2 * t)
            def _():
                run_stage(t, base)

        @pl.when(base >= 14)
        def _():
            last_stage(base - 7)

        for task in commit(pair + 1):
            task()
        return carry

    def steady(pair, carry):
        base = 2 * pair - 2
        done = pair - 1 - HB

        @pl.when(((done & 3) == 0) & (done >= 8))
        def _():
            page_copy((done >> 2) - 2).wait()

        early, middle, late = produce(pair + 1)
        turning = finish(pair - 1)
        run_stage(1, base, spread(mixed(early, turning[:2]), 2 * seglen))
        between = spread(mixed(middle + late, turning[2:]), 10 * seglen)
        for t in range(2, 7):
            run_stage(t, base, between)
        last_stage(base - 7, spread(commit(pair + 1), 2 * seglen))

        @pl.when((done & 3) == 3)
        def _():
            page_copy(done >> 2).start()

        return carry

    for ring in rings:
        for q in range(6):
            ring[4, q, :, :] = jnp.zeros(ring.shape[2:], jnp.float32)
            for zm in borders:
                for slot in range(4):
                    ring[slot, q, at(zm), :] = jnp.zeros((8, LANES), jnp.float32)
    for tasks in (*produce(1), commit(1)):
        for task in tasks:
            task()
    final = HB + ny // 2 - 1
    lax.fori_loop(1, HB + 1, ramp, 0)
    lax.fori_loop(HB + 1, final + 1, steady, 0)
    blocks = ny // 8
    pieces = []
    for c in range(3):
        for page in finish(final)[c::3]:
            page()
        piece = pltpu.make_async_copy(
            pages.at[(blocks - 1) & 1, :, :, c],
            out.at[:, :, c, pl.ds(8 * (blocks - 1), 8), :],
            page_sems.at[2 + c],
        )
        piece.start()
        pieces.append(piece)
    if blocks > 1:
        page_copy(blocks - 2).wait()
    for piece in pieces:
        piece.wait()


def solve_field(planes, flags, inside, across, tw, tc, vectors, edge, sleepers, count):
    height, _, width = inside.shape
    depth = planes.shape[2]
    ny = height - 2 * HB
    seglen = (depth + 2 * HB) // SEGS
    cells = 8 * seglen
    chunks = width // LANES
    ring = pltpu.VMEM((5, 6, 8 * (seglen + 2), LANES), jnp.float32)
    whole = pl.BlockSpec(memory_space=pltpu.VMEM)
    scratch = (
        pltpu.VMEM((4 * cells, 6 * LANES), jnp.float32),
        pltpu.VMEM((4, 6, 16, LANES), jnp.float32),
        pltpu.VMEM((16 * cells, 7 * LANES), jnp.float32),
        pltpu.VMEM((2 * cells, 8 * LANES), jnp.float32),
        pltpu.VMEM((2 * cells, 6 * width), jnp.bfloat16),
        pltpu.VMEM((2 * chunks, 2 * cells, LANES), jnp.float32),
        ring, ring, ring, ring, ring, ring,
        pltpu.VMEM((6, 2 * cells, LANES), jnp.float32),
        pltpu.VMEM((2, count, 2, 3, 8, depth), jnp.float32),
        pltpu.SemaphoreType.DMA((5,)),
    )
    return pl.pallas_call(
        functools.partial(field_kernel, sleepers, count, seglen, scratch),
        out_shape=jax.ShapeDtypeStruct((count, 2, 3, ny, depth), jnp.float32),
        in_specs=[pl.BlockSpec(memory_space=pltpu.SMEM)]
        + [whole] * 7,
        out_specs=pl.BlockSpec(memory_space=pl.ANY),
        compiler_params=pltpu.CompilerParams(vmem_limit_bytes=40 * 1024 * 1024),
        name="adjoint_field",
    )(flags, planes, inside, across, tw, tc, vectors, edge)


def local(loads, sleeper_pos, material, material_table):
    ka = lax.axis_size("ka")
    gy, gz = lax.axis_size("gy"), lax.axis_size("gz")
    count = KW // ka
    wave_start = lax.axis_index("ka") * count
    sleepers = ka * loads.shape[0]
    own = 3 * loads.shape[0]
    ny, depth = material.shape
    height = ny + 2 * HB
    loads = loads.reshape(own, ny, depth)
    material = material.astype(jnp.float32)[None]

    def swap(array, axis, size, first):
        pairs = [(i, i + 1) for i in range(first, size - 1, 2)]
        return lax.ppermute(array, axis, pairs + [(high, low) for low, high in pairs])

    y_at, z_at = lax.axis_index("gy"), lax.axis_index("gz")
    y_odd, z_odd = y_at % 2 == 1, z_at % 2 == 1
    turns = [[(i, (i + step) % ka) for i in range(ka)] for step in range(1, ka)]
    ends = jnp.concatenate([loads[:, :HB], loads[:, ny - HB :]], axis=1)
    ends, sleeper_pos = lax.optimization_barrier((ends, sleeper_pos))
    got_ends = [lax.ppermute(ends, "ka", turn) for turn in turns]
    all_pos = [sleeper_pos] + [lax.ppermute(sleeper_pos, "ka", turn) for turn in turns]
    met, tied = lax.optimization_barrier((all_pos, loads))
    low = jnp.concatenate([tied[:, :HB], material[:, :HB]], axis=0)
    high = jnp.concatenate([tied[:, ny - HB :], material[:, ny - HB :]], axis=0)
    halos = (
        swap(jnp.where(y_odd, low, high), "gy", gy, 0),
        swap(jnp.where(y_odd, high, low), "gy", gy, 1),
    )
    inner, got_ends = lax.optimization_barrier((loads[:, HB : ny - HB], got_ends))
    got_inner = [lax.ppermute(inner, "ka", turn) for turn in turns]

    pieces, spots = [], []
    sides = ((HB + ny, 0), (0, HB + ny))

    def place(array, *where):
        pieces.append(array)
        spots.extend((len(pieces) - 1, *spot) for spot in where)

    def place_middle(first, outer, middle):
        place(outer, (first, own, 0, (0, HB), HB), (first, own, 0, (HB, HB), ny))
        place(middle, (first, own, 0, (0, ny - 2 * HB), 2 * HB))

    place_middle(0, ends, inner)
    place(material, (3 * sleepers, 1, 0, (0, ny), HB))
    for array, row in zip(halos, sides):
        place(array, (0, own, 0, (0, HB), row), (3 * sleepers, 1, own, (0, HB), row))
    for step, (outer, middle) in enumerate(zip(got_ends, got_inner), 1):
        place_middle(own * step, outer, middle)
        low, high = outer[:, :HB], outer[:, HB:]
        far = (
            swap(jnp.where(y_odd, low, high), "gy", gy, 0),
            swap(jnp.where(y_odd, high, low), "gy", gy, 1),
        )
        for array, row in zip(far, sides):
            place(array, (own * step, own, 0, (0, HB), row))

    met, _ = lax.optimization_barrier((met, got_ends))
    tw, tc, vectors = tables(
        jnp.concatenate(met), material_table, wave_start, count, lanes_for(sleepers)
    )
    flags = jnp.stack([y_at == 0, y_at == gy - 1, y_odd, z_odd]).astype(jnp.int32)
    sub = jnp.arange(8)[:, None]
    lane = jnp.arange(LANES)[None, :]
    edge = jnp.stack(
        [
            jnp.where((z_at == 0) & (sub == 0) & (lane < HALF), 0.0, 1.0),
            jnp.where((z_at == gz - 1) & (sub == 7) & (lane >= HALF), 0.0, 1.0),
        ]
    ).astype(jnp.float32)
    pieces[-1], flags, edge, tw, tc, vectors = lax.optimization_barrier(
        (pieces[-1], flags, edge, tw, tc, vectors)
    )

    columns, planes = edges_of(spots, flags, pieces, sleepers, height, depth)
    high, low = columns[:, :HB], columns[:, HB:]
    inside = swap(jnp.where(z_odd, low, high), "gz", gz, 0)
    across = swap(jnp.where(z_odd, high, low), "gz", gz, 1)
    return solve_field(
        planes, flags, inside, across, tw, tc, vectors, edge, sleepers, count
    )


def solution(mesh):
    return jax.shard_map(
        local,
        mesh=mesh,
        in_specs=(P("ka", None, "gy", "gz"), P("ka"), P("gy", "gz"), P()),
        out_specs=P("ka", None, None, "gy", "gz"),
        check_vma=False,
    )
```
